256 devices in a mesh: section: 32 (over z_lo, x, y), dp: 8 (over z_hi, core).
Axes of the slice: x: 4, y: 4, z: 8 (z_hi: 4, z_lo: 2; z = z_hi * 2 + z_lo), core: 2. Of those that a mesh axis runs over, the one named last changes fastest.
Arguments:
- forward_state: bfloat16 [32, 1024, 4096], P('section', 'dp'), may hold values from -6 to 6
- backward_state: bfloat16 [32, 1024, 4096], P('section', 'dp'), may hold values from -6 to 6
- saved: bfloat16 [32, 2, 1024, 4096], P('section', None, 'dp'), may hold values from -6 to 6
- fresh: bfloat16 [1024, 4096], P('dp'), may hold values from -6 to 6
- target: bfloat16 [1024, 4096], P('dp'), may hold values from -6 to 6
- forward_adapter: int32 [32], P('section'), may hold values from 0 to 3
- backward_adapter: int32 [32], P('section'), may hold values from 0 to 3
- value_projection: bfloat16 [32, 4096, 512], P('section', 'dp'), may hold values from -0.09375 to 0.09375
- output_matrix: bfloat16 [32, 512, 4096], P('section', None, 'dp'), may hold values from -0.25 to 0.25
- norm_gain_frozen: float32 [32, 4096], P('section'), may hold values from 0.1 to 1.9
- adapter_down: bfloat16 [32, 4, 4096, 64], P('section'), may hold values from -0.09375 to 0.09375
- adapter_up: bfloat16 [32, 4, 64, 512], P('section'), may hold values from -0.75 to 0.75
Outputs:
- fwd_out: bfloat16 [32, 1024, 4096], P('section', 'dp')
- bwd_out: bfloat16 [32, 1024, 4096], P('section', 'dp')
- grad_down: float32 [32, 4, 4096, 64], P('section', None, 'dp')
- grad_up: float32 [32, 4, 64, 512], P('section', None, None, 'dp')
The draws below stay inside these ranges and needn't reach their ends.
All inputs are finite; a program needn't handle non-finite values.
Results may differ from the reference program's by a relative error of at most 0.01.
Values may be sent and summed in bfloat16 or wider, within the bound.
No kernel may reach another device: no remote copies, remote signals or barrier semaphores. Data moves between devices by JAX's collectives and lax.ppermute only.
A program may use at most 128 MiB of HBM per device.

```python
import jax
import jax.numpy as jnp
from jax import lax

MODEL_WIDTH = 4096
VALUE_WIDTH = 512
ADAPTER_RANK = 64
ADAPTER_COUNT = 4
RELAY_SECTIONS = 32
TOKENS_MB = 1024


def place_ends(entries, key, smallest, largest):
    longest = entries.shape.index(max(entries.shape))
    spots = []
    for shift in (0, 1):
        where = [jax.random.randint(jax.random.fold_in(key, axis), (), 0, length) for axis, length in enumerate(entries.shape)]
        where[longest] = (where[longest] + shift) % entries.shape[longest]
        spots.append(tuple(where))
    return entries.at[spots[0]].set(smallest).at[spots[1]].set(largest)


def shard_levels(stream_key, shape, split, low, top_value):
    level = 1.0
    for position, shards_of in split:
        steps = jax.random.uniform(jax.random.fold_in(jax.random.fold_in(stream_key, 6), position), (shards_of,), jnp.float32, low / len(split), top_value / len(split))
        level = level * jnp.repeat(jnp.exp(steps), shape[position] // shards_of).reshape((-1,) + (1,) * (len(shape) - 1 - position))
    return level


def gaussian(stream_key, dims, deviation, reach, pieces=(), dtype=jnp.bfloat16):
    level = shard_levels(stream_key, dims, pieces, -0.22, 0.18) if pieces else 1.0
    result = jax.random.normal(stream_key, dims, jnp.float32) * deviation * level
    return jnp.minimum(jnp.maximum(result, -reach), reach).astype(dtype)


def setup_inputs(seed: int = 0) -> dict:
    splits = jax.random.split(jax.random.key(seed), 13)
    return {
        "forward_state": gaussian(splits[0], (RELAY_SECTIONS, TOKENS_MB, MODEL_WIDTH), 1.0, 6.0, ((0, 32), (1, 8))),
        "backward_state": gaussian(splits[1], (RELAY_SECTIONS, TOKENS_MB, MODEL_WIDTH), 1.0, 6.0, ((0, 32), (1, 8))),
        "saved": gaussian(splits[2], (RELAY_SECTIONS, 2, TOKENS_MB, MODEL_WIDTH), 1.0, 6.0, ((0, 32), (2, 8))),
        "fresh": gaussian(splits[3], (TOKENS_MB, MODEL_WIDTH), 1.0, 6.0, ((0, 8),)),
        "target": gaussian(splits[4], (TOKENS_MB, MODEL_WIDTH), 1.0, 6.0, ((0, 8),)),
        "forward_adapter": place_ends(jax.random.randint(splits[5], (RELAY_SECTIONS,), 0, ADAPTER_COUNT), jax.random.fold_in(splits[5], 1), 0, ADAPTER_COUNT - 1).astype(jnp.int32),
        "backward_adapter": place_ends(jax.random.randint(splits[6], (RELAY_SECTIONS,), 0, ADAPTER_COUNT), jax.random.fold_in(splits[6], 1), 0, ADAPTER_COUNT - 1).astype(jnp.int32),
        "value_projection": gaussian(splits[7], (RELAY_SECTIONS, MODEL_WIDTH, VALUE_WIDTH), MODEL_WIDTH ** -0.5, 0.09375, ((0, 32), (1, 8))),
        "output_matrix": gaussian(splits[8], (RELAY_SECTIONS, VALUE_WIDTH, MODEL_WIDTH), VALUE_WIDTH ** -0.5, 0.25, ((0, 32), (2, 8))),
        "norm_gain_frozen": jnp.clip(1.0 + 0.18 * jax.random.normal(splits[9], (RELAY_SECTIONS, MODEL_WIDTH), jnp.float32), 0.1, 1.9),
        "adapter_down": gaussian(splits[10], (RELAY_SECTIONS, ADAPTER_COUNT, MODEL_WIDTH, ADAPTER_RANK), MODEL_WIDTH ** -0.5, 0.09375, ((0, 32),)),
        "adapter_up": gaussian(splits[11], (RELAY_SECTIONS, ADAPTER_COUNT, ADAPTER_RANK, VALUE_WIDTH), ADAPTER_RANK ** -0.5, 0.75, ((0, 32),)),
    }


adapter_scale = 0.5

def normalize(token_rows, gain):
    whole = token_rows.astype(jnp.float32)
    factor = lax.rsqrt(lax.optimization_barrier(jnp.mean(whole * whole, axis=-1, keepdims=True)) + 1e-05)
    scaled = whole * factor
    return ((scaled * gain.astype(jnp.float32)).astype(jnp.bfloat16), scaled, factor)

def forward_layer(token_rows, gain, value_matrix, output_mat, down_mat, up_matrix):
    normalized_input, scaled, factor = normalize(token_rows, gain)
    lowrank_product = jnp.dot(normalized_input, down_mat, preferred_element_type=jnp.float32).astype(jnp.bfloat16)
    value_rows = jnp.dot(normalized_input, value_matrix, preferred_element_type=jnp.float32) + adapter_scale * jnp.dot(lowrank_product, up_matrix, preferred_element_type=jnp.float32)
    value_rows = value_rows.astype(jnp.bfloat16)
    return (token_rows.astype(jnp.float32) + jnp.dot(value_rows, output_mat, preferred_element_type=jnp.float32)).astype(jnp.bfloat16)

def backward_layer(token_rows, upstream, gain, value_matrix, output_mat, down_mat, up_matrix):
    normalized_input, scaled, factor = normalize(token_rows, gain)
    lowrank_product = jnp.dot(normalized_input, down_mat, preferred_element_type=jnp.float32).astype(jnp.bfloat16)
    gradient_values = jnp.dot(upstream, output_mat.T, preferred_element_type=jnp.float32).astype(jnp.bfloat16)
    up_product = adapter_scale * jnp.dot(lowrank_product.T, gradient_values, preferred_element_type=jnp.float32)
    gradient_lowrank = (adapter_scale * jnp.dot(gradient_values, up_matrix.T, preferred_element_type=jnp.float32)).astype(jnp.bfloat16)
    down_term = jnp.dot(normalized_input.T, gradient_lowrank, preferred_element_type=jnp.float32)
    d_normed = jnp.dot(gradient_values, value_matrix.T, preferred_element_type=jnp.float32) + jnp.dot(gradient_lowrank, down_mat.T, preferred_element_type=jnp.float32)
    d_gained = d_normed * gain.astype(jnp.float32)
    inner = lax.optimization_barrier(jnp.mean(d_gained * scaled, axis=-1, keepdims=True))
    d_rows = upstream.astype(jnp.float32) + factor * (d_gained - scaled * inner)
    return (d_rows.astype(jnp.bfloat16), down_term, up_product)

def reference(forward_state, backward_state, saved, fresh, target, forward_adapter, backward_adapter, value_projection, output_matrix, norm_gain_frozen, adapter_down, adapter_up):

    def run_forward(token_rows, adapter_indices):

        def single_adapter(item):
            h, ident, gain, wv, wo, down_factors, up_factors = item
            return forward_layer(h, gain, wv, wo, down_factors[ident], up_factors[ident])
        return lax.map(single_adapter, (token_rows, adapter_indices, norm_gain_frozen, value_projection, output_matrix, adapter_down, adapter_up))

    def run_backward(token_rows, gradient_list, adapter_indices):

        def single_adapter(item):
            h, g, ident, gain, wv, wo, down_factors, up_factors = item
            return backward_layer(h, g, gain, wv, wo, down_factors[ident], up_factors[ident])
        return lax.map(single_adapter, (token_rows, gradient_list, adapter_indices, norm_gain_frozen, value_projection, output_matrix, adapter_down, adapter_up))
    first_out = run_forward(forward_state, forward_adapter)
    d_first, down_one, up_one = run_backward(saved[:, 0], backward_state, backward_adapter)
    loss_grad = (first_out[-1].astype(jnp.float32) - target.astype(jnp.float32)).astype(jnp.bfloat16)
    rows_next = jnp.concatenate([fresh[None], first_out[:-1]], axis=0)
    ident_next = jnp.concatenate([forward_adapter[-1:], forward_adapter[:-1]], axis=0).astype(jnp.int32)
    grad_next = jnp.concatenate([d_first[1:], loss_grad[None]], axis=0)
    grad_ident = jnp.concatenate([backward_adapter[1:], forward_adapter[-1:]], axis=0).astype(jnp.int32)
    saved_next = jnp.concatenate([saved[:-1, 1], forward_state[-1:]], axis=0)
    fwd_out = run_forward(rows_next, ident_next)
    bwd_out, down_two, up_two = run_backward(saved_next, grad_next, grad_ident)
    labels = jnp.arange(ADAPTER_COUNT).astype(jnp.int32)
    pick_first = (labels[None, :] == backward_adapter[:, None]).astype(jnp.float32)
    pick_second = (labels[None, :] == grad_ident[:, None]).astype(jnp.float32)
    grad_down = pick_first[:, :, None, None] * down_one[:, None] + pick_second[:, :, None, None] * down_two[:, None]
    grad_up = pick_first[:, :, None, None] * up_one[:, None] + pick_second[:, :, None, None] * up_two[:, None]
    return (fwd_out, bwd_out, grad_down, grad_up)
```

```python
import jax
import jax.numpy as jnp
from jax import lax
from jax.experimental import pallas as pl
from jax.experimental.pallas import tpu as pltpu
from jax.sharding import PartitionSpec as P

SCALE = 0.5
EPS = 1e-05
BF = jnp.bfloat16
F32 = jnp.float32
ROWS = 128
WIDTH = 4096
VALUES = 512
PART = 512
RANK = 64
ADAPTERS = 4
PACK = PART + 128
VMEM = 40 * 1024 * 1024


def dot(left, right, dims=((1,), (0,))):
    return lax.dot_general(left, right, (dims, ((), ())), preferred_element_type=F32)


def dot_t(left, right):
    return dot(left, right, ((1,), (1,)))


def t_dot(left, right):
    return dot(left, right, ((0,), (0,)))


def call(kernel, scalars, ins, outs, flops, scratch=()):
    specs, arrays = [], []
    for item in ins:
        array, block, index = item if isinstance(item, tuple) else (item, None, None)
        arrays.append(array)
        if block is None:
            zeros = (0,) * array.ndim
            specs.append(pl.BlockSpec(array.shape, lambda i, *s, z=zeros: z))
        else:
            specs.append(pl.BlockSpec(block, index))
    out_specs = [pl.BlockSpec(o.shape, lambda i, *s, z=(0,) * len(o.shape): z) for o in outs]
    size = sum(a.size * a.dtype.itemsize for a in arrays)
    return pl.pallas_call(
        kernel,
        out_shape=outs,
        grid_spec=pltpu.PrefetchScalarGridSpec(
            num_scalar_prefetch=len(scalars),
            grid=(1,),
            in_specs=specs,
            out_specs=out_specs,
            scratch_shapes=list(scratch),
        ),
        compiler_params=pltpu.CompilerParams(vmem_limit_bytes=VMEM),
        cost_estimate=pl.CostEstimate(flops=flops, bytes_accessed=size, transcendentals=0),
    )(*scalars, *arrays)


def shape(dims, dtype):
    return jax.ShapeDtypeStruct(dims, dtype)


def factor_of(rows):
    return lax.rsqrt(jnp.sum(rows * rows, axis=-1, keepdims=True) * (1.0 / WIDTH) + EPS)


def columns(index):
    return pl.ds(pl.multiple_of(index * PART, PART), PART)


def prepare_kernel(ident, rows, gain, down, normed, factor, low):
    for top in range(0, ROWS, 32):
        part = slice(top, top + 32)
        whole = rows[part, :].astype(F32)
        scale = factor_of(whole)
        normed[part, :] = (whole * scale * gain[...]).astype(BF)
        factor[part, :] = jnp.broadcast_to(scale, (32, 128))
    low[...] = dot_t(normed[...], down[0]).astype(BF)


def down_of(down):
    return (down, (1, RANK, WIDTH), lambda i, ident, *s: (ident[0], 0, 0))


def up_of(up):
    return (up, (1, RANK, VALUES), lambda i, ident, *s: (ident[0], 0, 0))


def prepare(rows, gain, down, ident):
    return call(
        prepare_kernel,
        (ident,),
        [rows, gain, down_of(down)],
        [shape((ROWS, WIDTH), BF), shape((ROWS, 128), F32), shape((ROWS, RANK), BF)],
        2 * ROWS * WIDTH * RANK,
    )


def pack_gradients(where, low, normed, d_values, d_low, mine, other):
    up_term = SCALE * t_dot(low, d_values)
    chip, core = where[0] // 2, where[0] % 2
    for ahead in range(4):
        target = lax.rem(chip + ahead, 4)
        pair = up_term[:, 0:128]
        for k in range(1, 4):
            pair = jnp.where(target == k, up_term[:, 128 * k : 128 * (k + 1)], pair)
        pair = pair.astype(BF)
        for ref, c in ((mine, core), (other, 1 - core)):
            ref[ahead, :, :PART] = t_dot(d_low, normed[:, columns(2 * target + c)]).astype(BF)
            ref[ahead, :, PART:] = pair


PACKED = [shape((4, RANK, PACK), BF), shape((4, RANK, PACK), BF)]


def values_kernel(ident, where, grad, low, normed, up, *refs):
    blocks, (d_values, d_low, mine, other) = refs[:8], refs[8:]
    total = jnp.zeros((ROWS, VALUES), F32)
    for i in range(8):
        total += dot_t(grad[:, columns(where[i])], blocks[i][...])
    values = total.astype(BF)
    lowered = (SCALE * dot_t(values, up[0])).astype(BF)
    d_values[...] = values
    d_low[...] = lowered
    pack_gradients(where, low[...], normed, values, lowered, mine, other)


def first_values(ident, where, grad, low, normed, up, blocks):
    return call(
        values_kernel,
        (ident, where),
        [grad, low, normed, up_of(up), *blocks],
        [shape((ROWS, VALUES), BF), shape((ROWS, RANK), BF), *PACKED],
        2 * ROWS * WIDTH * (VALUES + RANK),
    )


def group_kernel(
    first, ident, where, grad, rows, normed, gain, down, factor, d_values, d_low,
    one, two, inner_in, sum_in, part, inner, total,
):
    scale = factor[:, :1]
    inner_sum = inner_in[...]
    value_sum = sum_in[...]
    for i, block in ((0, one), (1, two)):
        span = columns(where[first + i])
        gained = (
            dot_t(d_values[...], block[...]) + dot(d_low[...], down[0, :, span])
        ) * gain[:, span]
        pre = rows[:, span].astype(F32) * scale
        part[:, i * PART : (i + 1) * PART] = (
            grad[:, span].astype(F32) + scale * gained
        ).astype(BF)
        inner_sum += jnp.sum(gained * pre, axis=-1, keepdims=True)
        value_sum += dot(normed[:, span], block[...])
    if first == 6:
        inner_sum = inner_sum * (scale * scale * (1.0 / WIDTH))
    inner[...] = inner_sum
    total[...] = value_sum


def group(first, ident, where, grad, rows, normed, gain, down, factor, d_values, d_low, pair, inner, total):
    def kernel(*refs):
        group_kernel(first, *refs)

    return call(
        kernel,
        (ident, where),
        [grad, rows, normed, gain, down_of(down), factor, d_values, d_low, *pair, inner, total],
        [shape((ROWS, 2 * PART), BF), shape((ROWS, 128), F32), shape((ROWS, VALUES), F32)],
        8 * ROWS * PART * VALUES,
    )


def output_kernel(ident, where, total, low, up, rows, *refs):
    blocks, out = refs[:8], refs[8]
    values = (total[...] + SCALE * dot(low[...], up[0])).astype(BF)
    for i in range(8):
        span = columns(where[i])
        out[:, span] = (rows[:, span].astype(F32) + dot(values, blocks[i][...])).astype(BF)


def output(ident, where, total, low, up, rows, blocks):
    return call(
        output_kernel,
        (ident, where),
        [total, low, up_of(up), rows, *blocks],
        [shape((ROWS, WIDTH), BF)],
        2 * ROWS * WIDTH * VALUES,
    )[0]


def second_kernel(
    ident, where, p0, p1, p2, p3, mean, behind, out, target, low, normed, up, *refs
):
    blocks, (grad, d_values, d_low, mine, other) = refs[:8], refs[8:]
    last = where[9] == 1
    factor = mean[:, :1]
    parts = (p0, p1, p2, p3)
    total = jnp.zeros((ROWS, VALUES), F32)
    for i in range(8):
        span = columns(where[i])
        piece = parts[i // 2][:, (i % 2) * PART : (i % 2 + 1) * PART].astype(F32)
        relayed = piece - factor * behind[:, span].astype(F32)
        loss = out[:, span].astype(F32) - target[:, span].astype(F32)
        chosen = jnp.where(last, loss, relayed).astype(BF)
        grad[:, span] = chosen
        total += dot_t(chosen, blocks[i][...])
    values = total.astype(BF)
    lowered = (SCALE * dot_t(values, up[0])).astype(BF)
    d_values[...] = values
    d_low[...] = lowered
    pack_gradients(where, low[...], normed, values, lowered, mine, other)


def second_values(ident, where, parts, mean, behind, out, target, low, normed, up, blocks):
    return call(
        second_kernel,
        (ident, where),
        [*parts, mean, behind, out, target, low, normed, up_of(up), *blocks],
        [shape((ROWS, WIDTH), BF), shape((ROWS, VALUES), BF), shape((ROWS, RANK), BF), *PACKED],
        2 * ROWS * WIDTH * (VALUES + RANK),
    )


def input_kernel(ident, where, grad, rows, gain, down, factor, d_values, d_low, *refs):
    blocks, out, kept = refs[:8], refs[8], refs[9]
    scale = factor[:, :1]
    inner = jnp.zeros((ROWS, 1), F32)
    for i in range(8):
        span = columns(where[i])
        gained = (
            dot_t(d_values[...], blocks[i][...]) + dot(d_low[...], down[0, :, span])
        ) * gain[:, span]
        kept[i] = gained
        pre = rows[:, span].astype(F32) * scale
        inner += jnp.sum(gained * pre, axis=-1, keepdims=True)
    inner = inner * (1.0 / WIDTH)
    for i in range(8):
        span = columns(where[i])
        pre = rows[:, span].astype(F32) * scale
        out[:, span] = (
            grad[:, span].astype(F32) + scale * (kept[i] - pre * inner)
        ).astype(BF)


def input_gradient(ident, where, grad, rows, gain, down, factor, d_values, d_low, blocks):
    return call(
        input_kernel,
        (ident, where),
        [grad, rows, gain, down_of(down), factor, d_values, d_low, *blocks],
        [shape((ROWS, WIDTH), BF)],
        2 * ROWS * WIDTH * (VALUES + RANK),
        [pltpu.VMEM((8, ROWS, PART), F32)],
    )[0]


def forward_kernel(ident, where, fresh, passed, gain, down, up, *refs):
    value_blocks, out_blocks, out, rows, normed = refs[:8], refs[8:16], refs[16], refs[17], refs[18]
    first = where[8] == 1
    for top in range(0, ROWS, 32):
        part = slice(top, top + 32)
        whole = jnp.where(first, fresh[part, :], passed[part, :]).astype(F32)
        rows[part, :] = whole.astype(BF)
        normed[part, :] = (whole * factor_of(whole) * gain[...]).astype(BF)
    low = dot_t(normed[...], down[0]).astype(BF)
    total = SCALE * dot(low, up[0])
    for i in range(8):
        total += dot(normed[:, columns(where[i])], value_blocks[i][...])
    values = total.astype(BF)
    for i in range(8):
        span = columns(where[i])
        out[:, span] = (
            rows[:, span].astype(F32) + dot(values, out_blocks[i][...])
        ).astype(BF)


def forward(ident, where, fresh, passed, gain, down, up, value_blocks, out_blocks):
    return call(
        forward_kernel,
        (ident, where),
        [fresh, passed, gain, down_of(down), up_of(up), *value_blocks, *out_blocks],
        [shape((ROWS, WIDTH), BF)],
        4 * ROWS * WIDTH * VALUES,
        [pltpu.VMEM((ROWS, WIDTH), BF), pltpu.VMEM((ROWS, WIDTH), BF)],
    )[0]


def pair_sum_kernel(mine, other, own, one, two, three):
    for ahead, ref in enumerate((own, one, two, three)):
        total = mine[ahead].astype(F32) + other[ahead].astype(F32)
        ref[...] = total.astype(ref.dtype)


def spread(mine, other):
    received = lax.ppermute(other, "dp", CORE)
    block = (RANK, PACK)
    own, one, two, three = call(
        pair_sum_kernel, (), [mine, received],
        [shape(block, F32), shape(block, BF), shape(block, BF), shape(block, BF)], 0,
    )
    return (
        own,
        lax.ppermute(one, "dp", chips(1)),
        lax.ppermute(two, "dp", chips(2)),
        lax.ppermute(three, "dp", chips(3)),
    )


def tables_kernel(ident, other_ident, where, *refs):
    terms, (down, up) = refs[:8], refs[8:]
    core = where[0] % 2
    sums = []
    for tick in range(2):
        total = terms[4 * tick][...]
        for k in range(1, 4):
            total += terms[4 * tick + k][...].astype(F32)
        sums.append(total)
    for label in range(ADAPTERS):
        one = jnp.where(ident[0] == label, 1.0, 0.0)
        two = jnp.where(other_ident[0] == label, 1.0, 0.0)
        total = one * sums[0] + two * sums[1]
        down[label] = total[:, :PART]
        up[label] = jnp.where(core == 0, total[:, PART : PART + 64], total[:, PART + 64 :])


def tables(ident, other_ident, where, terms):
    return call(
        tables_kernel,
        (ident, other_ident, where),
        list(terms),
        [shape((ADAPTERS, RANK, PART), F32), shape((ADAPTERS, RANK, 64), F32)],
        0,
    )


CORE = [(i, i ^ 1) for i in range(8)]


def chips(by):
    return [(i, ((i // 2 + by) % 4) * 2 + i % 2) for i in range(8)]


def split_ring(sign):
    return [(i, ((i // 2 + (sign if i % 2 == 0 else -sign)) % 4) * 2 + i % 2) for i in range(8)]


def gather_blocks(own, gate=None):
    sent = own if gate is None else lax.optimization_barrier((own, gate))[0]
    sibling = lax.ppermute(own, "dp", CORE)
    near = lax.ppermute(sent, "dp", split_ring(1))
    away = lax.ppermute(sent, "dp", split_ring(-1))
    far = lax.ppermute(near, "dp", split_ring(1))
    return (
        own, sibling,
        near, lax.ppermute(near, "dp", CORE),
        away, lax.ppermute(away, "dp", CORE),
        far, lax.ppermute(far, "dp", CORE),
    )


def block_index():
    place = lax.axis_index("dp")
    chip, core = place // 2, place % 2
    other = 1 - core
    step = jnp.where(core == 0, 1, -1)
    block = lambda k, c: 2 * (k % 4) + c
    return [
        block(chip, core), block(chip, other),
        block(chip - step + 4, core), block(chip + step + 4, other),
        block(chip + step + 4, core), block(chip - step + 4, other),
        block(chip + 2, core), block(chip + 2, other),
    ]


def body(
    forward_state, backward_state, saved, fresh, target, forward_adapter, backward_adapter,
    value_projection, output_matrix, norm_gain_frozen, adapter_down, adapter_up,
):
    count = lax.axis_size("section")
    ahead = [(i, (i + 1) % count) for i in range(count)]
    before = [(i, i - 1) for i in range(1, count)]
    position = lax.axis_index("section")
    is_last = position == count - 1
    where = jnp.stack(
        [v.astype(jnp.int32) for v in (*block_index(), position == 0, is_last)]
    )
    gain = norm_gain_frozen
    down = jnp.swapaxes(adapter_down[0], 1, 2)
    up = adapter_up[0]
    rows_f, grad_b, rows_b = forward_state[0], backward_state[0], saved[0, 0]

    outs = gather_blocks(output_matrix[0])
    vals = gather_blocks(value_projection[0], outs[2])
    behind = lax.ppermute(rows_b, "section", before)
    passed_ident = lax.ppermute(forward_adapter, "section", ahead)
    returned_ident = lax.ppermute(backward_adapter, "section", before)
    grad_ident = jnp.where(is_last, forward_adapter, returned_ident)
    rows_n = jnp.where(is_last, rows_f, saved[0, 1])

    normed_f, _, low_f = prepare(rows_f, gain, down, forward_adapter)
    normed_b, factor_b, low_b = prepare(rows_b, gain, down, backward_adapter)
    normed_n, factor_n, low_n = prepare(rows_n, gain, down, grad_ident)

    d_values, d_low, mine, other = first_values(
        backward_adapter, where, grad_b, low_b, normed_b, up, outs
    )
    first_terms = spread(mine, other)

    inner = jnp.zeros((ROWS, 128), F32)
    total = jnp.zeros((ROWS, VALUES), F32)
    parts = []
    for first in range(0, 8, 2):
        part, inner, total = group(
            first, backward_adapter, where, grad_b, rows_b, normed_f, gain, down, factor_b,
            d_values, d_low, vals[first : first + 2], inner, total,
        )
        parts.append(lax.ppermute(part, "section", before))
    mean = lax.ppermute(inner, "section", before)

    first_out = output(forward_adapter, where, total, low_f, up, rows_f, outs)
    passed = lax.ppermute(first_out, "section", ahead)

    grad_n, d_values, d_low, mine, other = second_values(
        grad_ident, where, parts, mean, behind, first_out, target, low_n, normed_n, up, outs
    )
    second_terms = spread(mine, other)
    bwd_out = input_gradient(
        grad_ident, where, grad_n, rows_n, gain, down, factor_n, d_values, d_low, vals
    )
    fwd_out = forward(passed_ident, where, fresh, passed, gain, down, up, vals, outs)
    down_table, up_table = tables(
        backward_adapter, grad_ident, where, (*first_terms, *second_terms)
    )
    return (
        fwd_out[None], bwd_out[None], jnp.swapaxes(down_table, 1, 2)[None], up_table[None]
    )


def solution(mesh):
    return jax.shard_map(
        body,
        mesh=mesh,
        in_specs=(
            P("section", "dp", None),
            P("section", "dp", None),
            P("section", None, "dp", None),
            P("dp", None),
            P("dp", None),
            P("section"),
            P("section"),
            P("section", "dp", None),
            P("section", None, "dp"),
            P("section", None),
            P("section", None, None, None),
            P("section", None, None, None),
        ),
        out_specs=(
            P("section", "dp", None),
            P("section", "dp", None),
            P("section", None, "dp", None),
            P("section", None, None, "dp"),
        ),
        check_vma=False,
    )
```

```python
import jax
import jax.numpy as jnp
from jax import lax
from jax.experimental import pallas as pl
from jax.experimental.pallas import tpu as pltpu
from jax.sharding import PartitionSpec as P

SCALE = 0.5
EPS = 1e-05
BF = jnp.bfloat16
F32 = jnp.float32
ROWS = 128
WIDTH = 4096
VALUES = 512
PART = 512
RANK = 64
ADAPTERS = 4
PACK = PART + 128
LOWS = 256
WIDE = WIDTH + 128
VMEM = 20 * 1024 * 1024
ONCE = pl.Buffered(1)


def dot(left, right, dims=((1,), (0,))):
    return lax.dot_general(left, right, (dims, ((), ())), preferred_element_type=F32)


def dot_t(left, right):
    return dot(left, right, ((1,), (1,)))


def t_dot(left, right):
    return dot(left, right, ((0,), (0,)))


def call(kernel, scalars, ins, outs, flops, scratch=()):
    specs, arrays = [], []
    for item in ins:
        array, block, index = item if isinstance(item, tuple) else (item, None, None)
        arrays.append(array)
        if block is None:
            zeros = (0,) * array.ndim
            specs.append(pl.BlockSpec(array.shape, lambda i, *s, z=zeros: z, pipeline_mode=ONCE))
        else:
            specs.append(pl.BlockSpec(block, index, pipeline_mode=ONCE))
    out_specs = [
        pl.BlockSpec(o.shape, lambda i, *s, z=(0,) * len(o.shape): z, pipeline_mode=ONCE)
        for o in outs
    ]
    size = sum(a.size * a.dtype.itemsize for a in arrays)
    return pl.pallas_call(
        kernel,
        out_shape=outs,
        grid_spec=pltpu.PrefetchScalarGridSpec(
            num_scalar_prefetch=len(scalars),
            grid=(1,),
            in_specs=specs,
            out_specs=out_specs,
            scratch_shapes=list(scratch),
        ),
        compiler_params=pltpu.CompilerParams(vmem_limit_bytes=VMEM),
        cost_estimate=pl.CostEstimate(
            flops=flops // 1000, bytes_accessed=size // 1000, transcendentals=0
        ),
    )(*scalars, *arrays)


def shape(dims, dtype):
    return jax.ShapeDtypeStruct(dims, dtype)


def factor_of(rows):
    return lax.rsqrt(jnp.sum(rows * rows, axis=-1, keepdims=True) * (1.0 / WIDTH) + EPS)


def columns(index):
    return pl.ds(pl.multiple_of(index * PART, PART), PART)


def only(lows, ident):
    lane = lax.broadcasted_iota(jnp.int32, lows.shape, 1)
    return jnp.where(lane // RANK == ident, lows, jnp.zeros_like(lows))


def compact(lows):
    total = lows[:, :RANK].astype(F32)
    for k in range(1, ADAPTERS):
        total += lows[:, k * RANK : (k + 1) * RANK].astype(F32)
    return total.astype(BF)


def saved_of(saved, which):
    return (saved, (1, 1, ROWS, WIDTH), lambda i, *s: (0, which, 0, 0))


def prepare_kernel(ahead, back, where, rows_f, rows_b, rows_s, gain, down, *refs):
    last = where[9] == 1
    for kind in range(3):
        normed, factor, low = refs[3 * kind : 3 * kind + 3]
        for top in range(0, ROWS, 32):
            part = slice(top, top + 32)
            if kind == 0:
                whole = rows_f[part, :]
            elif kind == 1:
                whole = rows_b[0, 0, part, :]
            else:
                whole = jnp.where(last, rows_f[part, :], rows_s[0, 0, part, :])
            whole = whole.astype(F32)
            scale = factor_of(whole)
            normed[part, :] = (whole * scale * gain[...]).astype(BF)
            factor[part, :] = jnp.broadcast_to(scale, (32, 128))
        lows = dot_t(normed[...], down[...])
        if kind == 0:
            lows = only(lows, ahead[0])
        elif kind == 1:
            lows = only(lows, back[0])
        low[...] = lows.astype(BF)


def prepare(ahead, back, where, rows, saved, gain, down):
    kinds = [shape((ROWS, WIDTH), BF), shape((ROWS, 128), F32), shape((ROWS, LOWS), BF)]
    return call(
        prepare_kernel,
        (ahead, back, where),
        [rows, saved_of(saved, 0), saved_of(saved, 1), gain, down],
        kinds * 3,
        6 * ROWS * WIDTH * LOWS,
    )


def near_kernel(where, grad, normed, *refs):
    outs, vals, (gradients, values) = refs[:6], refs[6:12], refs[12:]
    total = jnp.zeros((ROWS, VALUES), F32)
    for i in range(6):
        total += dot_t(grad[:, columns(where[i])], outs[i][...])
    gradients[...] = total
    total = jnp.zeros((ROWS, VALUES), F32)
    for i in range(6):
        total += dot(normed[:, columns(where[i])], vals[i][...])
    values[...] = total


def near_share(where, grad, normed, outs, vals):
    return call(
        near_kernel,
        (where,),
        [grad, normed, *outs, *vals],
        [shape((ROWS, VALUES), F32)] * 2,
        4 * ROWS * WIDTH * VALUES,
    )


def input_gradient(where, values, lowered, grad, rows, gain, down, scale, blocks, kept, out):
    inner = jnp.zeros((ROWS, 1), F32)
    for i in range(8):
        span = columns(where[i])
        gained = (
            dot_t(values, blocks[i][...]) + dot(lowered, down[:, span])
        ) * gain[:, span]
        kept[i] = gained
        pre = rows(span).astype(F32) * scale
        inner += jnp.sum(gained * pre, axis=-1, keepdims=True)
    inner = inner * (1.0 / WIDTH)
    for i in range(8):
        span = columns(where[i])
        pre = rows(span).astype(F32) * scale
        out[:, span] = (
            grad[:, span].astype(F32) + scale * (kept[i] - pre * inner)
        ).astype(BF)


def first_kernel(
    back, where, share, grad, rows, factor, gain, down, up, far, far_other, *refs
):
    blocks, (out, d_values, d_low, kept) = refs[:8], refs[8:]
    total = share[...]
    total += dot_t(grad[:, columns(where[6])], far[...])
    total += dot_t(grad[:, columns(where[7])], far_other[...])
    values = total.astype(BF)
    lowered = only(SCALE * dot_t(values, up[...]), back[0]).astype(BF)
    d_values[...] = values
    d_low[...] = lowered
    input_gradient(
        where, values, lowered, grad, lambda span: rows[0, 0, :, span], gain, down,
        factor[:, :1], blocks, kept, out,
    )
    out[:, WIDTH:] = jnp.full((ROWS, 128), back[0], jnp.int32).astype(F32).astype(BF)


KEPT = [pltpu.VMEM((8, ROWS, PART), F32)]
GRADS = [shape((ROWS, VALUES), BF), shape((ROWS, LOWS), BF)]


def first_gradient(back, where, share, grad, saved, factor, gain, down, up, outs, vals):
    return call(
        first_kernel,
        (back, where),
        [share, grad, saved_of(saved, 0), factor, gain, down, up, *outs[6:], *vals],
        [shape((ROWS, WIDE), BF), *GRADS],
        2 * ROWS * WIDTH * VALUES,
        KEPT,
    )


def output_kernel(ahead, where, share, normed, low, up, rows, far, far_other, *refs):
    blocks, out = refs[:8], refs[8]
    total = share[...] + SCALE * dot(low[...], up[...])
    total += dot(normed[:, columns(where[6])], far[...])
    total += dot(normed[:, columns(where[7])], far_other[...])
    values = total.astype(BF)
    for i in range(8):
        span = columns(where[i])
        out[:, span] = (rows[:, span].astype(F32) + dot(values, blocks[i][...])).astype(BF)
    out[:, WIDTH:] = jnp.full((ROWS, 128), ahead[0], jnp.int32).astype(F32).astype(BF)


def output(ahead, where, share, normed, low, up, rows, outs, vals):
    return call(
        output_kernel,
        (ahead, where),
        [share, normed, low, up, rows, *vals[6:], *outs],
        [shape((ROWS, WIDE), BF)],
        2 * ROWS * WIDTH * VALUES,
    )[0]


def pack_gradients(where, low, normed, d_values, d_low, mine, other):
    up_term = SCALE * t_dot(low, d_values)
    chip, core = where[0] // 2, where[0] % 2
    for ahead in range(4):
        target = lax.rem(chip + ahead, 4)
        pair = up_term[:, 0:128]
        for k in range(1, 4):
            pair = jnp.where(target == k, up_term[:, 128 * k : 128 * (k + 1)], pair)
        pair = pair.astype(BF)
        for ref, c in ((mine, core), (other, 1 - core)):
            ref[ahead, :, :PART] = t_dot(d_low, normed[:, columns(2 * target + c)]).astype(BF)
            ref[ahead, :, PART:] = pair


PACKED = [shape((4, RANK, PACK), BF)] * 2


def pack_kernel(where, low, normed, d_values, d_low, mine, other):
    pack_gradients(
        where, compact(low[...]), normed, d_values[...], compact(d_low[...]), mine, other
    )


def pack(where, low, normed, d_values, d_low):
    return call(
        pack_kernel, (where,), [low, normed, d_values, d_low], PACKED, 2 * ROWS * WIDTH * RANK
    )


def second_kernel(ahead, where, relayed, out, target, low, normed, up, *refs):
    blocks, (grad, d_values, d_low, mine, other) = refs[:8], refs[8:]
    last = where[9] == 1
    total = jnp.zeros((ROWS, VALUES), F32)
    for i in range(8):
        span = columns(where[i])
        loss = (out[:, span].astype(F32) - target[:, span].astype(F32)).astype(BF)
        chosen = jnp.where(last, loss, relayed[:, span])
        grad[:, span] = chosen
        total += dot_t(chosen, blocks[i][...])
    values = total.astype(BF)
    came = relayed[:, WIDTH : WIDTH + 1].astype(F32).astype(jnp.int32)
    ident = jnp.where(last, ahead[0], came)
    lowered = only(SCALE * dot_t(values, up[...]), ident).astype(BF)
    d_values[...] = values
    d_low[...] = lowered
    pack_gradients(
        where, compact(only(low[...], ident)), normed, values, compact(lowered), mine, other
    )


def second_values(ahead, where, relayed, out, target, low, normed, up, blocks):
    return call(
        second_kernel,
        (ahead, where),
        [relayed, out, target, low, normed, up, *blocks],
        [shape((ROWS, WIDTH), BF), *GRADS, *PACKED],
        2 * ROWS * WIDTH * (VALUES + RANK),
    )


def second_input_kernel(where, grad, rows_f, rows_s, factor, gain, down, d_values, d_low, *refs):
    blocks, (out, kept) = refs[:8], refs[8:]
    last = where[9] == 1
    input_gradient(
        where, d_values[...], d_low[...], grad,
        lambda span: jnp.where(last, rows_f[:, span], rows_s[0, 0, :, span]),
        gain, down, factor[:, :1], blocks, kept, out,
    )


def second_input(where, grad, rows, saved, factor, gain, down, d_values, d_low, blocks):
    return call(
        second_input_kernel,
        (where,),
        [grad, rows, saved_of(saved, 1), factor, gain, down, d_values, d_low, *blocks],
        [shape((ROWS, WIDTH), BF)],
        2 * ROWS * WIDTH * (VALUES + RANK),
        KEPT,
    )[0]


def forward_kernel(where, fresh, passed, gain, down, up, *refs):
    vals, outs, (out, rows, normed) = refs[:8], refs[8:16], refs[16:]
    first = where[8] == 1
    for top in range(0, ROWS, 32):
        part = slice(top, top + 32)
        chosen = jnp.where(first, fresh[part, :], passed[part, :WIDTH])
        whole = chosen.astype(F32)
        rows[part, :] = chosen
        normed[part, :] = (whole * factor_of(whole) * gain[...]).astype(BF)
    ident = passed[:, WIDTH : WIDTH + 1].astype(F32).astype(jnp.int32)
    low = only(dot_t(normed[...], down[...]), ident).astype(BF)
    total = SCALE * dot(low, up[...])
    for i in range(8):
        total += dot(normed[:, columns(where[i])], vals[i][...])
    values = total.astype(BF)
    for i in range(8):
        span = columns(where[i])
        out[:, span] = (rows[:, span].astype(F32) + dot(values, outs[i][...])).astype(BF)


def forward(where, fresh, passed, gain, down, up, vals, outs):
    return call(
        forward_kernel,
        (where,),
        [fresh, passed, gain, down, up, *vals, *outs],
        [shape((ROWS, WIDTH), BF)],
        4 * ROWS * WIDTH * VALUES,
        [pltpu.VMEM((ROWS, WIDTH), BF), pltpu.VMEM((ROWS, WIDTH), BF)],
    )[0]


def pair_sum_kernel(mine, other, own, one, two, three):
    for ahead, ref in enumerate((own, one, two, three)):
        ref[...] = (mine[ahead].astype(F32) + other[ahead].astype(F32)).astype(BF)


def spread(mine, received):
    block = shape((RANK, PACK), BF)
    own, one, two, three = call(pair_sum_kernel, (), [mine, received], [block] * 4, 0)
    return (
        own,
        lax.ppermute(two, "dp", chips(2)),
        lax.ppermute(one, "dp", chips(1)),
        lax.ppermute(three, "dp", chips(3)),
    )


def tables_kernel(ahead, back, where, relayed, *refs):
    terms, (down, up) = refs[:8], refs[8:]
    core = where[0] % 2
    came = relayed[:RANK, :1].astype(F32).astype(jnp.int32)
    ident = jnp.where(where[9] == 1, ahead[0], came)
    sums = []
    for tick in range(2):
        total = terms[4 * tick][...].astype(F32)
        for k in range(1, 4):
            total += terms[4 * tick + k][...].astype(F32)
        sums.append(total)
    for label in range(ADAPTERS):
        one = jnp.where(back[0] == label, 1.0, 0.0)
        two = jnp.where(ident == label, 1.0, 0.0)
        total = one * sums[0] + two * sums[1]
        down[label] = total[:, :PART]
        up[label] = jnp.where(core == 0, total[:, PART : PART + 64], total[:, PART + 64 :])


def tables(ahead, back, where, relayed, terms):
    tail = (relayed, (ROWS, 128), lambda i, *s: (0, WIDTH // 128))
    return call(
        tables_kernel,
        (ahead, back, where),
        [tail, *terms],
        [shape((ADAPTERS, RANK, PART), F32), shape((ADAPTERS, RANK, 64), F32)],
        0,
    )


CORE = [(i, i ^ 1) for i in range(8)]


def chips(by):
    return [(i, ((i // 2 + by) % 4) * 2 + i % 2) for i in range(8)]


def split_ring(sign):
    return [(i, ((i // 2 + (sign if i % 2 == 0 else -sign)) % 4) * 2 + i % 2) for i in range(8)]


def send(block, pairs):
    return lax.ppermute(block, "dp", pairs)


def block_index():
    place = lax.axis_index("dp")
    chip, core = place // 2, place % 2
    other = 1 - core
    step = jnp.where(core == 0, 1, -1)
    block = lambda k, c: 2 * (k % 4) + c
    return [
        block(chip, core), block(chip, other),
        block(chip - step + 4, core), block(chip + step + 4, other),
        block(chip + step + 4, core), block(chip - step + 4, other),
        block(chip + 2, core), block(chip + 2, other),
    ]


def body(
    forward_state, backward_state, saved, fresh, target, forward_adapter, backward_adapter,
    value_projection, output_matrix, norm_gain_frozen, adapter_down, adapter_up,
):
    count = lax.axis_size("section")
    onward = [(i, (i + 1) % count) for i in range(count)]
    before = [(i, i - 1) for i in range(1, count)]
    position = lax.axis_index("section")
    where = jnp.stack(
        [v.astype(jnp.int32) for v in (*block_index(), position == 0, position == count - 1)]
    )
    gain = norm_gain_frozen
    down = jnp.swapaxes(adapter_down[0], 1, 2).reshape(LOWS, WIDTH)
    up = adapter_up[0].reshape(LOWS, VALUES)
    rows, grad = forward_state[0], backward_state[0]
    ahead, back = forward_adapter, backward_adapter

    out_own, val_own = output_matrix[0], value_projection[0]
    out_near, out_away = send(out_own, split_ring(1)), send(out_own, split_ring(-1))
    val_near, val_away = send(val_own, split_ring(1)), send(val_own, split_ring(-1))
    out_sibling, val_sibling = send(out_own, CORE), send(val_own, CORE)

    normed_f, _, low_f, normed_b, factor_b, low_b, normed_n, factor_n, low_n = prepare(
        ahead, back, where, rows, saved, gain, down
    )
    out_near, normed_f = lax.optimization_barrier((out_near, normed_f))
    out_far, val_far = send(out_near, split_ring(1)), send(val_near, split_ring(1))
    outs = [
        out_own, out_sibling, out_near, send(out_near, CORE), out_away, send(out_away, CORE)
    ]
    vals = [
        val_own, val_sibling, val_near, send(val_near, CORE), val_away, send(val_away, CORE)
    ]
    share_b, share_f = near_share(where, grad, normed_f, outs, vals)
    out_far, val_far, share_b = lax.optimization_barrier((out_far, val_far, share_b))
    outs += [out_far, send(out_far, CORE)]
    vals += [val_far, send(val_far, CORE)]

    first_back, d_values, d_low = first_gradient(
        back, where, share_b, grad, saved, factor_b, gain, down, up, outs, vals
    )
    relayed = lax.ppermute(first_back, "section", before)
    share_f, d_values = lax.optimization_barrier((share_f, d_values))
    first_out = output(ahead, where, share_f, normed_f, low_f, up, rows, outs, vals)
    passed = lax.ppermute(first_out, "section", onward)
    d_low, first_out = lax.optimization_barrier((d_low, first_out))
    mine, other = pack(where, low_b, normed_b, d_values, d_low)
    first_terms = spread(mine, send(other, CORE))
    relayed, *first_terms = lax.optimization_barrier((relayed, *first_terms))

    grad_n, d_values, d_low, mine, other = second_values(
        ahead, where, relayed, first_out, target, low_n, normed_n, up, outs
    )
    received = send(other, CORE)
    second_terms = spread(mine, received)
    bwd_out = second_input(
        where, grad_n, rows, saved, factor_n, gain, down, d_values, d_low, vals
    )
    fwd_out = forward(where, fresh, passed, gain, down, up, vals, outs)
    down_table, up_table = tables(ahead, back, where, relayed, (*first_terms, *second_terms))
    return (
        fwd_out[None], bwd_out[None], jnp.swapaxes(down_table, 1, 2)[None], up_table[None]
    )


def solution(mesh):
    return jax.shard_map(
        body,
        mesh=mesh,
        in_specs=(
            P("section", "dp", None),
            P("section", "dp", None),
            P("section", None, "dp", None),
            P("dp", None),
            P("dp", None),
            P("section"),
            P("section"),
            P("section", "dp", None),
            P("section", None, "dp"),
            P("section", None),
            P("section", None, None, None),
            P("section", None, None, None),
        ),
        out_specs=(
            P("section", "dp", None),
            P("section", "dp", None),
            P("section", None, "dp", None),
            P("section", None, None, "dp"),
        ),
        check_vma=False,
    )
```

```python
import jax
import jax.numpy as jnp
from jax import lax
from jax.experimental import pallas as pl
from jax.experimental.pallas import tpu as pltpu
from jax.sharding import PartitionSpec as P

SCALE = 0.5
EPS = 1e-05
BF = jnp.bfloat16
F32 = jnp.float32
ROWS = 128
WIDTH = 4096
VALUES = 512
PART = 512
RANK = 64
ADAPTERS = 4
PACK = PART + 128
LOWS = 256
WIDE = WIDTH + 128
VMEM = 20 * 1024 * 1024
ONCE = pl.Buffered(1)


def dot(left, right, dims=((1,), (0,))):
    return lax.dot_general(left, right, (dims, ((), ())), preferred_element_type=F32)


def dot_t(left, right):
    return dot(left, right, ((1,), (1,)))


def t_dot(left, right):
    return dot(left, right, ((0,), (0,)))


def call(kernel, scalars, ins, outs, flops, scratch=()):
    specs, arrays = [], []
    for item in ins:
        array, block, index = item if isinstance(item, tuple) else (item, None, None)
        arrays.append(array)
        if block is None:
            zeros = (0,) * array.ndim
            specs.append(pl.BlockSpec(array.shape, lambda i, *s, z=zeros: z, pipeline_mode=ONCE))
        else:
            specs.append(pl.BlockSpec(block, index, pipeline_mode=ONCE))
    out_specs = [
        pl.BlockSpec(o.shape, lambda i, *s, z=(0,) * len(o.shape): z, pipeline_mode=ONCE)
        for o in outs
    ]
    size = sum(a.size * a.dtype.itemsize for a in arrays)
    return pl.pallas_call(
        kernel,
        out_shape=outs,
        grid_spec=pltpu.PrefetchScalarGridSpec(
            num_scalar_prefetch=len(scalars),
            grid=(1,),
            in_specs=specs,
            out_specs=out_specs,
            scratch_shapes=list(scratch),
        ),
        compiler_params=pltpu.CompilerParams(vmem_limit_bytes=VMEM),
        cost_estimate=pl.CostEstimate(
            flops=flops // 1000, bytes_accessed=size // 1000, transcendentals=0
        ),
    )(*scalars, *arrays)


def shape(dims, dtype):
    return jax.ShapeDtypeStruct(dims, dtype)


def factor_of(rows):
    return lax.rsqrt(jnp.sum(rows * rows, axis=-1, keepdims=True) * (1.0 / WIDTH) + EPS)


def columns(index):
    return pl.ds(pl.multiple_of(index * PART, PART), PART)


def only(lows, ident):
    lane = lax.broadcasted_iota(jnp.int32, lows.shape, 1)
    return jnp.where(lane // RANK == ident, lows, jnp.zeros_like(lows))


def compact(lows):
    total = lows[:, :RANK].astype(F32)
    for k in range(1, ADAPTERS):
        total += lows[:, k * RANK : (k + 1) * RANK].astype(F32)
    return total.astype(BF)


def saved_of(saved, which):
    return (saved, (1, 1, ROWS, WIDTH), lambda i, *s: (0, which, 0, 0))


def prepare_kernel(ahead, back, where, rows_f, rows_b, rows_s, gain, down, *refs):
    last = where[9] == 1
    for kind in range(3):
        normed, factor, low = refs[3 * kind : 3 * kind + 3]
        for top in range(0, ROWS, 32):
            part = slice(top, top + 32)
            if kind == 0:
                whole = rows_f[part, :]
            elif kind == 1:
                whole = rows_b[0, 0, part, :]
            else:
                whole = jnp.where(last, rows_f[part, :], rows_s[0, 0, part, :])
            whole = whole.astype(F32)
            scale = factor_of(whole)
            normed[part, :] = (whole * scale * gain[...]).astype(BF)
            factor[part, :] = jnp.broadcast_to(scale, (32, 128))
        lows = dot_t(normed[...], down[...])
        if kind == 0:
            lows = only(lows, ahead[0])
        elif kind == 1:
            lows = only(lows, back[0])
        low[...] = lows.astype(BF)


def prepare(ahead, back, where, rows, saved, gain, down):
    kinds = [shape((ROWS, WIDTH), BF), shape((ROWS, 128), F32), shape((ROWS, LOWS), BF)]
    return call(
        prepare_kernel,
        (ahead, back, where),
        [rows, saved_of(saved, 0), saved_of(saved, 1), gain, down],
        kinds * 3,
        6 * ROWS * WIDTH * LOWS,
    )


def gained_block(values, lowered, span, gain, down, block):
    return (dot_t(values, block[...]) + dot(lowered, down[:, span])) * gain[:, span]


def input_gradient(where, grad, rows, scale, inner, gained, out):
    inner = inner * (1.0 / WIDTH)
    for i in range(8):
        span = columns(where[i])
        pre = rows(span).astype(F32) * scale
        out[:, span] = (
            grad[:, span].astype(F32) + scale * (gained(i) - pre * inner)
        ).astype(BF)


def near_kernel(back, where, grad, normed, rows, factor, gain, down, up, *refs):
    outs, vals, (d_values, d_low, kept, inner, share) = refs[:8], refs[8:14], refs[14:]
    total = jnp.zeros((ROWS, VALUES), F32)
    for i in range(8):
        total += dot_t(grad[:, columns(where[i])], outs[i][...])
    values = total.astype(BF)
    lowered = only(SCALE * dot_t(values, up[...]), back[0]).astype(BF)
    d_values[...] = values
    d_low[...] = lowered
    scale = factor[:, :1]
    mean = jnp.zeros((ROWS, 1), F32)
    for i in range(6):
        span = columns(where[i])
        gained = gained_block(values, lowered, span, gain, down, vals[i])
        kept[i] = gained
        mean += jnp.sum(
            gained * (rows[0, 0, :, span].astype(F32) * scale), axis=-1, keepdims=True
        )
    inner[...] = jnp.broadcast_to(mean, (ROWS, 128))
    total = jnp.zeros((ROWS, VALUES), F32)
    for i in range(6):
        total += dot(normed[:, columns(where[i])], vals[i][...])
    share[...] = total


GRADS = [shape((ROWS, VALUES), BF), shape((ROWS, LOWS), BF)]
KEPT = [pltpu.VMEM((8, ROWS, PART), F32)]


def near_share(back, where, grad, normed, saved, factor, gain, down, up, outs, vals):
    return call(
        near_kernel,
        (back, where),
        [grad, normed, saved_of(saved, 0), factor, gain, down, up, *outs, *vals],
        [*GRADS, shape((6, ROWS, PART), F32), shape((ROWS, 128), F32), shape((ROWS, VALUES), F32)],
        6 * ROWS * WIDTH * VALUES,
    )


def first_kernel(
    back, where, kept, inner, values, lowered, grad, rows, factor, gain, down, far, far_other, out
):
    scale = factor[:, :1]
    mean = inner[:, :1]
    last = []
    for i, block in ((6, far), (7, far_other)):
        span = columns(where[i])
        gained = gained_block(values[...], lowered[...], span, gain, down, block)
        mean += jnp.sum(
            gained * (rows[0, 0, :, span].astype(F32) * scale), axis=-1, keepdims=True
        )
        last.append(gained)
    input_gradient(
        where, grad, lambda span: rows[0, 0, :, span], scale, mean,
        lambda i: kept[i] if i < 6 else last[i - 6], out,
    )
    out[:, WIDTH:] = jnp.full((ROWS, 128), back[0], jnp.int32).astype(F32).astype(BF)


def first_gradient(back, where, kept, inner, d_values, d_low, grad, saved, factor, gain, down, vals):
    return call(
        first_kernel,
        (back, where),
        [
            kept, inner, d_values, d_low, grad, saved_of(saved, 0), factor, gain, down, *vals[6:]
        ],
        [shape((ROWS, WIDE), BF)],
        ROWS * WIDTH * VALUES,
    )[0]


def output_kernel(ahead, where, share, normed, low, up, rows, far, far_other, *refs):
    blocks, out = refs[:8], refs[8]
    total = share[...] + SCALE * dot(low[...], up[...])
    total += dot(normed[:, columns(where[6])], far[...])
    total += dot(normed[:, columns(where[7])], far_other[...])
    values = total.astype(BF)
    for i in range(8):
        span = columns(where[i])
        out[:, span] = (rows[:, span].astype(F32) + dot(values, blocks[i][...])).astype(BF)
    out[:, WIDTH:] = jnp.full((ROWS, 128), ahead[0], jnp.int32).astype(F32).astype(BF)


def output(ahead, where, share, normed, low, up, rows, outs, vals):
    return call(
        output_kernel,
        (ahead, where),
        [share, normed, low, up, rows, *vals[6:], *outs],
        [shape((ROWS, WIDE), BF)],
        2 * ROWS * WIDTH * VALUES,
    )[0]


def pack_gradients(where, low, normed, d_values, d_low, mine, other):
    up_term = SCALE * t_dot(low, d_values)
    chip, core = where[0] // 2, where[0] % 2
    for ahead in range(4):
        target = lax.rem(chip + ahead, 4)
        pair = up_term[:, 0:128]
        for k in range(1, 4):
            pair = jnp.where(target == k, up_term[:, 128 * k : 128 * (k + 1)], pair)
        pair = pair.astype(BF)
        for ref, c in ((mine, core), (other, 1 - core)):
            ref[ahead, :, :PART] = t_dot(d_low, normed[:, columns(2 * target + c)]).astype(BF)
            ref[ahead, :, PART:] = pair


PACKED = [shape((4, RANK, PACK), BF)] * 2


def pack_kernel(where, low, normed, d_values, d_low, mine, other):
    pack_gradients(
        where, compact(low[...]), normed, d_values[...], compact(d_low[...]), mine, other
    )


def pack(where, low, normed, d_values, d_low):
    return call(
        pack_kernel, (where,), [low, normed, d_values, d_low], PACKED, 2 * ROWS * WIDTH * RANK
    )


def second_kernel(ahead, where, relayed, out, target, low, normed, up, *refs):
    blocks, (grad, d_values, d_low, mine, other) = refs[:8], refs[8:]
    last = where[9] == 1
    total = jnp.zeros((ROWS, VALUES), F32)
    for i in range(8):
        span = columns(where[i])
        loss = (out[:, span].astype(F32) - target[:, span].astype(F32)).astype(BF)
        chosen = jnp.where(last, loss, relayed[:, span])
        grad[:, span] = chosen
        total += dot_t(chosen, blocks[i][...])
    values = total.astype(BF)
    came = relayed[:, WIDTH : WIDTH + 1].astype(F32).astype(jnp.int32)
    ident = jnp.where(last, ahead[0], came)
    lowered = only(SCALE * dot_t(values, up[...]), ident).astype(BF)
    d_values[...] = values
    d_low[...] = lowered
    pack_gradients(
        where, compact(only(low[...], ident)), normed, values, compact(lowered), mine, other
    )


def second_values(ahead, where, relayed, out, target, low, normed, up, blocks):
    return call(
        second_kernel,
        (ahead, where),
        [relayed, out, target, low, normed, up, *blocks],
        [shape((ROWS, WIDTH), BF), *GRADS, *PACKED],
        2 * ROWS * WIDTH * (VALUES + RANK),
    )


def second_input_kernel(where, grad, rows_f, rows_s, factor, gain, down, d_values, d_low, *refs):
    blocks, (out, kept) = refs[:8], refs[8:]
    last = where[9] == 1
    scale = factor[:, :1]
    rows = lambda span: jnp.where(last, rows_f[:, span], rows_s[0, 0, :, span])
    mean = jnp.zeros((ROWS, 1), F32)
    for i in range(8):
        span = columns(where[i])
        gained = gained_block(d_values[...], d_low[...], span, gain, down, blocks[i])
        kept[i] = gained
        mean += jnp.sum(gained * (rows(span).astype(F32) * scale), axis=-1, keepdims=True)
    input_gradient(where, grad, rows, scale, mean, lambda i: kept[i], out)


def second_input(where, grad, rows, saved, factor, gain, down, d_values, d_low, blocks):
    return call(
        second_input_kernel,
        (where,),
        [grad, rows, saved_of(saved, 1), factor, gain, down, d_values, d_low, *blocks],
        [shape((ROWS, WIDTH), BF)],
        2 * ROWS * WIDTH * (VALUES + RANK),
        KEPT,
    )[0]


def forward_kernel(where, fresh, passed, gain, down, up, *refs):
    vals, outs, (out, rows, normed) = refs[:8], refs[8:16], refs[16:]
    first = where[8] == 1
    for top in range(0, ROWS, 32):
        part = slice(top, top + 32)
        chosen = jnp.where(first, fresh[part, :], passed[part, :WIDTH])
        whole = chosen.astype(F32)
        rows[part, :] = chosen
        normed[part, :] = (whole * factor_of(whole) * gain[...]).astype(BF)
    ident = passed[:, WIDTH : WIDTH + 1].astype(F32).astype(jnp.int32)
    low = only(dot_t(normed[...], down[...]), ident).astype(BF)
    total = SCALE * dot(low, up[...])
    for i in range(8):
        total += dot(normed[:, columns(where[i])], vals[i][...])
    values = total.astype(BF)
    for i in range(8):
        span = columns(where[i])
        out[:, span] = (rows[:, span].astype(F32) + dot(values, outs[i][...])).astype(BF)


def forward(where, fresh, passed, gain, down, up, vals, outs):
    return call(
        forward_kernel,
        (where,),
        [fresh, passed, gain, down, up, *vals, *outs],
        [shape((ROWS, WIDTH), BF)],
        4 * ROWS * WIDTH * VALUES,
        [pltpu.VMEM((ROWS, WIDTH), BF), pltpu.VMEM((ROWS, WIDTH), BF)],
    )[0]


def pair_sum_kernel(mine, other, total):
    total[...] = (mine[...].astype(F32) + other[...].astype(F32)).astype(BF)


def pair_sum(mine, other):
    return call(pair_sum_kernel, (), [mine, other], [shape((4, RANK, PACK), BF)], 0)[0]


def stack_kernel(first, mine, other, own, one, two, three):
    for ahead, ref in enumerate((own, one, two, three)):
        ref[0] = first[ahead]
        ref[1] = (mine[ahead].astype(F32) + other[ahead].astype(F32)).astype(BF)


def spread(first, mine, received):
    block = shape((2, RANK, PACK), BF)
    own, one, two, three = call(stack_kernel, (), [first, mine, received], [block] * 4, 0)
    return (
        own,
        lax.ppermute(two, "dp", chips(2)),
        lax.ppermute(one, "dp", chips(1)),
        lax.ppermute(three, "dp", chips(3)),
    )


def tables_kernel(ahead, back, where, relayed, *refs):
    terms, (down, up) = refs[:4], refs[4:]
    core = where[0] % 2
    came = relayed[:RANK, :1].astype(F32).astype(jnp.int32)
    ident = jnp.where(where[9] == 1, ahead[0], came)
    sums = []
    for tick in range(2):
        total = terms[0][tick].astype(F32)
        for k in range(1, 4):
            total += terms[k][tick].astype(F32)
        sums.append(total)
    for label in range(ADAPTERS):
        one = jnp.where(back[0] == label, 1.0, 0.0)
        two = jnp.where(ident == label, 1.0, 0.0)
        total = one * sums[0] + two * sums[1]
        down[label] = total[:, :PART]
        up[label] = jnp.where(core == 0, total[:, PART : PART + 64], total[:, PART + 64 :])


def tables(ahead, back, where, relayed, terms):
    tail = (relayed, (ROWS, 128), lambda i, *s: (0, WIDTH // 128))
    return call(
        tables_kernel,
        (ahead, back, where),
        [tail, *terms],
        [shape((ADAPTERS, RANK, PART), F32), shape((ADAPTERS, RANK, 64), F32)],
        0,
    )


CORE = [(i, i ^ 1) for i in range(8)]


def chips(by):
    return [(i, ((i // 2 + by) % 4) * 2 + i % 2) for i in range(8)]


def split_ring(sign):
    return [(i, ((i // 2 + (sign if i % 2 == 0 else -sign)) % 4) * 2 + i % 2) for i in range(8)]


def send(block, pairs):
    return lax.ppermute(block, "dp", pairs)


def block_index():
    place = lax.axis_index("dp")
    chip, core = place // 2, place % 2
    other = 1 - core
    step = jnp.where(core == 0, 1, -1)
    block = lambda k, c: 2 * (k % 4) + c
    return [
        block(chip, core), block(chip, other),
        block(chip - step + 4, core), block(chip + step + 4, other),
        block(chip + step + 4, core), block(chip - step + 4, other),
        block(chip + 2, core), block(chip + 2, other),
    ]


def body(
    forward_state, backward_state, saved, fresh, target, forward_adapter, backward_adapter,
    value_projection, output_matrix, norm_gain_frozen, adapter_down, adapter_up,
):
    count = lax.axis_size("section")
    onward = [(i, (i + 1) % count) for i in range(count)]
    before = [(i, i - 1) for i in range(1, count)]
    position = lax.axis_index("section")
    where = jnp.stack(
        [v.astype(jnp.int32) for v in (*block_index(), position == 0, position == count - 1)]
    )
    gain = norm_gain_frozen
    down = jnp.swapaxes(adapter_down[0], 1, 2).reshape(LOWS, WIDTH)
    up = adapter_up[0].reshape(LOWS, VALUES)
    rows, grad = forward_state[0], backward_state[0]
    ahead, back = forward_adapter, backward_adapter

    out_own, val_own = output_matrix[0], value_projection[0]
    out_near, out_away = send(out_own, split_ring(1)), send(out_own, split_ring(-1))
    val_near, val_away = send(val_own, split_ring(1)), send(val_own, split_ring(-1))
    out_sibling, val_sibling = send(out_own, CORE), send(val_own, CORE)

    normed_f, _, low_f, normed_b, factor_b, low_b, normed_n, factor_n, low_n = prepare(
        ahead, back, where, rows, saved, gain, down
    )
    out_near, normed_f = lax.optimization_barrier((out_near, normed_f))
    out_far, val_far = send(out_near, split_ring(1)), send(val_near, split_ring(1))
    outs = [
        out_own, out_sibling, out_near, send(out_near, CORE), out_away, send(out_away, CORE)
    ]
    vals = [
        val_own, val_sibling, val_near, send(val_near, CORE), val_away, send(val_away, CORE)
    ]
    outs += [out_far, send(out_far, CORE)]
    d_values, d_low, kept, inner, share_f = near_share(
        back, where, grad, normed_f, saved, factor_b, gain, down, up, outs, vals
    )
    mine, other = pack(where, low_b, normed_b, d_values, d_low)
    first_sums = pair_sum(mine, send(other, CORE))
    val_far, first_sums = lax.optimization_barrier((val_far, first_sums))
    vals += [val_far, send(val_far, CORE)]

    first_back = first_gradient(
        back, where, kept, inner, d_values, d_low, grad, saved, factor_b, gain, down, vals
    )
    relayed = lax.ppermute(first_back, "section", before)
    share_f, first_back = lax.optimization_barrier((share_f, first_back))
    first_out = output(ahead, where, share_f, normed_f, low_f, up, rows, outs, vals)
    passed = lax.ppermute(first_out, "section", onward)

    grad_n, d_values, d_low, mine, other = second_values(
        ahead, where, relayed, first_out, target, low_n, normed_n, up, outs
    )
    terms = spread(first_sums, mine, send(other, CORE))
    bwd_out = second_input(
        where, grad_n, rows, saved, factor_n, gain, down, d_values, d_low, vals
    )
    fwd_out = forward(where, fresh, passed, gain, down, up, vals, outs)
    down_table, up_table = tables(ahead, back, where, relayed, terms)
    return (
        fwd_out[None], bwd_out[None], jnp.swapaxes(down_table, 1, 2)[None], up_table[None]
    )


def solution(mesh):
    return jax.shard_map(
        body,
        mesh=mesh,
        in_specs=(
            P("section", "dp", None),
            P("section", "dp", None),
            P("section", None, "dp", None),
            P("dp", None),
            P("dp", None),
            P("section"),
            P("section"),
            P("section", "dp", None),
            P("section", None, "dp"),
            P("section", None),
            P("section", None, None, None),
            P("section", None, None, None),
        ),
        out_specs=(
            P("section", "dp", None),
            P("section", "dp", None),
            P("section", None, "dp", None),
            P("section", None, None, "dp"),
        ),
        check_vma=False,
    )
```

```python
import jax
import jax.numpy as jnp
from jax import lax
from jax.experimental import pallas as pl
from jax.experimental.pallas import tpu as pltpu
from jax.sharding import PartitionSpec as P

SCALE = 0.5
EPS = 1e-05
BF = jnp.bfloat16
F32 = jnp.float32
ROWS = 128
WIDTH = 4096
VALUES = 512
PART = 512
RANK = 64
ADAPTERS = 4
PACK = PART + 128
LOWS = 256
WIDE = WIDTH + 128
VMEM = 20 * 1024 * 1024
ONCE = pl.Buffered(1)


def dot(left, right, dims=((1,), (0,))):
    return lax.dot_general(left, right, (dims, ((), ())), preferred_element_type=F32)


def dot_t(left, right):
    return dot(left, right, ((1,), (1,)))


def t_dot(left, right):
    return dot(left, right, ((0,), (0,)))


def call(kernel, scalars, ins, outs, flops, scratch=()):
    specs, arrays = [], []
    for item in ins:
        array, block, index = item if isinstance(item, tuple) else (item, None, None)
        arrays.append(array)
        if block is None:
            zeros = (0,) * array.ndim
            specs.append(pl.BlockSpec(array.shape, lambda i, *s, z=zeros: z, pipeline_mode=ONCE))
        else:
            specs.append(pl.BlockSpec(block, index, pipeline_mode=ONCE))
    out_specs = [
        pl.BlockSpec(o.shape, lambda i, *s, z=(0,) * len(o.shape): z, pipeline_mode=ONCE)
        for o in outs
    ]
    size = sum(a.size * a.dtype.itemsize for a in arrays)
    return pl.pallas_call(
        kernel,
        out_shape=outs,
        grid_spec=pltpu.PrefetchScalarGridSpec(
            num_scalar_prefetch=len(scalars),
            grid=(1,),
            in_specs=specs,
            out_specs=out_specs,
            scratch_shapes=list(scratch),
        ),
        compiler_params=pltpu.CompilerParams(vmem_limit_bytes=VMEM),
        cost_estimate=pl.CostEstimate(
            flops=flops // 1000, bytes_accessed=size // 1000, transcendentals=0
        ),
    )(*scalars, *arrays)


def shape(dims, dtype):
    return jax.ShapeDtypeStruct(dims, dtype)


def factor_of(rows):
    return lax.rsqrt(jnp.sum(rows * rows, axis=-1, keepdims=True) * (1.0 / WIDTH) + EPS)


def columns(index):
    return pl.ds(pl.multiple_of(index * PART, PART), PART)


def only(lows, ident):
    lane = lax.broadcasted_iota(jnp.int32, lows.shape, 1)
    return jnp.where(lane // RANK == ident, lows, jnp.zeros_like(lows))


def compact(lows):
    total = lows[:, :RANK].astype(F32)
    for k in range(1, ADAPTERS):
        total += lows[:, k * RANK : (k + 1) * RANK].astype(F32)
    return total.astype(BF)


def saved_of(saved, which):
    return (saved, (1, 1, ROWS, WIDTH), lambda i, *s: (0, which, 0, 0))


def prepare_kernel(ahead, back, where, rows_f, rows_b, rows_s, gain, down, *refs):
    last = where[9] == 1
    for kind in range(3):
        normed, factor, low = refs[3 * kind : 3 * kind + 3]
        for top in range(0, ROWS, 32):
            part = slice(top, top + 32)
            if kind == 0:
                whole = rows_f[part, :]
            elif kind == 1:
                whole = rows_b[0, 0, part, :]
            else:
                whole = jnp.where(last, rows_f[part, :], rows_s[0, 0, part, :])
            whole = whole.astype(F32)
            scale = factor_of(whole)
            normed[part, :] = (whole * scale * gain[...]).astype(BF)
            factor[part, :] = jnp.broadcast_to(scale, (32, 128))
        lows = dot_t(normed[...], down[...])
        if kind == 0:
            lows = only(lows, ahead[0])
        elif kind == 1:
            lows = only(lows, back[0])
        low[...] = lows.astype(BF)


def prepare(ahead, back, where, rows, saved, gain, down):
    kinds = [shape((ROWS, WIDTH), BF), shape((ROWS, 128), F32), shape((ROWS, LOWS), BF)]
    return call(
        prepare_kernel,
        (ahead, back, where),
        [rows, saved_of(saved, 0), saved_of(saved, 1), gain, down],
        kinds * 3,
        6 * ROWS * WIDTH * LOWS,
    )


def gained_block(values, lowered, span, gain, down, block):
    return (dot_t(values, block[...]) + dot(lowered, down[:, span])) * gain[:, span]


def input_gradient(where, grad, rows, scale, inner, gained, out):
    inner = inner * (1.0 / WIDTH)
    for i in range(8):
        span = columns(where[i])
        pre = rows(span).astype(F32) * scale
        out[:, span] = (
            grad[:, span].astype(F32) + scale * (gained(i) - pre * inner)
        ).astype(BF)


def near_kernel(back, where, grad, normed, rows, factor, gain, down, up, *refs):
    outs, vals, (d_values, d_low, kept, inner, share) = refs[:8], refs[8:14], refs[14:]
    total = jnp.zeros((ROWS, VALUES), F32)
    for i in range(8):
        total += dot_t(grad[:, columns(where[i])], outs[i][...])
    values = total.astype(BF)
    lowered = only(SCALE * dot_t(values, up[...]), back[0]).astype(BF)
    d_values[...] = values
    d_low[...] = lowered
    scale = factor[:, :1]
    mean = jnp.zeros((ROWS, 1), F32)
    for i in range(6):
        span = columns(where[i])
        gained = gained_block(values, lowered, span, gain, down, vals[i])
        kept[i] = gained
        mean += jnp.sum(
            gained * (rows[0, 0, :, span].astype(F32) * scale), axis=-1, keepdims=True
        )
    inner[...] = jnp.broadcast_to(mean, (ROWS, 128))
    total = jnp.zeros((ROWS, VALUES), F32)
    for i in range(6):
        total += dot(normed[:, columns(where[i])], vals[i][...])
    share[...] = total


GRADS = [shape((ROWS, VALUES), BF), shape((ROWS, LOWS), BF)]
KEPT = [pltpu.VMEM((8, ROWS, PART), F32)]


def near_share(back, where, grad, normed, saved, factor, gain, down, up, outs, vals):
    return call(
        near_kernel,
        (back, where),
        [grad, normed, saved_of(saved, 0), factor, gain, down, up, *outs, *vals],
        [*GRADS, shape((6, ROWS, PART), F32), shape((ROWS, 128), F32), shape((ROWS, VALUES), F32)],
        6 * ROWS * WIDTH * VALUES,
    )


def first_kernel(
    back, where, kept, inner, values, lowered, grad, rows, factor, gain, down, far, far_other, out
):
    scale = factor[:, :1]
    mean = inner[:, :1]
    last = []
    for i, block in ((6, far), (7, far_other)):
        span = columns(where[i])
        gained = gained_block(values[...], lowered[...], span, gain, down, block)
        mean += jnp.sum(
            gained * (rows[0, 0, :, span].astype(F32) * scale), axis=-1, keepdims=True
        )
        last.append(gained)
    input_gradient(
        where, grad, lambda span: rows[0, 0, :, span], scale, mean,
        lambda i: kept[i] if i < 6 else last[i - 6], out,
    )
    out[:, WIDTH:] = jnp.full((ROWS, 128), back[0], jnp.int32).astype(F32).astype(BF)


def first_gradient(back, where, kept, inner, d_values, d_low, grad, saved, factor, gain, down, vals):
    return call(
        first_kernel,
        (back, where),
        [
            kept, inner, d_values, d_low, grad, saved_of(saved, 0), factor, gain, down, *vals[6:]
        ],
        [shape((ROWS, WIDE), BF)],
        ROWS * WIDTH * VALUES,
    )[0]


def output_kernel(ahead, where, share, normed, low, up, rows, far, far_other, *refs):
    blocks, out = refs[:8], refs[8]
    total = share[...] + SCALE * dot(low[...], up[...])
    total += dot(normed[:, columns(where[6])], far[...])
    total += dot(normed[:, columns(where[7])], far_other[...])
    values = total.astype(BF)
    for i in range(8):
        span = columns(where[i])
        out[:, span] = (rows[:, span].astype(F32) + dot(values, blocks[i][...])).astype(BF)
    out[:, WIDTH:] = jnp.full((ROWS, 128), ahead[0], jnp.int32).astype(F32).astype(BF)


def output(ahead, where, share, normed, low, up, rows, outs, vals):
    return call(
        output_kernel,
        (ahead, where),
        [share, normed, low, up, rows, *vals[6:], *outs],
        [shape((ROWS, WIDE), BF)],
        2 * ROWS * WIDTH * VALUES,
    )[0]


def pack_gradients(where, low, normed, d_values, d_low, mine, other):
    up_term = SCALE * t_dot(low, d_values)
    chip, core = where[0] // 2, where[0] % 2
    for ahead in range(4):
        target = lax.rem(chip + ahead, 4)
        pair = up_term[:, 0:128]
        for k in range(1, 4):
            pair = jnp.where(target == k, up_term[:, 128 * k : 128 * (k + 1)], pair)
        pair = pair.astype(BF)
        for ref, c in ((mine, core), (other, 1 - core)):
            ref[ahead, :, :PART] = t_dot(d_low, normed[:, columns(2 * target + c)]).astype(BF)
            ref[ahead, :, PART:] = pair


PACKED = [shape((4, RANK, PACK), BF)] * 2


def pack_kernel(where, low, normed, d_values, d_low, mine, other):
    pack_gradients(
        where, compact(low[...]), normed, d_values[...], compact(d_low[...]), mine, other
    )


def pack(where, low, normed, d_values, d_low):
    return call(
        pack_kernel, (where,), [low, normed, d_values, d_low], PACKED, 2 * ROWS * WIDTH * RANK
    )


def second_kernel(ahead, where, relayed, out, target, low, normed, up, *refs):
    blocks, (grad, d_values, d_low, mine, other) = refs[:8], refs[8:]
    last = where[9] == 1
    total = jnp.zeros((ROWS, VALUES), F32)
    for i in range(8):
        span = columns(where[i])
        loss = (out[:, span].astype(F32) - target[:, span].astype(F32)).astype(BF)
        chosen = jnp.where(last, loss, relayed[:, span])
        grad[:, span] = chosen
        total += dot_t(chosen, blocks[i][...])
    values = total.astype(BF)
    came = relayed[:, WIDTH : WIDTH + 1].astype(F32).astype(jnp.int32)
    ident = jnp.where(last, ahead[0], came)
    lowered = only(SCALE * dot_t(values, up[...]), ident).astype(BF)
    d_values[...] = values
    d_low[...] = lowered
    pack_gradients(
        where, compact(only(low[...], ident)), normed, values, compact(lowered), mine, other
    )


def second_values(ahead, where, relayed, out, target, low, normed, up, blocks):
    return call(
        second_kernel,
        (ahead, where),
        [relayed, out, target, low, normed, up, *blocks],
        [shape((ROWS, WIDTH), BF), *GRADS, *PACKED],
        2 * ROWS * WIDTH * (VALUES + RANK),
    )


def second_input_kernel(where, grad, rows_f, rows_s, factor, gain, down, d_values, d_low, *refs):
    blocks, (out, kept) = refs[:8], refs[8:]
    last = where[9] == 1
    scale = factor[:, :1]
    rows = lambda span: jnp.where(last, rows_f[:, span], rows_s[0, 0, :, span])
    mean = jnp.zeros((ROWS, 1), F32)
    for i in range(8):
        span = columns(where[i])
        gained = gained_block(d_values[...], d_low[...], span, gain, down, blocks[i])
        kept[i] = gained
        mean += jnp.sum(gained * (rows(span).astype(F32) * scale), axis=-1, keepdims=True)
    input_gradient(where, grad, rows, scale, mean, lambda i: kept[i], out)


def second_input(where, grad, rows, saved, factor, gain, down, d_values, d_low, blocks):
    return call(
        second_input_kernel,
        (where,),
        [grad, rows, saved_of(saved, 1), factor, gain, down, d_values, d_low, *blocks],
        [shape((ROWS, WIDTH), BF)],
        2 * ROWS * WIDTH * (VALUES + RANK),
        KEPT,
    )[0]


def forward_kernel(where, fresh, passed, gain, down, up, *refs):
    vals, outs, (out, rows, normed) = refs[:8], refs[8:16], refs[16:]
    first = where[8] == 1
    for top in range(0, ROWS, 32):
        part = slice(top, top + 32)
        chosen = jnp.where(first, fresh[part, :], passed[part, :WIDTH])
        whole = chosen.astype(F32)
        rows[part, :] = chosen
        normed[part, :] = (whole * factor_of(whole) * gain[...]).astype(BF)
    ident = passed[:, WIDTH : WIDTH + 1].astype(F32).astype(jnp.int32)
    low = only(dot_t(normed[...], down[...]), ident).astype(BF)
    total = SCALE * dot(low, up[...])
    for i in range(8):
        total += dot(normed[:, columns(where[i])], vals[i][...])
    values = total.astype(BF)
    for i in range(8):
        span = columns(where[i])
        out[:, span] = (rows[:, span].astype(F32) + dot(values, outs[i][...])).astype(BF)


def forward(where, fresh, passed, gain, down, up, vals, outs):
    return call(
        forward_kernel,
        (where,),
        [fresh, passed, gain, down, up, *vals, *outs],
        [shape((ROWS, WIDTH), BF)],
        4 * ROWS * WIDTH * VALUES,
        [pltpu.VMEM((ROWS, WIDTH), BF), pltpu.VMEM((ROWS, WIDTH), BF)],
    )[0]


def pair_sum_kernel(mine, other, total):
    total[...] = (mine[...].astype(F32) + other[...].astype(F32)).astype(BF)


def pair_sum(mine, other):
    return call(pair_sum_kernel, (), [mine, other], [shape((4, RANK, PACK), BF)], 0)[0]


def stack_kernel(first, mine, other, own, one, two, three):
    for ahead, ref in enumerate((own, one, two, three)):
        ref[0] = first[ahead]
        ref[1] = (mine[ahead].astype(F32) + other[ahead].astype(F32)).astype(BF)


def spread(first, mine, received):
    block = shape((2, RANK, PACK), BF)
    own, one, two, three = call(stack_kernel, (), [first, mine, received], [block] * 4, 0)
    return (
        own,
        lax.ppermute(two, "dp", chips(2)),
        lax.ppermute(one, "dp", chips(1)),
        lax.ppermute(three, "dp", chips(3)),
    )


def tables_kernel(ahead, back, where, relayed, *refs):
    terms, (down, up) = refs[:4], refs[4:]
    core = where[0] % 2
    came = relayed[:RANK, :1].astype(F32).astype(jnp.int32)
    ident = jnp.where(where[9] == 1, ahead[0], came)
    sums = []
    for tick in range(2):
        total = terms[0][tick].astype(F32)
        for k in range(1, 4):
            total += terms[k][tick].astype(F32)
        sums.append(total)
    for label in range(ADAPTERS):
        one = jnp.where(back[0] == label, 1.0, 0.0)
        two = jnp.where(ident == label, 1.0, 0.0)
        total = one * sums[0] + two * sums[1]
        down[label] = total[:, :PART]
        up[label] = jnp.where(core == 0, total[:, PART : PART + 64], total[:, PART + 64 :])


def tables(ahead, back, where, relayed, terms):
    tail = (relayed, (ROWS, 128), lambda i, *s: (0, WIDTH // 128))
    return call(
        tables_kernel,
        (ahead, back, where),
        [tail, *terms],
        [shape((ADAPTERS, RANK, PART), F32), shape((ADAPTERS, RANK, 64), F32)],
        0,
    )


CORE = [(i, i ^ 1) for i in range(8)]


def chips(by):
    return [(i, ((i // 2 + by) % 4) * 2 + i % 2) for i in range(8)]


def split_ring(by):
    return [(i, ((i // 2 + (by if i % 2 == 0 else -by)) % 4) * 2 + i % 2) for i in range(8)]


def send(block, pairs):
    return lax.ppermute(block, "dp", pairs)


def block_index():
    place = lax.axis_index("dp")
    chip, core = place // 2, place % 2
    other = 1 - core
    step = jnp.where(core == 0, 1, -1)
    block = lambda k, c: 2 * (k % 4) + c
    return [
        block(chip, core), block(chip, other),
        block(chip - step + 4, core), block(chip + step + 4, other),
        block(chip + 2, core), block(chip + 2, other),
        block(chip + step + 4, core), block(chip - step + 4, other),
    ]


def body(
    forward_state, backward_state, saved, fresh, target, forward_adapter, backward_adapter,
    value_projection, output_matrix, norm_gain_frozen, adapter_down, adapter_up,
):
    count = lax.axis_size("section")
    onward = [(i, (i + 1) % count) for i in range(count)]
    before = [(i, i - 1) for i in range(1, count)]
    position = lax.axis_index("section")
    where = jnp.stack(
        [v.astype(jnp.int32) for v in (*block_index(), position == 0, position == count - 1)]
    )
    gain = norm_gain_frozen
    down = jnp.swapaxes(adapter_down[0], 1, 2).reshape(LOWS, WIDTH)
    up = adapter_up[0].reshape(LOWS, VALUES)
    rows, grad = forward_state[0], backward_state[0]
    ahead, back = forward_adapter, backward_adapter

    out_own, val_own = output_matrix[0], value_projection[0]
    out_one, val_one = send(out_own, split_ring(1)), send(val_own, split_ring(1))
    out_sibling, val_sibling = send(out_own, CORE), send(val_own, CORE)

    normed_f, _, low_f, normed_b, factor_b, low_b, normed_n, factor_n, low_n = prepare(
        ahead, back, where, rows, saved, gain, down
    )
    out_one, normed_f, out_sibling, val_sibling = lax.optimization_barrier(
        (out_one, normed_f, out_sibling, val_sibling)
    )
    out_two, val_two = send(out_one, split_ring(1)), send(val_one, split_ring(1))
    out_far, val_far = send(out_two, split_ring(1)), send(val_two, split_ring(1))
    outs = [out_own, out_sibling, out_one, send(out_one, CORE), out_two, send(out_two, CORE)]
    vals = [val_own, val_sibling, val_one, send(val_one, CORE), val_two, send(val_two, CORE)]
    outs += [out_far, send(out_far, CORE)]
    d_values, d_low, kept, inner, share_f = near_share(
        back, where, grad, normed_f, saved, factor_b, gain, down, up, outs, vals
    )
    mine, other = pack(where, low_b, normed_b, d_values, d_low)
    val_far, mine = lax.optimization_barrier((val_far, mine))
    vals += [val_far, send(val_far, CORE)]

    first_back = first_gradient(
        back, where, kept, inner, d_values, d_low, grad, saved, factor_b, gain, down, vals
    )
    relayed = lax.ppermute(first_back, "section", before)
    share_f, first_back = lax.optimization_barrier((share_f, first_back))
    first_out = output(ahead, where, share_f, normed_f, low_f, up, rows, outs, vals)
    passed = lax.ppermute(first_out, "section", onward)
    first_out, other = lax.optimization_barrier((first_out, other))
    first_sums = pair_sum(mine, send(other, CORE))
    relayed, first_sums = lax.optimization_barrier((relayed, first_sums))

    grad_n, d_values, d_low, mine, other = second_values(
        ahead, where, relayed, first_out, target, low_n, normed_n, up, outs
    )
    terms = spread(first_sums, mine, send(other, CORE))
    bwd_out = second_input(
        where, grad_n, rows, saved, factor_n, gain, down, d_values, d_low, vals
    )
    fwd_out = forward(where, fresh, passed, gain, down, up, vals, outs)
    down_table, up_table = tables(ahead, back, where, relayed, terms)
    return (
        fwd_out[None], bwd_out[None], jnp.swapaxes(down_table, 1, 2)[None], up_table[None]
    )


def solution(mesh):
    return jax.shard_map(
        body,
        mesh=mesh,
        in_specs=(
            P("section", "dp", None),
            P("section", "dp", None),
            P("section", None, "dp", None),
            P("dp", None),
            P("dp", None),
            P("section"),
            P("section"),
            P("section", "dp", None),
            P("section", None, "dp"),
            P("section", None),
            P("section", None, None, None),
            P("section", None, None, None),
        ),
        out_specs=(
            P("section", "dp", None),
            P("section", "dp", None),
            P("section", None, "dp", None),
            P("section", None, None, "dp"),
        ),
        check_vma=False,
    )
```

```python
import jax
import jax.numpy as jnp
from jax import lax
from jax.experimental import pallas as pl
from jax.experimental.pallas import tpu as pltpu
from jax.sharding import PartitionSpec as P

SCALE = 0.5
EPS = 1e-05
BF = jnp.bfloat16
F32 = jnp.float32
ROWS = 128
WIDTH = 4096
VALUES = 512
PART = 512
RANK = 64
ADAPTERS = 4
PACK = PART + 128
LOWS = 256
WIDE = WIDTH + 128
VMEM = 20 * 1024 * 1024
ONCE = pl.Buffered(1)


def dot(left, right, dims=((1,), (0,))):
    return lax.dot_general(left, right, (dims, ((), ())), preferred_element_type=F32)


def dot_t(left, right):
    return dot(left, right, ((1,), (1,)))


def t_dot(left, right):
    return dot(left, right, ((0,), (0,)))


def call(kernel, scalars, ins, outs, flops, scratch=()):
    specs, arrays = [], []
    for item in ins:
        array, block, index = item if isinstance(item, tuple) else (item, None, None)
        arrays.append(array)
        if block is None:
            zeros = (0,) * array.ndim
            specs.append(pl.BlockSpec(array.shape, lambda i, *s, z=zeros: z, pipeline_mode=ONCE))
        else:
            specs.append(pl.BlockSpec(block, index, pipeline_mode=ONCE))
    out_specs = [
        pl.BlockSpec(o.shape, lambda i, *s, z=(0,) * len(o.shape): z, pipeline_mode=ONCE)
        for o in outs
    ]
    size = sum(a.size * a.dtype.itemsize for a in arrays)
    return pl.pallas_call(
        kernel,
        out_shape=outs,
        grid_spec=pltpu.PrefetchScalarGridSpec(
            num_scalar_prefetch=len(scalars),
            grid=(1,),
            in_specs=specs,
            out_specs=out_specs,
            scratch_shapes=list(scratch),
        ),
        compiler_params=pltpu.CompilerParams(vmem_limit_bytes=VMEM),
        cost_estimate=pl.CostEstimate(
            flops=flops // 1000, bytes_accessed=size // 1000, transcendentals=0
        ),
    )(*scalars, *arrays)


def shape(dims, dtype):
    return jax.ShapeDtypeStruct(dims, dtype)


def factor_of(rows):
    return lax.rsqrt(jnp.sum(rows * rows, axis=-1, keepdims=True) * (1.0 / WIDTH) + EPS)


def columns(index):
    return pl.ds(pl.multiple_of(index * PART, PART), PART)


def only(lows, ident):
    lane = lax.broadcasted_iota(jnp.int32, lows.shape, 1)
    return jnp.where(lane // RANK == ident, lows, jnp.zeros_like(lows))


def compact(lows):
    total = lows[:, :RANK].astype(F32)
    for k in range(1, ADAPTERS):
        total += lows[:, k * RANK : (k + 1) * RANK].astype(F32)
    return total.astype(BF)


def saved_of(saved, which):
    return (saved, (1, 1, ROWS, WIDTH), lambda i, *s: (0, which, 0, 0))


def prepare_kernel(ahead, back, where, rows_f, rows_b, rows_s, gain, down, *refs):
    last = where[9] == 1
    for kind in range(3):
        normed, factor, low = refs[3 * kind : 3 * kind + 3]
        for top in range(0, ROWS, 32):
            part = slice(top, top + 32)
            if kind == 0:
                whole = rows_f[part, :]
            elif kind == 1:
                whole = rows_b[0, 0, part, :]
            else:
                whole = jnp.where(last, rows_f[part, :], rows_s[0, 0, part, :])
            whole = whole.astype(F32)
            scale = factor_of(whole)
            normed[part, :] = (whole * scale * gain[...]).astype(BF)
            factor[part, :] = jnp.broadcast_to(scale, (32, 128))
        lows = dot_t(normed[...], down[...])
        if kind == 0:
            lows = only(lows, ahead[0])
        elif kind == 1:
            lows = only(lows, back[0])
        low[...] = lows.astype(BF)


def prepare(ahead, back, where, rows, saved, gain, down):
    kinds = [shape((ROWS, WIDTH), BF), shape((ROWS, 128), F32), shape((ROWS, LOWS), BF)]
    return call(
        prepare_kernel,
        (ahead, back, where),
        [rows, saved_of(saved, 0), saved_of(saved, 1), gain, down],
        kinds * 3,
        6 * ROWS * WIDTH * LOWS,
    )


def input_gradient(where, values, lowered, sums, low, grad, rows, scale, gain, down, blocks, out):
    inner = jnp.sum(values.astype(F32) * sums, axis=-1, keepdims=True)
    inner += jnp.sum(lowered.astype(F32) * low.astype(F32), axis=-1, keepdims=True)
    weight = scale * scale * inner * (1.0 / WIDTH)
    for i in range(8):
        span = columns(where[i])
        gained = (dot_t(values, blocks[i][...]) + dot(lowered, down[:, span])) * gain[:, span]
        out[:, span] = (
            grad[:, span].astype(F32) + scale * gained - weight * rows(span).astype(F32)
        ).astype(BF)


def near_kernel(where, grad, normed_f, normed_b, *refs):
    outs, vals, results = refs[:6], refs[6:12], refs[12:]
    total = jnp.zeros((ROWS, VALUES), F32)
    for i in range(6):
        total += dot_t(grad[:, columns(where[i])], outs[i][...])
    results[0][...] = total
    for normed, result in ((normed_f, results[1]), (normed_b, results[2])):
        total = jnp.zeros((ROWS, VALUES), F32)
        for i in range(6):
            total += dot(normed[:, columns(where[i])], vals[i][...])
        result[...] = total


def near_share(where, grad, normed_f, normed_b, outs, vals):
    return call(
        near_kernel,
        (where,),
        [grad, normed_f, normed_b, *outs, *vals],
        [shape((ROWS, VALUES), F32)] * 3,
        6 * ROWS * WIDTH * VALUES,
    )


GRADS = [shape((ROWS, VALUES), BF), shape((ROWS, LOWS), BF)]


def first_kernel(
    back, where, share, sums, grad, normed, low, rows, factor, gain, down, up, far, far_other, *refs
):
    blocks, (out, d_values, d_low) = refs[:8], refs[8:]
    total = share[...]
    total += dot_t(grad[:, columns(where[6])], far[...])
    total += dot_t(grad[:, columns(where[7])], far_other[...])
    values = total.astype(BF)
    lowered = only(SCALE * dot_t(values, up[...]), back[0]).astype(BF)
    d_values[...] = values
    d_low[...] = lowered
    total = sums[...]
    for i in (6, 7):
        total += dot(normed[:, columns(where[i])], blocks[i][...])
    input_gradient(
        where, values, lowered, total, low[...], grad, lambda span: rows[0, 0, :, span],
        factor[:, :1], gain, down, blocks, out,
    )
    out[:, WIDTH:] = jnp.full((ROWS, 128), back[0], jnp.int32).astype(F32).astype(BF)


def first_gradient(
    back, where, share, sums, grad, normed, low, saved, factor, gain, down, up, outs, vals
):
    return call(
        first_kernel,
        (back, where),
        [
            share, sums, grad, normed, low, saved_of(saved, 0), factor, gain, down, up,
            *outs[6:], *vals,
        ],
        [shape((ROWS, WIDE), BF), *GRADS],
        2 * ROWS * WIDTH * VALUES,
    )


def project_kernel(where, normed, *refs):
    blocks, out = refs[:8], refs[8]
    total = jnp.zeros((ROWS, VALUES), F32)
    for i in range(8):
        total += dot(normed[:, columns(where[i])], blocks[i][...])
    out[...] = total


def project(where, normed, vals):
    return call(
        project_kernel, (where,), [normed, *vals], [shape((ROWS, VALUES), F32)],
        2 * ROWS * WIDTH * VALUES,
    )[0]


def output_kernel(ahead, where, share, normed, low, up, rows, far, far_other, *refs):
    blocks, out = refs[:8], refs[8]
    total = share[...] + SCALE * dot(low[...], up[...])
    total += dot(normed[:, columns(where[6])], far[...])
    total += dot(normed[:, columns(where[7])], far_other[...])
    values = total.astype(BF)
    for i in range(8):
        span = columns(where[i])
        out[:, span] = (rows[:, span].astype(F32) + dot(values, blocks[i][...])).astype(BF)
    out[:, WIDTH:] = jnp.full((ROWS, 128), ahead[0], jnp.int32).astype(F32).astype(BF)


def output(ahead, where, share, normed, low, up, rows, outs, vals):
    return call(
        output_kernel,
        (ahead, where),
        [share, normed, low, up, rows, *vals[6:], *outs],
        [shape((ROWS, WIDE), BF)],
        2 * ROWS * WIDTH * VALUES,
    )[0]


def pack_gradients(where, low, normed, d_values, d_low, mine, other):
    up_term = SCALE * t_dot(low, d_values)
    chip, core = where[0] // 2, where[0] % 2
    for ahead in range(4):
        target = lax.rem(chip + ahead, 4)
        pair = up_term[:, 0:128]
        for k in range(1, 4):
            pair = jnp.where(target == k, up_term[:, 128 * k : 128 * (k + 1)], pair)
        pair = pair.astype(BF)
        for ref, c in ((mine, core), (other, 1 - core)):
            ref[ahead, :, :PART] = t_dot(d_low, normed[:, columns(2 * target + c)]).astype(BF)
            ref[ahead, :, PART:] = pair


PACKED = [shape((4, RANK, PACK), BF)] * 2


def pack_kernel(where, low, normed, d_values, d_low, mine, other):
    pack_gradients(
        where, compact(low[...]), normed, d_values[...], compact(d_low[...]), mine, other
    )


def pack(where, low, normed, d_values, d_low):
    return call(
        pack_kernel, (where,), [low, normed, d_values, d_low], PACKED, 2 * ROWS * WIDTH * RANK
    )


def second_kernel(ahead, where, relayed, out, target, low, normed, up, *refs):
    blocks, (grad, d_values, d_low, mine, other) = refs[:8], refs[8:]
    last = where[9] == 1
    total = jnp.zeros((ROWS, VALUES), F32)
    for i in range(8):
        span = columns(where[i])
        loss = (out[:, span].astype(F32) - target[:, span].astype(F32)).astype(BF)
        chosen = jnp.where(last, loss, relayed[:, span])
        grad[:, span] = chosen
        total += dot_t(chosen, blocks[i][...])
    values = total.astype(BF)
    came = relayed[:, WIDTH : WIDTH + 1].astype(F32).astype(jnp.int32)
    ident = jnp.where(last, ahead[0], came)
    lowered = only(SCALE * dot_t(values, up[...]), ident).astype(BF)
    d_values[...] = values
    d_low[...] = lowered
    pack_gradients(
        where, compact(only(low[...], ident)), normed, values, compact(lowered), mine, other
    )


def second_values(ahead, where, relayed, out, target, low, normed, up, blocks):
    return call(
        second_kernel,
        (ahead, where),
        [relayed, out, target, low, normed, up, *blocks],
        [shape((ROWS, WIDTH), BF), *GRADS, *PACKED],
        2 * ROWS * WIDTH * (VALUES + RANK),
    )


def second_input_kernel(
    where, sums, low, grad, rows_f, rows_s, factor, gain, down, d_values, d_low, *refs
):
    blocks, out = refs[:8], refs[8]
    last = where[9] == 1
    input_gradient(
        where, d_values[...], d_low[...], sums[...], low[...], grad,
        lambda span: jnp.where(last, rows_f[:, span], rows_s[0, 0, :, span]),
        factor[:, :1], gain, down, blocks, out,
    )


def second_input(where, sums, low, grad, rows, saved, factor, gain, down, d_values, d_low, blocks):
    return call(
        second_input_kernel,
        (where,),
        [
            sums, low, grad, rows, saved_of(saved, 1), factor, gain, down, d_values, d_low, *blocks
        ],
        [shape((ROWS, WIDTH), BF)],
        2 * ROWS * WIDTH * (VALUES + RANK),
    )[0]


def forward_kernel(wrapped, where, fresh, passed, gain, down, up, *refs):
    vals, outs, (out, rows, normed) = refs[:8], refs[8:16], refs[16:]
    first = where[8] == 1
    for top in range(0, ROWS, 32):
        part = slice(top, top + 32)
        chosen = jnp.where(first, fresh[part, :], passed[part, :WIDTH])
        whole = chosen.astype(F32)
        rows[part, :] = chosen
        normed[part, :] = (whole * factor_of(whole) * gain[...]).astype(BF)
    came = passed[:, WIDTH : WIDTH + 1].astype(F32).astype(jnp.int32)
    ident = jnp.where(first, wrapped[0], came)
    low = only(dot_t(normed[...], down[...]), ident).astype(BF)
    total = SCALE * dot(low, up[...])
    for i in range(8):
        total += dot(normed[:, columns(where[i])], vals[i][...])
    values = total.astype(BF)
    for i in range(8):
        span = columns(where[i])
        out[:, span] = (rows[:, span].astype(F32) + dot(values, outs[i][...])).astype(BF)


def forward(wrapped, where, fresh, passed, gain, down, up, vals, outs):
    return call(
        forward_kernel,
        (wrapped, where),
        [fresh, passed, gain, down, up, *vals, *outs],
        [shape((ROWS, WIDTH), BF)],
        4 * ROWS * WIDTH * VALUES,
        [pltpu.VMEM((ROWS, WIDTH), BF), pltpu.VMEM((ROWS, WIDTH), BF)],
    )[0]


def pair_sum_kernel(mine, other, own, one, two, three):
    for ahead, ref in enumerate((own, one, two, three)):
        ref[...] = (mine[ahead].astype(F32) + other[ahead].astype(F32)).astype(BF)


def spread(mine, received):
    block = shape((RANK, PACK), BF)
    own, one, two, three = call(pair_sum_kernel, (), [mine, received], [block] * 4, 0)
    return (
        own,
        lax.ppermute(two, "dp", chips(2)),
        lax.ppermute(one, "dp", chips(1)),
        lax.ppermute(three, "dp", chips(3)),
    )


def tables_kernel(ahead, back, where, relayed, *refs):
    terms, (down, up) = refs[:8], refs[8:]
    core = where[0] % 2
    came = relayed[:RANK, :1].astype(F32).astype(jnp.int32)
    ident = jnp.where(where[9] == 1, ahead[0], came)
    sums = []
    for tick in range(2):
        total = terms[4 * tick][...].astype(F32)
        for k in range(1, 4):
            total += terms[4 * tick + k][...].astype(F32)
        sums.append(total)
    for label in range(ADAPTERS):
        one = jnp.where(back[0] == label, 1.0, 0.0)
        two = jnp.where(ident == label, 1.0, 0.0)
        total = one * sums[0] + two * sums[1]
        down[label] = total[:, :PART]
        up[label] = jnp.where(core == 0, total[:, PART : PART + 64], total[:, PART + 64 :])


def tables(ahead, back, where, relayed, terms):
    tail = (relayed, (ROWS, 128), lambda i, *s: (0, WIDTH // 128))
    return call(
        tables_kernel,
        (ahead, back, where),
        [tail, *terms],
        [shape((ADAPTERS, RANK, PART), F32), shape((ADAPTERS, RANK, 64), F32)],
        0,
    )


CORE = [(i, i ^ 1) for i in range(8)]


def chips(by):
    return [(i, ((i // 2 + by) % 4) * 2 + i % 2) for i in range(8)]


def split_ring(by):
    return [(i, ((i // 2 + (by if i % 2 == 0 else -by)) % 4) * 2 + i % 2) for i in range(8)]


def send(block, pairs):
    return lax.ppermute(block, "dp", pairs)


def block_index():
    place = lax.axis_index("dp")
    chip, core = place // 2, place % 2
    other = 1 - core
    step = jnp.where(core == 0, 1, -1)
    block = lambda k, c: 2 * (k % 4) + c
    return [
        block(chip, core), block(chip, other),
        block(chip - step + 4, core), block(chip + step + 4, other),
        block(chip + 2, core), block(chip + 2, other),
        block(chip + step + 4, core), block(chip - step + 4, other),
    ]


def body(
    forward_state, backward_state, saved, fresh, target, forward_adapter, backward_adapter,
    value_projection, output_matrix, norm_gain_frozen, adapter_down, adapter_up,
):
    count = lax.axis_size("section")
    onward = [(i, i + 1) for i in range(count - 1)]
    before = [(i, i - 1) for i in range(1, count)]
    position = lax.axis_index("section")
    where = jnp.stack(
        [v.astype(jnp.int32) for v in (*block_index(), position == 0, position == count - 1)]
    )
    gain = norm_gain_frozen
    down = jnp.swapaxes(adapter_down[0], 1, 2).reshape(LOWS, WIDTH)
    up = adapter_up[0].reshape(LOWS, VALUES)
    rows, grad = forward_state[0], backward_state[0]
    ahead, back = forward_adapter, backward_adapter

    out_own, val_own = output_matrix[0], value_projection[0]
    wrapped = lax.ppermute(ahead, "section", [(count - 1, 0)])
    out_one, val_one = send(out_own, split_ring(1)), send(val_own, split_ring(1))
    out_sibling, val_sibling = send(out_own, CORE), send(val_own, CORE)

    normed_f, _, low_f, normed_b, factor_b, low_b, normed_n, factor_n, low_n = prepare(
        ahead, back, where, rows, saved, gain, down
    )
    out_one, normed_f, out_sibling, val_sibling, wrapped = lax.optimization_barrier(
        (out_one, normed_f, out_sibling, val_sibling, wrapped)
    )
    out_two, val_two = send(out_one, split_ring(1)), send(val_one, split_ring(1))
    out_far, val_far = send(out_two, split_ring(1)), send(val_two, split_ring(1))
    outs = [out_own, out_sibling, out_one, send(out_one, CORE), out_two, send(out_two, CORE)]
    vals = [val_own, val_sibling, val_one, send(val_one, CORE), val_two, send(val_two, CORE)]
    share_b, share_f, sums_b = near_share(where, grad, normed_f, normed_b, outs, vals)
    out_far, val_far, share_b = lax.optimization_barrier((out_far, val_far, share_b))
    outs += [out_far, send(out_far, CORE)]
    vals += [val_far, send(val_far, CORE)]

    first_back, d_values, d_low = first_gradient(
        back, where, share_b, sums_b, grad, normed_b, low_b, saved, factor_b, gain, down, up,
        outs, vals,
    )
    relayed = lax.ppermute(first_back, "section", before)
    share_f, first_back = lax.optimization_barrier((share_f, first_back))
    first_out = output(ahead, where, share_f, normed_f, low_f, up, rows, outs, vals)
    passed = lax.ppermute(first_out, "section", onward)
    first_out, d_low, normed_n = lax.optimization_barrier((first_out, d_low, normed_n))
    mine, other = pack(where, low_b, normed_b, d_values, d_low)
    first_terms = spread(mine, send(other, CORE))
    sums_n = project(where, normed_n, vals)
    relayed, sums_n, *first_terms = lax.optimization_barrier((relayed, sums_n, *first_terms))

    grad_n, d_values, d_low, mine, other = second_values(
        ahead, where, relayed, first_out, target, low_n, normed_n, up, outs
    )
    second_terms = spread(mine, send(other, CORE))
    bwd_out = second_input(
        where, sums_n, low_n, grad_n, rows, saved, factor_n, gain, down, d_values, d_low, vals
    )
    fwd_out = forward(wrapped, where, fresh, passed, gain, down, up, vals, outs)
    down_table, up_table = tables(ahead, back, where, relayed, (*first_terms, *second_terms))
    return (
        fwd_out[None], bwd_out[None], jnp.swapaxes(down_table, 1, 2)[None], up_table[None]
    )


def solution(mesh):
    return jax.shard_map(
        body,
        mesh=mesh,
        in_specs=(
            P("section", "dp", None),
            P("section", "dp", None),
            P("section", None, "dp", None),
            P("dp", None),
            P("dp", None),
            P("section"),
            P("section"),
            P("section", "dp", None),
            P("section", None, "dp"),
            P("section", None),
            P("section", None, None, None),
            P("section", None, None, None),
        ),
        out_specs=(
            P("section", "dp", None),
            P("section", "dp", None),
            P("section", None, "dp", None),
            P("section", None, None, "dp"),
        ),
        check_vma=False,
    )
```

```python
import jax
import jax.numpy as jnp
from jax import lax
from jax.experimental import pallas as pl
from jax.experimental.pallas import tpu as pltpu
from jax.sharding import PartitionSpec as P

SCALE = 0.5
EPS = 1e-05
BF = jnp.bfloat16
F32 = jnp.float32
ROWS = 128
WIDTH = 4096
VALUES = 512
PART = 512
RANK = 64
ADAPTERS = 4
PACK = PART + 128
LOWS = 256
WIDE = WIDTH + 128
VMEM = 20 * 1024 * 1024
ONCE = pl.Buffered(1)


def dot(left, right, dims=((1,), (0,))):
    return lax.dot_general(left, right, (dims, ((), ())), preferred_element_type=F32)


def dot_t(left, right):
    return dot(left, right, ((1,), (1,)))


def t_dot(left, right):
    return dot(left, right, ((0,), (0,)))


def call(kernel, scalars, ins, outs, flops, scratch=()):
    specs, arrays = [], []
    for item in ins:
        array, block, index = item if isinstance(item, tuple) else (item, None, None)
        arrays.append(array)
        if block is None:
            zeros = (0,) * array.ndim
            specs.append(pl.BlockSpec(array.shape, lambda i, *s, z=zeros: z, pipeline_mode=ONCE))
        else:
            specs.append(pl.BlockSpec(block, index, pipeline_mode=ONCE))
    out_specs = [
        pl.BlockSpec(o.shape, lambda i, *s, z=(0,) * len(o.shape): z, pipeline_mode=ONCE)
        for o in outs
    ]
    size = sum(a.size * a.dtype.itemsize for a in arrays)
    return pl.pallas_call(
        kernel,
        out_shape=outs,
        grid_spec=pltpu.PrefetchScalarGridSpec(
            num_scalar_prefetch=len(scalars),
            grid=(1,),
            in_specs=specs,
            out_specs=out_specs,
            scratch_shapes=list(scratch),
        ),
        compiler_params=pltpu.CompilerParams(vmem_limit_bytes=VMEM),
        cost_estimate=pl.CostEstimate(
            flops=flops // 1000, bytes_accessed=size // 1000, transcendentals=0
        ),
    )(*scalars, *arrays)


def shape(dims, dtype):
    return jax.ShapeDtypeStruct(dims, dtype)


def factor_of(rows):
    return lax.rsqrt(jnp.sum(rows * rows, axis=-1, keepdims=True) * (1.0 / WIDTH) + EPS)


def columns(index):
    return pl.ds(pl.multiple_of(index * PART, PART), PART)


def only(lows, ident):
    lane = lax.broadcasted_iota(jnp.int32, lows.shape, 1)
    return jnp.where(lane // RANK == ident, lows, jnp.zeros_like(lows))


def compact(lows):
    total = lows[:, :RANK].astype(F32)
    for k in range(1, ADAPTERS):
        total += lows[:, k * RANK : (k + 1) * RANK].astype(F32)
    return total.astype(BF)


def saved_of(saved, which):
    return (saved, (1, 1, ROWS, WIDTH), lambda i, *s: (0, which, 0, 0))


def prepare_kernel(ahead, back, where, rows_f, rows_b, rows_s, gain, down, *refs):
    last = where[9] == 1
    for kind in range(3):
        normed, factor, low = refs[3 * kind : 3 * kind + 3]
        for top in range(0, ROWS, 32):
            part = slice(top, top + 32)
            if kind == 0:
                whole = rows_f[part, :]
            elif kind == 1:
                whole = rows_b[0, 0, part, :]
            else:
                whole = jnp.where(last, rows_f[part, :], rows_s[0, 0, part, :])
            whole = whole.astype(F32)
            scale = factor_of(whole)
            normed[part, :] = (whole * scale * gain[...]).astype(BF)
            factor[part, :] = jnp.broadcast_to(scale, (32, 128))
        lows = dot_t(normed[...], down[...])
        if kind == 0:
            lows = only(lows, ahead[0])
        elif kind == 1:
            lows = only(lows, back[0])
        low[...] = lows.astype(BF)


def prepare(ahead, back, where, rows, saved, gain, down):
    kinds = [shape((ROWS, WIDTH), BF), shape((ROWS, 128), F32), shape((ROWS, LOWS), BF)]
    return call(
        prepare_kernel,
        (ahead, back, where),
        [rows, saved_of(saved, 0), saved_of(saved, 1), gain, down],
        kinds * 3,
        6 * ROWS * WIDTH * LOWS,
    )


def input_gradient(where, values, lowered, sums, low, grad, rows, scale, gain, down, blocks, out):
    inner = jnp.sum(values.astype(F32) * sums, axis=-1, keepdims=True)
    inner += jnp.sum(lowered.astype(F32) * low.astype(F32), axis=-1, keepdims=True)
    weight = scale * scale * inner * (1.0 / WIDTH)
    for i in range(8):
        span = columns(where[i])
        gained = (dot_t(values, blocks[i][...]) + dot(lowered, down[:, span])) * gain[:, span]
        out[:, span] = (
            grad[:, span].astype(F32) + scale * gained - weight * rows(span).astype(F32)
        ).astype(BF)


def near_kernel(where, grad, normed_f, normed_b, *refs):
    outs, vals, results = refs[:6], refs[6:12], refs[12:]
    total = jnp.zeros((ROWS, VALUES), F32)
    for i in range(6):
        total += dot_t(grad[:, columns(where[i])], outs[i][...])
    results[0][...] = total
    for normed, result in ((normed_f, results[1]), (normed_b, results[2])):
        total = jnp.zeros((ROWS, VALUES), F32)
        for i in range(6):
            total += dot(normed[:, columns(where[i])], vals[i][...])
        result[...] = total


def near_share(where, grad, normed_f, normed_b, outs, vals):
    return call(
        near_kernel,
        (where,),
        [grad, normed_f, normed_b, *outs, *vals],
        [shape((ROWS, VALUES), F32)] * 3,
        6 * ROWS * WIDTH * VALUES,
    )


GRADS = [shape((ROWS, VALUES), BF), shape((ROWS, LOWS), BF)]


def first_kernel(
    back, where, share, sums, grad, normed, low, rows, factor, gain, down, up, far, far_other, *refs
):
    blocks, (out, d_values, d_low) = refs[:8], refs[8:]
    total = share[...]
    total += dot_t(grad[:, columns(where[6])], far[...])
    total += dot_t(grad[:, columns(where[7])], far_other[...])
    values = total.astype(BF)
    lowered = only(SCALE * dot_t(values, up[...]), back[0]).astype(BF)
    d_values[...] = values
    d_low[...] = lowered
    total = sums[...]
    for i in (6, 7):
        total += dot(normed[:, columns(where[i])], blocks[i][...])
    input_gradient(
        where, values, lowered, total, low[...], grad, lambda span: rows[0, 0, :, span],
        factor[:, :1], gain, down, blocks, out,
    )
    out[:, WIDTH:] = jnp.full((ROWS, 128), back[0], jnp.int32).astype(F32).astype(BF)


def first_gradient(
    back, where, share, sums, grad, normed, low, saved, factor, gain, down, up, outs, vals
):
    return call(
        first_kernel,
        (back, where),
        [
            share, sums, grad, normed, low, saved_of(saved, 0), factor, gain, down, up,
            *outs[6:], *vals,
        ],
        [shape((ROWS, WIDE), BF), *GRADS],
        2 * ROWS * WIDTH * VALUES,
    )


def project_kernel(where, normed, *refs):
    blocks, out = refs[:8], refs[8]
    total = jnp.zeros((ROWS, VALUES), F32)
    for i in range(8):
        total += dot(normed[:, columns(where[i])], blocks[i][...])
    out[...] = total


def project(where, normed, vals):
    return call(
        project_kernel, (where,), [normed, *vals], [shape((ROWS, VALUES), F32)],
        2 * ROWS * WIDTH * VALUES,
    )[0]


def output_kernel(ahead, where, share, normed, low, up, rows, far, far_other, *refs):
    blocks, out = refs[:8], refs[8]
    total = share[...] + SCALE * dot(low[...], up[...])
    total += dot(normed[:, columns(where[6])], far[...])
    total += dot(normed[:, columns(where[7])], far_other[...])
    values = total.astype(BF)
    for i in range(8):
        span = columns(where[i])
        out[:, span] = (rows[:, span].astype(F32) + dot(values, blocks[i][...])).astype(BF)
    out[:, WIDTH:] = jnp.full((ROWS, 128), ahead[0], jnp.int32).astype(F32).astype(BF)


def output(ahead, where, share, normed, low, up, rows, outs, vals):
    return call(
        output_kernel,
        (ahead, where),
        [share, normed, low, up, rows, *vals[6:], *outs],
        [shape((ROWS, WIDE), BF)],
        2 * ROWS * WIDTH * VALUES,
    )[0]


def pack_gradients(where, low, normed, d_values, d_low, mine, other):
    up_term = SCALE * t_dot(low, d_values)
    chip, core = where[0] // 2, where[0] % 2
    for ahead in range(4):
        target = lax.rem(chip + ahead, 4)
        pair = up_term[:, 0:128]
        for k in range(1, 4):
            pair = jnp.where(target == k, up_term[:, 128 * k : 128 * (k + 1)], pair)
        pair = pair.astype(BF)
        for ref, c in ((mine, core), (other, 1 - core)):
            ref[ahead, :, :PART] = t_dot(d_low, normed[:, columns(2 * target + c)]).astype(BF)
            ref[ahead, :, PART:] = pair


PACKED = [shape((4, RANK, PACK), BF)] * 2


def pack_kernel(where, low, normed, d_values, d_low, mine, other):
    pack_gradients(
        where, compact(low[...]), normed, d_values[...], compact(d_low[...]), mine, other
    )


def pack(where, low, normed, d_values, d_low):
    return call(
        pack_kernel, (where,), [low, normed, d_values, d_low], PACKED, 2 * ROWS * WIDTH * RANK
    )


def second_kernel(ahead, where, relayed, out, target, low, normed, up, *refs):
    blocks, (grad, d_values, d_low, mine, other) = refs[:8], refs[8:]
    last = where[9] == 1
    total = jnp.zeros((ROWS, VALUES), F32)
    for i in range(8):
        span = columns(where[i])
        loss = (out[:, span].astype(F32) - target[:, span].astype(F32)).astype(BF)
        chosen = jnp.where(last, loss, relayed[:, span])
        grad[:, span] = chosen
        total += dot_t(chosen, blocks[i][...])
    values = total.astype(BF)
    came = relayed[:, WIDTH : WIDTH + 1].astype(F32).astype(jnp.int32)
    ident = jnp.where(last, ahead[0], came)
    lowered = only(SCALE * dot_t(values, up[...]), ident).astype(BF)
    d_values[...] = values
    d_low[...] = lowered
    pack_gradients(
        where, compact(only(low[...], ident)), normed, values, compact(lowered), mine, other
    )


def second_values(ahead, where, relayed, out, target, low, normed, up, blocks):
    return call(
        second_kernel,
        (ahead, where),
        [relayed, out, target, low, normed, up, *blocks],
        [shape((ROWS, WIDTH), BF), *GRADS, *PACKED],
        2 * ROWS * WIDTH * (VALUES + RANK),
    )


def second_input_kernel(
    where, sums, low, grad, rows_f, rows_s, factor, gain, down, d_values, d_low, *refs
):
    blocks, out = refs[:8], refs[8]
    last = where[9] == 1
    input_gradient(
        where, d_values[...], d_low[...], sums[...], low[...], grad,
        lambda span: jnp.where(last, rows_f[:, span], rows_s[0, 0, :, span]),
        factor[:, :1], gain, down, blocks, out,
    )


def second_input(where, sums, low, grad, rows, saved, factor, gain, down, d_values, d_low, blocks):
    return call(
        second_input_kernel,
        (where,),
        [
            sums, low, grad, rows, saved_of(saved, 1), factor, gain, down, d_values, d_low, *blocks
        ],
        [shape((ROWS, WIDTH), BF)],
        2 * ROWS * WIDTH * (VALUES + RANK),
    )[0]


def forward_kernel(where, fresh, passed, gain, down, up, *refs):
    vals, outs, (out, rows, normed) = refs[:8], refs[8:16], refs[16:]
    first = where[8] == 1
    for top in range(0, ROWS, 32):
        part = slice(top, top + 32)
        chosen = jnp.where(first, fresh[part, :], passed[part, :WIDTH])
        whole = chosen.astype(F32)
        rows[part, :] = chosen
        normed[part, :] = (whole * factor_of(whole) * gain[...]).astype(BF)
    ident = passed[:, WIDTH : WIDTH + 1].astype(F32).astype(jnp.int32)
    low = only(dot_t(normed[...], down[...]), ident).astype(BF)
    total = SCALE * dot(low, up[...])
    for i in range(8):
        total += dot(normed[:, columns(where[i])], vals[i][...])
    values = total.astype(BF)
    for i in range(8):
        span = columns(where[i])
        out[:, span] = (rows[:, span].astype(F32) + dot(values, outs[i][...])).astype(BF)


def forward(where, fresh, passed, gain, down, up, vals, outs):
    return call(
        forward_kernel,
        (where,),
        [fresh, passed, gain, down, up, *vals, *outs],
        [shape((ROWS, WIDTH), BF)],
        4 * ROWS * WIDTH * VALUES,
        [pltpu.VMEM((ROWS, WIDTH), BF), pltpu.VMEM((ROWS, WIDTH), BF)],
    )[0]


def pair_sum_kernel(mine, other, total):
    total[...] = (mine[...].astype(F32) + other[...].astype(F32)).astype(BF)


def pair_sum(mine, other):
    return call(pair_sum_kernel, (), [mine, other], [shape((4, RANK, PACK), BF)], 0)[0]


def stack_kernel(first, mine, other, own, one, two, three):
    for ahead, ref in enumerate((own, one, two, three)):
        ref[0] = first[ahead]
        ref[1] = (mine[ahead].astype(F32) + other[ahead].astype(F32)).astype(BF)


def spread(first, mine, received):
    block = shape((2, RANK, PACK), BF)
    own, one, two, three = call(stack_kernel, (), [first, mine, received], [block] * 4, 0)
    return (
        own,
        lax.ppermute(two, "dp", chips(2)),
        lax.ppermute(one, "dp", chips(1)),
        lax.ppermute(three, "dp", chips(3)),
    )


def tables_kernel(ahead, back, where, relayed, *refs):
    terms, (down, up) = refs[:4], refs[4:]
    core = where[0] % 2
    came = relayed[:RANK, :1].astype(F32).astype(jnp.int32)
    ident = jnp.where(where[9] == 1, ahead[0], came)
    sums = []
    for tick in range(2):
        total = terms[0][tick].astype(F32)
        for k in range(1, 4):
            total += terms[k][tick].astype(F32)
        sums.append(total)
    for label in range(ADAPTERS):
        one = jnp.where(back[0] == label, 1.0, 0.0)
        two = jnp.where(ident == label, 1.0, 0.0)
        total = one * sums[0] + two * sums[1]
        down[label] = total[:, :PART]
        up[label] = jnp.where(core == 0, total[:, PART : PART + 64], total[:, PART + 64 :])


def tables(ahead, back, where, relayed, terms):
    tail = (relayed, (ROWS, 128), lambda i, *s: (0, WIDTH // 128))
    return call(
        tables_kernel,
        (ahead, back, where),
        [tail, *terms],
        [shape((ADAPTERS, RANK, PART), F32), shape((ADAPTERS, RANK, 64), F32)],
        0,
    )


CORE = [(i, i ^ 1) for i in range(8)]


def chips(by):
    return [(i, ((i // 2 + by) % 4) * 2 + i % 2) for i in range(8)]


def split_ring(by):
    return [(i, ((i // 2 + (by if i % 2 == 0 else -by)) % 4) * 2 + i % 2) for i in range(8)]


def send(block, pairs):
    return lax.ppermute(block, "dp", pairs)


def block_index():
    place = lax.axis_index("dp")
    chip, core = place // 2, place % 2
    other = 1 - core
    step = jnp.where(core == 0, 1, -1)
    block = lambda k, c: 2 * (k % 4) + c
    return [
        block(chip, core), block(chip, other),
        block(chip - step + 4, core), block(chip + step + 4, other),
        block(chip + 2, core), block(chip + 2, other),
        block(chip + step + 4, core), block(chip - step + 4, other),
    ]


def body(
    forward_state, backward_state, saved, fresh, target, forward_adapter, backward_adapter,
    value_projection, output_matrix, norm_gain_frozen, adapter_down, adapter_up,
):
    count = lax.axis_size("section")
    onward = [(i, (i + 1) % count) for i in range(count)]
    before = [(i, i - 1) for i in range(1, count)]
    position = lax.axis_index("section")
    where = jnp.stack(
        [v.astype(jnp.int32) for v in (*block_index(), position == 0, position == count - 1)]
    )
    gain = norm_gain_frozen
    down = jnp.swapaxes(adapter_down[0], 1, 2).reshape(LOWS, WIDTH)
    up = adapter_up[0].reshape(LOWS, VALUES)
    rows, grad = forward_state[0], backward_state[0]
    ahead, back = forward_adapter, backward_adapter

    out_own, val_own = output_matrix[0], value_projection[0]
    out_one, val_one = send(out_own, split_ring(1)), send(val_own, split_ring(1))
    out_sibling, val_sibling = send(out_own, CORE), send(val_own, CORE)

    normed_f, _, low_f, normed_b, factor_b, low_b, normed_n, factor_n, low_n = prepare(
        ahead, back, where, rows, saved, gain, down
    )
    out_one, normed_f, out_sibling, val_sibling = lax.optimization_barrier(
        (out_one, normed_f, out_sibling, val_sibling)
    )
    out_two, val_two = send(out_one, split_ring(1)), send(val_one, split_ring(1))
    out_far, val_far = send(out_two, split_ring(1)), send(val_two, split_ring(1))
    outs = [out_own, out_sibling, out_one, send(out_one, CORE), out_two, send(out_two, CORE)]
    vals = [val_own, val_sibling, val_one, send(val_one, CORE), val_two, send(val_two, CORE)]
    share_b, share_f, sums_b = near_share(where, grad, normed_f, normed_b, outs, vals)
    out_far, val_far, share_b = lax.optimization_barrier((out_far, val_far, share_b))
    outs += [out_far, send(out_far, CORE)]
    vals += [val_far, send(val_far, CORE)]

    first_back, d_values, d_low = first_gradient(
        back, where, share_b, sums_b, grad, normed_b, low_b, saved, factor_b, gain, down, up,
        outs, vals,
    )
    relayed = lax.ppermute(first_back, "section", before)
    share_f, first_back = lax.optimization_barrier((share_f, first_back))
    first_out = output(ahead, where, share_f, normed_f, low_f, up, rows, outs, vals)
    passed = lax.ppermute(first_out, "section", onward)
    first_out, d_low, normed_n = lax.optimization_barrier((first_out, d_low, normed_n))
    mine, other = pack(where, low_b, normed_b, d_values, d_low)
    first_sums = pair_sum(mine, send(other, CORE))
    sums_n = project(where, normed_n, vals)
    relayed, sums_n, first_sums = lax.optimization_barrier((relayed, sums_n, first_sums))

    grad_n, d_values, d_low, mine, other = second_values(
        ahead, where, relayed, first_out, target, low_n, normed_n, up, outs
    )
    terms = spread(first_sums, mine, send(other, CORE))
    bwd_out = second_input(
        where, sums_n, low_n, grad_n, rows, saved, factor_n, gain, down, d_values, d_low, vals
    )
    fwd_out = forward(where, fresh, passed, gain, down, up, vals, outs)
    down_table, up_table = tables(ahead, back, where, relayed, terms)
    return (
        fwd_out[None], bwd_out[None], jnp.swapaxes(down_table, 1, 2)[None], up_table[None]
    )


def solution(mesh):
    return jax.shard_map(
        body,
        mesh=mesh,
        in_specs=(
            P("section", "dp", None),
            P("section", "dp", None),
            P("section", None, "dp", None),
            P("dp", None),
            P("dp", None),
            P("section"),
            P("section"),
            P("section", "dp", None),
            P("section", None, "dp"),
            P("section", None),
            P("section", None, None, None),
            P("section", None, None, None),
        ),
        out_specs=(
            P("section", "dp", None),
            P("section", "dp", None),
            P("section", None, "dp", None),
            P("section", None, None, "dp"),
        ),
        check_vma=False,
    )
```

```python
import jax
import jax.numpy as jnp
from jax import lax
from jax.experimental import pallas as pl
from jax.experimental.pallas import tpu as pltpu
from jax.sharding import PartitionSpec as P

SCALE = 0.5
EPS = 1e-05
BF = jnp.bfloat16
F32 = jnp.float32
ROWS = 128
WIDTH = 4096
VALUES = 512
PART = 512
RANK = 64
ADAPTERS = 4
PACK = PART + 128
LOWS = 256
WIDE = WIDTH + 128
VMEM = 20 * 1024 * 1024
ONCE = pl.Buffered(1)


def dot(left, right, dims=((1,), (0,))):
    return lax.dot_general(left, right, (dims, ((), ())), preferred_element_type=F32)


def dot_t(left, right):
    return dot(left, right, ((1,), (1,)))


def t_dot(left, right):
    return dot(left, right, ((0,), (0,)))


def call(kernel, scalars, ins, outs, flops, scratch=()):
    specs, arrays = [], []
    for item in ins:
        array, block, index = item if isinstance(item, tuple) else (item, None, None)
        arrays.append(array)
        if block is None:
            zeros = (0,) * array.ndim
            specs.append(pl.BlockSpec(array.shape, lambda i, *s, z=zeros: z, pipeline_mode=ONCE))
        else:
            specs.append(pl.BlockSpec(block, index, pipeline_mode=ONCE))
    out_specs = [
        pl.BlockSpec(o.shape, lambda i, *s, z=(0,) * len(o.shape): z, pipeline_mode=ONCE)
        for o in outs
    ]
    size = sum(a.size * a.dtype.itemsize for a in arrays)
    return pl.pallas_call(
        kernel,
        out_shape=outs,
        grid_spec=pltpu.PrefetchScalarGridSpec(
            num_scalar_prefetch=len(scalars),
            grid=(1,),
            in_specs=specs,
            out_specs=out_specs,
            scratch_shapes=list(scratch),
        ),
        compiler_params=pltpu.CompilerParams(vmem_limit_bytes=VMEM),
        cost_estimate=pl.CostEstimate(
            flops=flops // 1000, bytes_accessed=size // 1000, transcendentals=0
        ),
    )(*scalars, *arrays)


def shape(dims, dtype):
    return jax.ShapeDtypeStruct(dims, dtype)


def factor_of(rows):
    return lax.rsqrt(jnp.sum(rows * rows, axis=-1, keepdims=True) * (1.0 / WIDTH) + EPS)


def columns(index):
    return pl.ds(pl.multiple_of(index * PART, PART), PART)


def only(lows, ident):
    lane = lax.broadcasted_iota(jnp.int32, lows.shape, 1)
    return jnp.where(lane // RANK == ident, lows, jnp.zeros_like(lows))


def compact(lows):
    total = lows[:, :RANK].astype(F32)
    for k in range(1, ADAPTERS):
        total += lows[:, k * RANK : (k + 1) * RANK].astype(F32)
    return total.astype(BF)


def saved_of(saved, which):
    return (saved, (1, 1, ROWS, WIDTH), lambda i, *s: (0, which, 0, 0))


def prepare_kernel(ahead, back, where, rows_f, rows_b, rows_s, gain, down, *refs):
    last = where[9] == 1
    for kind in range(3):
        normed, factor, low = refs[3 * kind : 3 * kind + 3]
        for top in range(0, ROWS, 32):
            part = slice(top, top + 32)
            if kind == 0:
                whole = rows_f[part, :]
            elif kind == 1:
                whole = rows_b[0, 0, part, :]
            else:
                whole = jnp.where(last, rows_f[part, :], rows_s[0, 0, part, :])
            whole = whole.astype(F32)
            scale = factor_of(whole)
            normed[part, :] = (whole * scale * gain[...]).astype(BF)
            factor[part, :] = jnp.broadcast_to(scale, (32, 128))
        lows = dot_t(normed[...], down[...])
        if kind == 0:
            lows = only(lows, ahead[0])
        elif kind == 1:
            lows = only(lows, back[0])
        low[...] = lows.astype(BF)


def prepare(ahead, back, where, rows, saved, gain, down):
    kinds = [shape((ROWS, WIDTH), BF), shape((ROWS, 128), F32), shape((ROWS, LOWS), BF)]
    return call(
        prepare_kernel,
        (ahead, back, where),
        [rows, saved_of(saved, 0), saved_of(saved, 1), gain, down],
        kinds * 3,
        6 * ROWS * WIDTH * LOWS,
    )


def gained_block(values, lowered, span, gain, down, block):
    return (dot_t(values, block[...]) + dot(lowered, down[:, span])) * gain[:, span]


def input_gradient(where, grad, rows, scale, inner, gained, out):
    inner = inner * (1.0 / WIDTH)
    for i in range(8):
        span = columns(where[i])
        pre = rows(span).astype(F32) * scale
        out[:, span] = (
            grad[:, span].astype(F32) + scale * (gained(i) - pre * inner)
        ).astype(BF)


def near_kernel(back, where, grad, normed, rows, factor, gain, down, up, *refs):
    outs, vals, (d_values, d_low, kept, inner, share) = refs[:8], refs[8:14], refs[14:]
    total = jnp.zeros((ROWS, VALUES), F32)
    for i in range(8):
        total += dot_t(grad[:, columns(where[i])], outs[i][...])
    values = total.astype(BF)
    lowered = only(SCALE * dot_t(values, up[...]), back[0]).astype(BF)
    d_values[...] = values
    d_low[...] = lowered
    scale = factor[:, :1]
    mean = jnp.zeros((ROWS, 1), F32)
    for i in range(6):
        span = columns(where[i])
        gained = gained_block(values, lowered, span, gain, down, vals[i])
        kept[i] = gained
        mean += jnp.sum(
            gained * (rows[0, 0, :, span].astype(F32) * scale), axis=-1, keepdims=True
        )
    inner[...] = jnp.broadcast_to(mean, (ROWS, 128))
    total = jnp.zeros((ROWS, VALUES), F32)
    for i in range(6):
        total += dot(normed[:, columns(where[i])], vals[i][...])
    share[...] = total


GRADS = [shape((ROWS, VALUES), BF), shape((ROWS, LOWS), BF)]


def near_share(back, where, grad, normed, saved, factor, gain, down, up, outs, vals):
    return call(
        near_kernel,
        (back, where),
        [grad, normed, saved_of(saved, 0), factor, gain, down, up, *outs, *vals],
        [*GRADS, shape((6, ROWS, PART), F32), shape((ROWS, 128), F32), shape((ROWS, VALUES), F32)],
        6 * ROWS * WIDTH * VALUES,
    )


def first_kernel(
    back, where, kept, inner, values, lowered, grad, rows, factor, gain, down, far, far_other, out
):
    scale = factor[:, :1]
    mean = inner[:, :1]
    last = []
    for i, block in ((6, far), (7, far_other)):
        span = columns(where[i])
        gained = gained_block(values[...], lowered[...], span, gain, down, block)
        mean += jnp.sum(
            gained * (rows[0, 0, :, span].astype(F32) * scale), axis=-1, keepdims=True
        )
        last.append(gained)
    input_gradient(
        where, grad, lambda span: rows[0, 0, :, span], scale, mean,
        lambda i: kept[i] if i < 6 else last[i - 6], out,
    )
    out[:, WIDTH:] = jnp.full((ROWS, 128), back[0], jnp.int32).astype(F32).astype(BF)


def first_gradient(back, where, kept, inner, d_values, d_low, grad, saved, factor, gain, down, vals):
    return call(
        first_kernel,
        (back, where),
        [
            kept, inner, d_values, d_low, grad, saved_of(saved, 0), factor, gain, down, *vals[6:]
        ],
        [shape((ROWS, WIDE), BF)],
        ROWS * WIDTH * VALUES,
    )[0]


def output_kernel(ahead, where, share, normed, low, up, rows, far, far_other, *refs):
    blocks, out = refs[:8], refs[8]
    total = share[...] + SCALE * dot(low[...], up[...])
    total += dot(normed[:, columns(where[6])], far[...])
    total += dot(normed[:, columns(where[7])], far_other[...])
    values = total.astype(BF)
    for i in range(8):
        span = columns(where[i])
        out[:, span] = (rows[:, span].astype(F32) + dot(values, blocks[i][...])).astype(BF)
    out[:, WIDTH:] = jnp.full((ROWS, 128), ahead[0], jnp.int32).astype(F32).astype(BF)


def output(ahead, where, share, normed, low, up, rows, outs, vals):
    return call(
        output_kernel,
        (ahead, where),
        [share, normed, low, up, rows, *vals[6:], *outs],
        [shape((ROWS, WIDE), BF)],
        2 * ROWS * WIDTH * VALUES,
    )[0]


def pack_gradients(where, low, normed, d_values, d_low, mine, other):
    up_term = SCALE * t_dot(low, d_values)
    chip, core = where[0] // 2, where[0] % 2
    for ahead in range(4):
        target = lax.rem(chip + ahead, 4)
        pair = up_term[:, 0:128]
        for k in range(1, 4):
            pair = jnp.where(target == k, up_term[:, 128 * k : 128 * (k + 1)], pair)
        pair = pair.astype(BF)
        for ref, c in ((mine, core), (other, 1 - core)):
            ref[ahead, :, :PART] = t_dot(d_low, normed[:, columns(2 * target + c)]).astype(BF)
            ref[ahead, :, PART:] = pair


PACKED = [shape((4, RANK, PACK), BF)] * 2


def pack_kernel(where, low, normed, d_values, d_low, mine, other):
    pack_gradients(
        where, compact(low[...]), normed, d_values[...], compact(d_low[...]), mine, other
    )


def pack(where, low, normed, d_values, d_low):
    return call(
        pack_kernel, (where,), [low, normed, d_values, d_low], PACKED, 2 * ROWS * WIDTH * RANK
    )


def second_kernel(ahead, where, relayed, out, target, low, normed, up, *refs):
    blocks, (grad, d_values, d_low, mine, other) = refs[:8], refs[8:]
    last = where[9] == 1
    total = jnp.zeros((ROWS, VALUES), F32)
    for i in range(8):
        span = columns(where[i])
        loss = (out[:, span].astype(F32) - target[:, span].astype(F32)).astype(BF)
        chosen = jnp.where(last, loss, relayed[:, span])
        grad[:, span] = chosen
        total += dot_t(chosen, blocks[i][...])
    values = total.astype(BF)
    came = relayed[:, WIDTH : WIDTH + 1].astype(F32).astype(jnp.int32)
    ident = jnp.where(last, ahead[0], came)
    lowered = only(SCALE * dot_t(values, up[...]), ident).astype(BF)
    d_values[...] = values
    d_low[...] = lowered
    pack_gradients(
        where, compact(only(low[...], ident)), normed, values, compact(lowered), mine, other
    )


def second_values(ahead, where, relayed, out, target, low, normed, up, blocks):
    return call(
        second_kernel,
        (ahead, where),
        [relayed, out, target, low, normed, up, *blocks],
        [shape((ROWS, WIDTH), BF), *GRADS, *PACKED],
        2 * ROWS * WIDTH * (VALUES + RANK),
    )


def project_kernel(where, normed, *refs):
    blocks, out = refs[:8], refs[8]
    total = jnp.zeros((ROWS, VALUES), F32)
    for i in range(8):
        total += dot(normed[:, columns(where[i])], blocks[i][...])
    out[...] = total


def project(where, normed, vals):
    return call(
        project_kernel, (where,), [normed, *vals], [shape((ROWS, VALUES), F32)],
        2 * ROWS * WIDTH * VALUES,
    )[0]


def second_input_kernel(
    where, sums, low, grad, rows_f, rows_s, factor, gain, down, d_values, d_low, *refs
):
    blocks, out = refs[:8], refs[8]
    last = where[9] == 1
    scale = factor[:, :1]
    values, lowered = d_values[...], d_low[...]
    inner = jnp.sum(values.astype(F32) * sums[...], axis=-1, keepdims=True)
    inner += jnp.sum(lowered.astype(F32) * low[...].astype(F32), axis=-1, keepdims=True)
    weight = scale * scale * inner * (1.0 / WIDTH)
    for i in range(8):
        span = columns(where[i])
        rows = jnp.where(last, rows_f[:, span], rows_s[0, 0, :, span]).astype(F32)
        gained = gained_block(values, lowered, span, gain, down, blocks[i])
        out[:, span] = (grad[:, span].astype(F32) + scale * gained - weight * rows).astype(BF)


def second_input(where, sums, low, grad, rows, saved, factor, gain, down, d_values, d_low, blocks):
    return call(
        second_input_kernel,
        (where,),
        [
            sums, low, grad, rows, saved_of(saved, 1), factor, gain, down, d_values, d_low, *blocks
        ],
        [shape((ROWS, WIDTH), BF)],
        2 * ROWS * WIDTH * (VALUES + RANK),
    )[0]


def forward_kernel(where, fresh, passed, gain, down, up, *refs):
    vals, outs, (out, rows, normed) = refs[:8], refs[8:16], refs[16:]
    first = where[8] == 1
    for top in range(0, ROWS, 32):
        part = slice(top, top + 32)
        chosen = jnp.where(first, fresh[part, :], passed[part, :WIDTH])
        whole = chosen.astype(F32)
        rows[part, :] = chosen
        normed[part, :] = (whole * factor_of(whole) * gain[...]).astype(BF)
    ident = passed[:, WIDTH : WIDTH + 1].astype(F32).astype(jnp.int32)
    low = only(dot_t(normed[...], down[...]), ident).astype(BF)
    total = SCALE * dot(low, up[...])
    for i in range(8):
        total += dot(normed[:, columns(where[i])], vals[i][...])
    values = total.astype(BF)
    for i in range(8):
        span = columns(where[i])
        out[:, span] = (rows[:, span].astype(F32) + dot(values, outs[i][...])).astype(BF)


def forward(where, fresh, passed, gain, down, up, vals, outs):
    return call(
        forward_kernel,
        (where,),
        [fresh, passed, gain, down, up, *vals, *outs],
        [shape((ROWS, WIDTH), BF)],
        4 * ROWS * WIDTH * VALUES,
        [pltpu.VMEM((ROWS, WIDTH), BF), pltpu.VMEM((ROWS, WIDTH), BF)],
    )[0]


def pair_sum_kernel(mine, other, own, one, two, three):
    for ahead, ref in enumerate((own, one, two, three)):
        ref[...] = (mine[ahead].astype(F32) + other[ahead].astype(F32)).astype(BF)


def chip_sums(mine, received):
    return call(pair_sum_kernel, (), [mine, received], [shape((RANK, PACK), BF)] * 4, 0)


def spread(own, one, two, three):
    return (own, *(send(block, chips(k)) for k, block in ((2, two), (1, one), (3, three))))


def tables_kernel(ahead, back, where, relayed, *refs):
    terms, (down, up) = refs[:8], refs[8:]
    core = where[0] % 2
    came = relayed[:RANK, :1].astype(F32).astype(jnp.int32)
    ident = jnp.where(where[9] == 1, ahead[0], came)
    sums = []
    for tick in range(2):
        total = terms[4 * tick][...].astype(F32)
        for k in range(1, 4):
            total += terms[4 * tick + k][...].astype(F32)
        sums.append(total)
    for label in range(ADAPTERS):
        one = jnp.where(back[0] == label, 1.0, 0.0)
        two = jnp.where(ident == label, 1.0, 0.0)
        total = one * sums[0] + two * sums[1]
        down[label] = total[:, :PART]
        up[label] = jnp.where(core == 0, total[:, PART : PART + 64], total[:, PART + 64 :])


def tables(ahead, back, where, relayed, terms):
    tail = (relayed, (ROWS, 128), lambda i, *s: (0, WIDTH // 128))
    return call(
        tables_kernel,
        (ahead, back, where),
        [tail, *terms],
        [shape((ADAPTERS, RANK, PART), F32), shape((ADAPTERS, RANK, 64), F32)],
        0,
    )


CORE = [(i, i ^ 1) for i in range(8)]


def chips(by):
    return [(i, ((i // 2 + by) % 4) * 2 + i % 2) for i in range(8)]


def split_ring(sign):
    return [(i, ((i // 2 + (sign if i % 2 == 0 else -sign)) % 4) * 2 + i % 2) for i in range(8)]


def send(block, pairs):
    return lax.ppermute(block, "dp", pairs)


def block_index():
    place = lax.axis_index("dp")
    chip, core = place // 2, place % 2
    other = 1 - core
    step = jnp.where(core == 0, 1, -1)
    block = lambda k, c: 2 * (k % 4) + c
    return [
        block(chip, core), block(chip, other),
        block(chip - step + 4, core), block(chip + step + 4, other),
        block(chip + step + 4, core), block(chip - step + 4, other),
        block(chip + 2, core), block(chip + 2, other),
    ]


def body(
    forward_state, backward_state, saved, fresh, target, forward_adapter, backward_adapter,
    value_projection, output_matrix, norm_gain_frozen, adapter_down, adapter_up,
):
    count = lax.axis_size("section")
    onward = [(i, (i + 1) % count) for i in range(count)]
    before = [(i, i - 1) for i in range(1, count)]
    position = lax.axis_index("section")
    where = jnp.stack(
        [v.astype(jnp.int32) for v in (*block_index(), position == 0, position == count - 1)]
    )
    gain = norm_gain_frozen
    down = jnp.swapaxes(adapter_down[0], 1, 2).reshape(LOWS, WIDTH)
    up = adapter_up[0].reshape(LOWS, VALUES)
    rows, grad = forward_state[0], backward_state[0]
    ahead, back = forward_adapter, backward_adapter

    out_own, val_own = output_matrix[0], value_projection[0]
    out_near, out_away = send(out_own, split_ring(1)), send(out_own, split_ring(-1))
    val_near, val_away = send(val_own, split_ring(1)), send(val_own, split_ring(-1))
    out_sibling, val_sibling = send(out_own, CORE), send(val_own, CORE)

    normed_f, _, low_f, normed_b, factor_b, low_b, normed_n, factor_n, low_n = prepare(
        ahead, back, where, rows, saved, gain, down
    )
    out_near, normed_f = lax.optimization_barrier((out_near, normed_f))
    out_far, val_far = send(out_near, split_ring(1)), send(val_near, split_ring(1))
    outs = [
        out_own, out_sibling, out_near, send(out_near, CORE), out_away, send(out_away, CORE)
    ]
    vals = [
        val_own, val_sibling, val_near, send(val_near, CORE), val_away, send(val_away, CORE)
    ]
    outs += [out_far, send(out_far, CORE)]
    d_values, d_low, kept, inner, share_f = near_share(
        back, where, grad, normed_f, saved, factor_b, gain, down, up, outs, vals
    )
    mine, other = pack(where, low_b, normed_b, d_values, d_low)
    first_sums = chip_sums(mine, send(other, CORE))
    val_far, *first_sums = lax.optimization_barrier((val_far, *first_sums))
    vals += [val_far, send(val_far, CORE)]

    first_back = first_gradient(
        back, where, kept, inner, d_values, d_low, grad, saved, factor_b, gain, down, vals
    )
    relayed = lax.ppermute(first_back, "section", before)
    share_f, first_back, *first_sums = lax.optimization_barrier(
        (share_f, first_back, *first_sums)
    )
    first_terms = list(spread(*first_sums))
    share_f, first_terms[2] = lax.optimization_barrier((share_f, first_terms[2]))
    first_out = output(ahead, where, share_f, normed_f, low_f, up, rows, outs, vals)
    passed = lax.ppermute(first_out, "section", onward)
    sums_n = project(where, normed_n, vals)
    relayed, sums_n, *first_terms = lax.optimization_barrier((relayed, sums_n, *first_terms))

    grad_n, d_values, d_low, mine, other = second_values(
        ahead, where, relayed, first_out, target, low_n, normed_n, up, outs
    )
    second_terms = spread(*chip_sums(mine, send(other, CORE)))
    bwd_out = second_input(
        where, sums_n, low_n, grad_n, rows, saved, factor_n, gain, down, d_values, d_low, vals
    )
    fwd_out = forward(where, fresh, passed, gain, down, up, vals, outs)
    down_table, up_table = tables(ahead, back, where, relayed, (*first_terms, *second_terms))
    return (
        fwd_out[None], bwd_out[None], jnp.swapaxes(down_table, 1, 2)[None], up_table[None]
    )


def solution(mesh):
    return jax.shard_map(
        body,
        mesh=mesh,
        in_specs=(
            P("section", "dp", None),
            P("section", "dp", None),
            P("section", None, "dp", None),
            P("dp", None),
            P("dp", None),
            P("section"),
            P("section"),
            P("section", "dp", None),
            P("section", None, "dp"),
            P("section", None),
            P("section", None, None, None),
            P("section", None, None, None),
        ),
        out_specs=(
            P("section", "dp", None),
            P("section", "dp", None),
            P("section", None, "dp", None),
            P("section", None, None, "dp"),
        ),
        check_vma=False,
    )
```

```python
import jax
import jax.numpy as jnp
from jax import lax
from jax.experimental import pallas as pl
from jax.experimental.pallas import tpu as pltpu
from jax.sharding import PartitionSpec as P

SCALE = 0.5
EPS = 1e-05
BF = jnp.bfloat16
F32 = jnp.float32
ROWS = 128
WIDTH = 4096
VALUES = 512
PART = 512
RANK = 64
ADAPTERS = 4
PACK = PART + 128
LOWS = 256
WIDE = WIDTH + 128
VMEM = 20 * 1024 * 1024
ONCE = pl.Buffered(1)


def dot(left, right, dims=((1,), (0,))):
    return lax.dot_general(left, right, (dims, ((), ())), preferred_element_type=F32)


def dot_t(left, right):
    return dot(left, right, ((1,), (1,)))


def t_dot(left, right):
    return dot(left, right, ((0,), (0,)))


def call(kernel, scalars, ins, outs, flops, scratch=()):
    specs, arrays = [], []
    for item in ins:
        array, block, index = item if isinstance(item, tuple) else (item, None, None)
        arrays.append(array)
        if block is None:
            zeros = (0,) * array.ndim
            specs.append(pl.BlockSpec(array.shape, lambda i, *s, z=zeros: z, pipeline_mode=ONCE))
        else:
            specs.append(pl.BlockSpec(block, index, pipeline_mode=ONCE))
    out_specs = [
        pl.BlockSpec(o.shape, lambda i, *s, z=(0,) * len(o.shape): z, pipeline_mode=ONCE)
        for o in outs
    ]
    size = sum(a.size * a.dtype.itemsize for a in arrays)
    return pl.pallas_call(
        kernel,
        out_shape=outs,
        grid_spec=pltpu.PrefetchScalarGridSpec(
            num_scalar_prefetch=len(scalars),
            grid=(1,),
            in_specs=specs,
            out_specs=out_specs,
            scratch_shapes=list(scratch),
        ),
        compiler_params=pltpu.CompilerParams(vmem_limit_bytes=VMEM),
        cost_estimate=pl.CostEstimate(
            flops=flops // 1000, bytes_accessed=size // 1000, transcendentals=0
        ),
    )(*scalars, *arrays)


def shape(dims, dtype):
    return jax.ShapeDtypeStruct(dims, dtype)


def factor_of(rows):
    return lax.rsqrt(jnp.sum(rows * rows, axis=-1, keepdims=True) * (1.0 / WIDTH) + EPS)


def columns(index):
    return pl.ds(pl.multiple_of(index * PART, PART), PART)


def only(lows, ident):
    lane = lax.broadcasted_iota(jnp.int32, lows.shape, 1)
    return jnp.where(lane // RANK == ident, lows, jnp.zeros_like(lows))


def compact(lows):
    total = lows[:, :RANK].astype(F32)
    for k in range(1, ADAPTERS):
        total += lows[:, k * RANK : (k + 1) * RANK].astype(F32)
    return total.astype(BF)


def saved_of(saved, which):
    return (saved, (1, 1, ROWS, WIDTH), lambda i, *s: (0, which, 0, 0))


def prepare_kernel(ahead, back, where, rows_f, rows_b, rows_s, gain, down, *refs):
    last = where[9] == 1
    for kind in range(3):
        normed, factor, low = refs[3 * kind : 3 * kind + 3]
        for top in range(0, ROWS, 32):
            part = slice(top, top + 32)
            if kind == 0:
                whole = rows_f[part, :]
            elif kind == 1:
                whole = rows_b[0, 0, part, :]
            else:
                whole = jnp.where(last, rows_f[part, :], rows_s[0, 0, part, :])
            whole = whole.astype(F32)
            scale = factor_of(whole)
            normed[part, :] = (whole * scale * gain[...]).astype(BF)
            factor[part, :] = jnp.broadcast_to(scale, (32, 128))
        lows = dot_t(normed[...], down[...])
        if kind == 0:
            lows = only(lows, ahead[0])
        elif kind == 1:
            lows = only(lows, back[0])
        low[...] = lows.astype(BF)


def prepare(ahead, back, where, rows, saved, gain, down):
    kinds = [shape((ROWS, WIDTH), BF), shape((ROWS, 128), F32), shape((ROWS, LOWS), BF)]
    return call(
        prepare_kernel,
        (ahead, back, where),
        [rows, saved_of(saved, 0), saved_of(saved, 1), gain, down],
        kinds * 3,
        6 * ROWS * WIDTH * LOWS,
    )


def gained_block(values, lowered, span, gain, down, block):
    return (dot_t(values, block[...]) + dot(lowered, down[:, span])) * gain[:, span]


def input_gradient(where, grad, rows, scale, inner, gained, out):
    inner = inner * (1.0 / WIDTH)
    for i in range(8):
        span = columns(where[i])
        pre = rows(span).astype(F32) * scale
        out[:, span] = (
            grad[:, span].astype(F32) + scale * (gained(i) - pre * inner)
        ).astype(BF)


def near_kernel(back, where, grad, normed, rows, factor, gain, down, up, *refs):
    outs, vals, (d_values, d_low, kept, inner, share) = refs[:8], refs[8:14], refs[14:]
    total = jnp.zeros((ROWS, VALUES), F32)
    for i in range(8):
        total += dot_t(grad[:, columns(where[i])], outs[i][...])
    values = total.astype(BF)
    lowered = only(SCALE * dot_t(values, up[...]), back[0]).astype(BF)
    d_values[...] = values
    d_low[...] = lowered
    scale = factor[:, :1]
    mean = jnp.zeros((ROWS, 1), F32)
    for i in range(6):
        span = columns(where[i])
        gained = gained_block(values, lowered, span, gain, down, vals[i])
        kept[i] = gained
        mean += jnp.sum(
            gained * (rows[0, 0, :, span].astype(F32) * scale), axis=-1, keepdims=True
        )
    inner[...] = jnp.broadcast_to(mean, (ROWS, 128))
    total = jnp.zeros((ROWS, VALUES), F32)
    for i in range(6):
        total += dot(normed[:, columns(where[i])], vals[i][...])
    share[...] = total


GRADS = [shape((ROWS, VALUES), BF), shape((ROWS, LOWS), BF)]


def near_share(back, where, grad, normed, saved, factor, gain, down, up, outs, vals):
    return call(
        near_kernel,
        (back, where),
        [grad, normed, saved_of(saved, 0), factor, gain, down, up, *outs, *vals],
        [*GRADS, shape((6, ROWS, PART), F32), shape((ROWS, 128), F32), shape((ROWS, VALUES), F32)],
        6 * ROWS * WIDTH * VALUES,
    )


def first_kernel(
    back, where, kept, inner, values, lowered, grad, rows, factor, gain, down, far, far_other, out
):
    scale = factor[:, :1]
    mean = inner[:, :1]
    last = []
    for i, block in ((6, far), (7, far_other)):
        span = columns(where[i])
        gained = gained_block(values[...], lowered[...], span, gain, down, block)
        mean += jnp.sum(
            gained * (rows[0, 0, :, span].astype(F32) * scale), axis=-1, keepdims=True
        )
        last.append(gained)
    input_gradient(
        where, grad, lambda span: rows[0, 0, :, span], scale, mean,
        lambda i: kept[i] if i < 6 else last[i - 6], out,
    )
    out[:, WIDTH:] = jnp.full((ROWS, 128), back[0], jnp.int32).astype(F32).astype(BF)


def first_gradient(back, where, kept, inner, d_values, d_low, grad, saved, factor, gain, down, vals):
    return call(
        first_kernel,
        (back, where),
        [
            kept, inner, d_values, d_low, grad, saved_of(saved, 0), factor, gain, down, *vals[6:]
        ],
        [shape((ROWS, WIDE), BF)],
        ROWS * WIDTH * VALUES,
    )[0]


def output_kernel(ahead, where, share, normed, low, up, rows, far, far_other, *refs):
    blocks, out = refs[:8], refs[8]
    total = share[...] + SCALE * dot(low[...], up[...])
    total += dot(normed[:, columns(where[6])], far[...])
    total += dot(normed[:, columns(where[7])], far_other[...])
    values = total.astype(BF)
    for i in range(8):
        span = columns(where[i])
        out[:, span] = (rows[:, span].astype(F32) + dot(values, blocks[i][...])).astype(BF)
    out[:, WIDTH:] = jnp.full((ROWS, 128), ahead[0], jnp.int32).astype(F32).astype(BF)


def output(ahead, where, share, normed, low, up, rows, outs, vals):
    return call(
        output_kernel,
        (ahead, where),
        [share, normed, low, up, rows, *vals[6:], *outs],
        [shape((ROWS, WIDE), BF)],
        2 * ROWS * WIDTH * VALUES,
    )[0]


def pack_gradients(where, low, normed, d_values, d_low, mine, other):
    up_term = SCALE * t_dot(low, d_values)
    chip, core = where[0] // 2, where[0] % 2
    for ahead in range(4):
        target = lax.rem(chip + ahead, 4)
        pair = up_term[:, 0:128]
        for k in range(1, 4):
            pair = jnp.where(target == k, up_term[:, 128 * k : 128 * (k + 1)], pair)
        pair = pair.astype(BF)
        for ref, c in ((mine, core), (other, 1 - core)):
            ref[ahead, :, :PART] = t_dot(d_low, normed[:, columns(2 * target + c)]).astype(BF)
            ref[ahead, :, PART:] = pair


PACKED = [shape((4, RANK, PACK), BF)] * 2


def pack_kernel(where, low, normed, d_values, d_low, mine, other):
    pack_gradients(
        where, compact(low[...]), normed, d_values[...], compact(d_low[...]), mine, other
    )


def pack(where, low, normed, d_values, d_low):
    return call(
        pack_kernel, (where,), [low, normed, d_values, d_low], PACKED, 2 * ROWS * WIDTH * RANK
    )


def second_kernel(ahead, where, relayed, out, target, low, normed, up, *refs):
    blocks, (grad, d_values, d_low, mine, other) = refs[:8], refs[8:]
    last = where[9] == 1
    total = jnp.zeros((ROWS, VALUES), F32)
    for i in range(8):
        span = columns(where[i])
        loss = (out[:, span].astype(F32) - target[:, span].astype(F32)).astype(BF)
        chosen = jnp.where(last, loss, relayed[:, span])
        grad[:, span] = chosen
        total += dot_t(chosen, blocks[i][...])
    values = total.astype(BF)
    came = relayed[:, WIDTH : WIDTH + 1].astype(F32).astype(jnp.int32)
    ident = jnp.where(last, ahead[0], came)
    lowered = only(SCALE * dot_t(values, up[...]), ident).astype(BF)
    d_values[...] = values
    d_low[...] = lowered
    pack_gradients(
        where, compact(only(low[...], ident)), normed, values, compact(lowered), mine, other
    )


def second_values(ahead, where, relayed, out, target, low, normed, up, blocks):
    return call(
        second_kernel,
        (ahead, where),
        [relayed, out, target, low, normed, up, *blocks],
        [shape((ROWS, WIDTH), BF), *GRADS, *PACKED],
        2 * ROWS * WIDTH * (VALUES + RANK),
    )


def project_kernel(where, normed, *refs):
    blocks, out = refs[:8], refs[8]
    total = jnp.zeros((ROWS, VALUES), F32)
    for i in range(8):
        total += dot(normed[:, columns(where[i])], blocks[i][...])
    out[...] = total


def project(where, normed, vals):
    return call(
        project_kernel, (where,), [normed, *vals], [shape((ROWS, VALUES), F32)],
        2 * ROWS * WIDTH * VALUES,
    )[0]


def second_input_kernel(
    where, sums, low, grad, rows_f, rows_s, factor, gain, down, d_values, d_low, *refs
):
    blocks, out = refs[:8], refs[8]
    last = where[9] == 1
    scale = factor[:, :1]
    values, lowered = d_values[...], d_low[...]
    inner = jnp.sum(values.astype(F32) * sums[...], axis=-1, keepdims=True)
    inner += jnp.sum(lowered.astype(F32) * low[...].astype(F32), axis=-1, keepdims=True)
    weight = scale * scale * inner * (1.0 / WIDTH)
    for i in range(8):
        span = columns(where[i])
        rows = jnp.where(last, rows_f[:, span], rows_s[0, 0, :, span]).astype(F32)
        gained = gained_block(values, lowered, span, gain, down, blocks[i])
        out[:, span] = (grad[:, span].astype(F32) + scale * gained - weight * rows).astype(BF)


def second_input(where, sums, low, grad, rows, saved, factor, gain, down, d_values, d_low, blocks):
    return call(
        second_input_kernel,
        (where,),
        [
            sums, low, grad, rows, saved_of(saved, 1), factor, gain, down, d_values, d_low, *blocks
        ],
        [shape((ROWS, WIDTH), BF)],
        2 * ROWS * WIDTH * (VALUES + RANK),
    )[0]


def forward_kernel(wrapped, where, fresh, passed, gain, down, up, *refs):
    vals, outs, (out, rows, normed) = refs[:8], refs[8:16], refs[16:]
    first = where[8] == 1
    for top in range(0, ROWS, 32):
        part = slice(top, top + 32)
        chosen = jnp.where(first, fresh[part, :], passed[part, :WIDTH])
        whole = chosen.astype(F32)
        rows[part, :] = chosen
        normed[part, :] = (whole * factor_of(whole) * gain[...]).astype(BF)
    came = passed[:, WIDTH : WIDTH + 1].astype(F32).astype(jnp.int32)
    ident = jnp.where(first, wrapped[0], came)
    low = only(dot_t(normed[...], down[...]), ident).astype(BF)
    total = SCALE * dot(low, up[...])
    for i in range(8):
        total += dot(normed[:, columns(where[i])], vals[i][...])
    values = total.astype(BF)
    for i in range(8):
        span = columns(where[i])
        out[:, span] = (rows[:, span].astype(F32) + dot(values, outs[i][...])).astype(BF)


def forward(wrapped, where, fresh, passed, gain, down, up, vals, outs):
    return call(
        forward_kernel,
        (wrapped, where),
        [fresh, passed, gain, down, up, *vals, *outs],
        [shape((ROWS, WIDTH), BF)],
        4 * ROWS * WIDTH * VALUES,
        [pltpu.VMEM((ROWS, WIDTH), BF), pltpu.VMEM((ROWS, WIDTH), BF)],
    )[0]


def pair_sum_kernel(mine, other, total):
    total[...] = (mine[...].astype(F32) + other[...].astype(F32)).astype(BF)


def pair_sum(mine, other):
    return call(pair_sum_kernel, (), [mine, other], [shape((4, RANK, PACK), BF)], 0)[0]


def stack_kernel(first, mine, other, own, one, two, three):
    for ahead, ref in enumerate((own, one, two, three)):
        ref[0] = first[ahead]
        ref[1] = (mine[ahead].astype(F32) + other[ahead].astype(F32)).astype(BF)


def spread(first, mine, received):
    block = shape((2, RANK, PACK), BF)
    own, one, two, three = call(stack_kernel, (), [first, mine, received], [block] * 4, 0)
    return (
        own,
        lax.ppermute(two, "dp", chips(2)),
        lax.ppermute(one, "dp", chips(1)),
        lax.ppermute(three, "dp", chips(3)),
    )


def tables_kernel(ahead, back, where, relayed, *refs):
    terms, (down, up) = refs[:4], refs[4:]
    core = where[0] % 2
    came = relayed[:RANK, :1].astype(F32).astype(jnp.int32)
    ident = jnp.where(where[9] == 1, ahead[0], came)
    sums = []
    for tick in range(2):
        total = terms[0][tick].astype(F32)
        for k in range(1, 4):
            total += terms[k][tick].astype(F32)
        sums.append(total)
    for label in range(ADAPTERS):
        one = jnp.where(back[0] == label, 1.0, 0.0)
        two = jnp.where(ident == label, 1.0, 0.0)
        total = one * sums[0] + two * sums[1]
        down[label] = total[:, :PART]
        up[label] = jnp.where(core == 0, total[:, PART : PART + 64], total[:, PART + 64 :])


def tables(ahead, back, where, relayed, terms):
    tail = (relayed, (ROWS, 128), lambda i, *s: (0, WIDTH // 128))
    return call(
        tables_kernel,
        (ahead, back, where),
        [tail, *terms],
        [shape((ADAPTERS, RANK, PART), F32), shape((ADAPTERS, RANK, 64), F32)],
        0,
    )


CORE = [(i, i ^ 1) for i in range(8)]


def chips(by):
    return [(i, ((i // 2 + by) % 4) * 2 + i % 2) for i in range(8)]


def split_ring(sign):
    return [(i, ((i // 2 + (sign if i % 2 == 0 else -sign)) % 4) * 2 + i % 2) for i in range(8)]


def send(block, pairs):
    return lax.ppermute(block, "dp", pairs)


def block_index():
    place = lax.axis_index("dp")
    chip, core = place // 2, place % 2
    other = 1 - core
    step = jnp.where(core == 0, 1, -1)
    block = lambda k, c: 2 * (k % 4) + c
    return [
        block(chip, core), block(chip, other),
        block(chip - step + 4, core), block(chip + step + 4, other),
        block(chip + step + 4, core), block(chip - step + 4, other),
        block(chip + 2, core), block(chip + 2, other),
    ]


def body(
    forward_state, backward_state, saved, fresh, target, forward_adapter, backward_adapter,
    value_projection, output_matrix, norm_gain_frozen, adapter_down, adapter_up,
):
    count = lax.axis_size("section")
    onward = [(i, i + 1) for i in range(count - 1)]
    before = [(i, i - 1) for i in range(1, count)]
    position = lax.axis_index("section")
    where = jnp.stack(
        [v.astype(jnp.int32) for v in (*block_index(), position == 0, position == count - 1)]
    )
    gain = norm_gain_frozen
    down = jnp.swapaxes(adapter_down[0], 1, 2).reshape(LOWS, WIDTH)
    up = adapter_up[0].reshape(LOWS, VALUES)
    rows, grad = forward_state[0], backward_state[0]
    ahead, back = forward_adapter, backward_adapter

    out_own, val_own = output_matrix[0], value_projection[0]
    out_near, out_away = send(out_own, split_ring(1)), send(out_own, split_ring(-1))
    val_near, val_away = send(val_own, split_ring(1)), send(val_own, split_ring(-1))
    out_sibling, val_sibling = send(out_own, CORE), send(val_own, CORE)

    normed_f, _, low_f, normed_b, factor_b, low_b, normed_n, factor_n, low_n = prepare(
        ahead, back, where, rows, saved, gain, down
    )
    out_near, out_away, normed_f, out_sibling, val_sibling = lax.optimization_barrier(
        (out_near, out_away, normed_f, out_sibling, val_sibling)
    )
    out_far, val_far = send(out_near, split_ring(1)), send(val_near, split_ring(1))
    outs = [
        out_own, out_sibling, out_near, send(out_near, CORE), out_away, send(out_away, CORE)
    ]
    vals = [
        val_own, val_sibling, val_near, send(val_near, CORE), val_away, send(val_away, CORE)
    ]
    outs += [out_far, send(out_far, CORE)]
    d_values, d_low, kept, inner, share_f = near_share(
        back, where, grad, normed_f, saved, factor_b, gain, down, up, outs, vals
    )
    mine, other = pack(where, low_b, normed_b, d_values, d_low)
    first_sums = pair_sum(mine, send(other, CORE))
    val_far, first_sums = lax.optimization_barrier((val_far, first_sums))
    vals += [val_far, send(val_far, CORE)]

    first_back = first_gradient(
        back, where, kept, inner, d_values, d_low, grad, saved, factor_b, gain, down, vals
    )
    relayed = lax.ppermute(first_back, "section", before)
    share_f, first_back = lax.optimization_barrier((share_f, first_back))
    first_out = output(ahead, where, share_f, normed_f, low_f, up, rows, outs, vals)
    passed = lax.ppermute(first_out, "section", onward)
    first_out, sent, normed_n = lax.optimization_barrier((first_out, ahead, normed_n))
    wrapped = lax.ppermute(sent, "section", [(count - 1, 0)])
    sums_n = project(where, normed_n, vals)
    relayed, sums_n, wrapped = lax.optimization_barrier((relayed, sums_n, wrapped))

    grad_n, d_values, d_low, mine, other = second_values(
        ahead, where, relayed, first_out, target, low_n, normed_n, up, outs
    )
    terms = spread(first_sums, mine, send(other, CORE))
    bwd_out = second_input(
        where, sums_n, low_n, grad_n, rows, saved, factor_n, gain, down, d_values, d_low, vals
    )
    fwd_out = forward(wrapped, where, fresh, passed, gain, down, up, vals, outs)
    down_table, up_table = tables(ahead, back, where, relayed, terms)
    return (
        fwd_out[None], bwd_out[None], jnp.swapaxes(down_table, 1, 2)[None], up_table[None]
    )


def solution(mesh):
    return jax.shard_map(
        body,
        mesh=mesh,
        in_specs=(
            P("section", "dp", None),
            P("section", "dp", None),
            P("section", None, "dp", None),
            P("dp", None),
            P("dp", None),
            P("section"),
            P("section"),
            P("section", "dp", None),
            P("section", None, "dp"),
            P("section", None),
            P("section", None, None, None),
            P("section", None, None, None),
        ),
        out_specs=(
            P("section", "dp", None),
            P("section", "dp", None),
            P("section", None, "dp", None),
            P("section", None, None, "dp"),
        ),
        check_vma=False,
    )
```

```python
import jax
import jax.numpy as jnp
from jax import lax
from jax.experimental import pallas as pl
from jax.experimental.pallas import tpu as pltpu
from jax.sharding import PartitionSpec as P

SCALE = 0.5
EPS = 1e-05
BF = jnp.bfloat16
F32 = jnp.float32
ROWS = 128
WIDTH = 4096
VALUES = 512
PART = 512
RANK = 64
ADAPTERS = 4
PACK = PART + 128
LOWS = 256
WIDE = WIDTH + 128
VMEM = 20 * 1024 * 1024
ONCE = pl.Buffered(1)


def dot(left, right, dims=((1,), (0,))):
    return lax.dot_general(left, right, (dims, ((), ())), preferred_element_type=F32)


def dot_t(left, right):
    return dot(left, right, ((1,), (1,)))


def t_dot(left, right):
    return dot(left, right, ((0,), (0,)))


def call(kernel, scalars, ins, outs, flops, scratch=()):
    specs, arrays = [], []
    for item in ins:
        array, block, index = item if isinstance(item, tuple) else (item, None, None)
        arrays.append(array)
        if block is None:
            zeros = (0,) * array.ndim
            specs.append(pl.BlockSpec(array.shape, lambda i, *s, z=zeros: z, pipeline_mode=ONCE))
        else:
            specs.append(pl.BlockSpec(block, index, pipeline_mode=ONCE))
    out_specs = [
        pl.BlockSpec(o.shape, lambda i, *s, z=(0,) * len(o.shape): z, pipeline_mode=ONCE)
        for o in outs
    ]
    size = sum(a.size * a.dtype.itemsize for a in arrays)
    return pl.pallas_call(
        kernel,
        out_shape=outs,
        grid_spec=pltpu.PrefetchScalarGridSpec(
            num_scalar_prefetch=len(scalars),
            grid=(1,),
            in_specs=specs,
            out_specs=out_specs,
            scratch_shapes=list(scratch),
        ),
        compiler_params=pltpu.CompilerParams(vmem_limit_bytes=VMEM),
        cost_estimate=pl.CostEstimate(
            flops=flops // 1000, bytes_accessed=size // 1000, transcendentals=0
        ),
    )(*scalars, *arrays)


def shape(dims, dtype):
    return jax.ShapeDtypeStruct(dims, dtype)


def factor_of(rows):
    return lax.rsqrt(jnp.sum(rows * rows, axis=-1, keepdims=True) * (1.0 / WIDTH) + EPS)


def columns(index):
    return pl.ds(pl.multiple_of(index * PART, PART), PART)


def only(lows, ident):
    lane = lax.broadcasted_iota(jnp.int32, lows.shape, 1)
    return jnp.where(lane // RANK == ident, lows, jnp.zeros_like(lows))


def compact(lows):
    total = lows[:, :RANK].astype(F32)
    for k in range(1, ADAPTERS):
        total += lows[:, k * RANK : (k + 1) * RANK].astype(F32)
    return total.astype(BF)


def saved_of(saved, which):
    return (saved, (1, 1, ROWS, WIDTH), lambda i, *s: (0, which, 0, 0))


def prepare_kernel(ahead, back, where, rows_f, rows_b, rows_s, gain, down, *refs):
    last = where[9] == 1
    for kind in range(3):
        normed, factor, low = refs[3 * kind : 3 * kind + 3]
        for top in range(0, ROWS, 32):
            part = slice(top, top + 32)
            if kind == 0:
                whole = rows_f[part, :]
            elif kind == 1:
                whole = rows_b[0, 0, part, :]
            else:
                whole = jnp.where(last, rows_f[part, :], rows_s[0, 0, part, :])
            whole = whole.astype(F32)
            scale = factor_of(whole)
            normed[part, :] = (whole * scale * gain[...]).astype(BF)
            factor[part, :] = jnp.broadcast_to(scale, (32, 128))
        lows = dot_t(normed[...], down[...])
        if kind == 0:
            lows = only(lows, ahead[0])
        elif kind == 1:
            lows = only(lows, back[0])
        low[...] = lows.astype(BF)


def prepare(ahead, back, where, rows, saved, gain, down):
    kinds = [shape((ROWS, WIDTH), BF), shape((ROWS, 128), F32), shape((ROWS, LOWS), BF)]
    return call(
        prepare_kernel,
        (ahead, back, where),
        [rows, saved_of(saved, 0), saved_of(saved, 1), gain, down],
        kinds * 3,
        6 * ROWS * WIDTH * LOWS,
    )


def gained_block(values, lowered, span, gain, down, block):
    return (dot_t(values, block[...]) + dot(lowered, down[:, span])) * gain[:, span]


def input_gradient(where, grad, rows, scale, inner, gained, out):
    inner = inner * (1.0 / WIDTH)
    for i in range(8):
        span = columns(where[i])
        pre = rows(span).astype(F32) * scale
        out[:, span] = (
            grad[:, span].astype(F32) + scale * (gained(i) - pre * inner)
        ).astype(BF)


def near_kernel(back, where, grad, normed, rows, factor, gain, down, up, *refs):
    outs, vals, (d_values, d_low, kept, inner, share) = refs[:8], refs[8:14], refs[14:]
    total = jnp.zeros((ROWS, VALUES), F32)
    for i in range(8):
        total += dot_t(grad[:, columns(where[i])], outs[i][...])
    values = total.astype(BF)
    lowered = only(SCALE * dot_t(values, up[...]), back[0]).astype(BF)
    d_values[...] = values
    d_low[...] = lowered
    scale = factor[:, :1]
    mean = jnp.zeros((ROWS, 1), F32)
    for i in range(6):
        span = columns(where[i])
        gained = gained_block(values, lowered, span, gain, down, vals[i])
        kept[i] = gained
        mean += jnp.sum(
            gained * (rows[0, 0, :, span].astype(F32) * scale), axis=-1, keepdims=True
        )
    inner[...] = jnp.broadcast_to(mean, (ROWS, 128))
    total = jnp.zeros((ROWS, VALUES), F32)
    for i in range(6):
        total += dot(normed[:, columns(where[i])], vals[i][...])
    share[...] = total


GRADS = [shape((ROWS, VALUES), BF), shape((ROWS, LOWS), BF)]


def near_share(back, where, grad, normed, saved, factor, gain, down, up, outs, vals):
    return call(
        near_kernel,
        (back, where),
        [grad, normed, saved_of(saved, 0), factor, gain, down, up, *outs, *vals],
        [*GRADS, shape((6, ROWS, PART), F32), shape((ROWS, 128), F32), shape((ROWS, VALUES), F32)],
        6 * ROWS * WIDTH * VALUES,
    )


def first_kernel(
    back, where, kept, inner, values, lowered, grad, rows, factor, gain, down, far, far_other, out
):
    scale = factor[:, :1]
    mean = inner[:, :1]
    last = []
    for i, block in ((6, far), (7, far_other)):
        span = columns(where[i])
        gained = gained_block(values[...], lowered[...], span, gain, down, block)
        mean += jnp.sum(
            gained * (rows[0, 0, :, span].astype(F32) * scale), axis=-1, keepdims=True
        )
        last.append(gained)
    input_gradient(
        where, grad, lambda span: rows[0, 0, :, span], scale, mean,
        lambda i: kept[i] if i < 6 else last[i - 6], out,
    )
    out[:, WIDTH:] = jnp.full((ROWS, 128), back[0], jnp.int32).astype(F32).astype(BF)


def first_gradient(back, where, kept, inner, d_values, d_low, grad, saved, factor, gain, down, vals):
    return call(
        first_kernel,
        (back, where),
        [
            kept, inner, d_values, d_low, grad, saved_of(saved, 0), factor, gain, down, *vals[6:]
        ],
        [shape((ROWS, WIDE), BF)],
        ROWS * WIDTH * VALUES,
    )[0]


def output_kernel(ahead, where, share, normed, low, up, rows, far, far_other, *refs):
    blocks, out = refs[:8], refs[8]
    total = share[...] + SCALE * dot(low[...], up[...])
    total += dot(normed[:, columns(where[6])], far[...])
    total += dot(normed[:, columns(where[7])], far_other[...])
    values = total.astype(BF)
    for i in range(8):
        span = columns(where[i])
        out[:, span] = (rows[:, span].astype(F32) + dot(values, blocks[i][...])).astype(BF)
    out[:, WIDTH:] = jnp.full((ROWS, 128), ahead[0], jnp.int32).astype(F32).astype(BF)


def output(ahead, where, share, normed, low, up, rows, outs, vals):
    return call(
        output_kernel,
        (ahead, where),
        [share, normed, low, up, rows, *vals[6:], *outs],
        [shape((ROWS, WIDE), BF)],
        2 * ROWS * WIDTH * VALUES,
    )[0]


def pack_gradients(where, low, normed, d_values, d_low, core, ref):
    up_term = SCALE * t_dot(low, d_values)
    chip = where[0] // 2
    for ahead in range(4):
        target = lax.rem(chip + ahead, 4)
        pair = up_term[:, 0:128]
        for k in range(1, 4):
            pair = jnp.where(target == k, up_term[:, 128 * k : 128 * (k + 1)], pair)
        ref[ahead, :, :PART] = t_dot(d_low, normed[:, columns(2 * target + core)]).astype(BF)
        ref[ahead, :, PART:] = pair.astype(BF)


PACKED = [shape((4, RANK, PACK), BF)]


def pack(where, low, normed, d_values, d_low, other):
    def kernel(where, low, normed, d_values, d_low, ref):
        core = 1 - where[0] % 2 if other else where[0] % 2
        pack_gradients(
            where, compact(low[...]), normed, d_values[...], compact(d_low[...]), core, ref
        )

    return call(
        kernel, (where,), [low, normed, d_values, d_low], PACKED, ROWS * WIDTH * RANK
    )[0]


def second_kernel(ahead, where, relayed, out, target, low, normed, up, *refs):
    blocks, (grad, d_values, d_low, chosen_low, other) = refs[:8], refs[8:]
    last = where[9] == 1
    total = jnp.zeros((ROWS, VALUES), F32)
    for i in range(8):
        span = columns(where[i])
        loss = (out[:, span].astype(F32) - target[:, span].astype(F32)).astype(BF)
        chosen = jnp.where(last, loss, relayed[:, span])
        grad[:, span] = chosen
        total += dot_t(chosen, blocks[i][...])
    values = total.astype(BF)
    came = relayed[:, WIDTH : WIDTH + 1].astype(F32).astype(jnp.int32)
    ident = jnp.where(last, ahead[0], came)
    lowered = only(SCALE * dot_t(values, up[...]), ident).astype(BF)
    d_values[...] = values
    d_low[...] = lowered
    chosen = only(low[...], ident)
    chosen_low[...] = chosen
    pack_gradients(
        where, compact(chosen), normed, values, compact(lowered), 1 - where[0] % 2, other
    )


def second_values(ahead, where, relayed, out, target, low, normed, up, blocks):
    return call(
        second_kernel,
        (ahead, where),
        [relayed, out, target, low, normed, up, *blocks],
        [shape((ROWS, WIDTH), BF), *GRADS, shape((ROWS, LOWS), BF), *PACKED],
        2 * ROWS * WIDTH * (VALUES + RANK),
    )


def project_kernel(where, normed, *refs):
    blocks, out = refs[:8], refs[8]
    total = jnp.zeros((ROWS, VALUES), F32)
    for i in range(8):
        total += dot(normed[:, columns(where[i])], blocks[i][...])
    out[...] = total


def project(where, normed, vals):
    return call(
        project_kernel, (where,), [normed, *vals], [shape((ROWS, VALUES), F32)],
        2 * ROWS * WIDTH * VALUES,
    )[0]


def second_input_kernel(
    where, sums, low, grad, rows_f, rows_s, factor, gain, down, d_values, d_low, *refs
):
    blocks, out = refs[:8], refs[8]
    last = where[9] == 1
    scale = factor[:, :1]
    values, lowered = d_values[...], d_low[...]
    inner = jnp.sum(values.astype(F32) * sums[...], axis=-1, keepdims=True)
    inner += jnp.sum(lowered.astype(F32) * low[...].astype(F32), axis=-1, keepdims=True)
    weight = scale * scale * inner * (1.0 / WIDTH)
    for i in range(8):
        span = columns(where[i])
        rows = jnp.where(last, rows_f[:, span], rows_s[0, 0, :, span]).astype(F32)
        gained = gained_block(values, lowered, span, gain, down, blocks[i])
        out[:, span] = (grad[:, span].astype(F32) + scale * gained - weight * rows).astype(BF)


def second_input(where, sums, low, grad, rows, saved, factor, gain, down, d_values, d_low, blocks):
    return call(
        second_input_kernel,
        (where,),
        [
            sums, low, grad, rows, saved_of(saved, 1), factor, gain, down, d_values, d_low, *blocks
        ],
        [shape((ROWS, WIDTH), BF)],
        2 * ROWS * WIDTH * (VALUES + RANK),
    )[0]


def forward_kernel(where, fresh, passed, gain, down, up, *refs):
    vals, outs, (out, rows, normed) = refs[:8], refs[8:16], refs[16:]
    first = where[8] == 1
    for top in range(0, ROWS, 32):
        part = slice(top, top + 32)
        chosen = jnp.where(first, fresh[part, :], passed[part, :WIDTH])
        whole = chosen.astype(F32)
        rows[part, :] = chosen
        normed[part, :] = (whole * factor_of(whole) * gain[...]).astype(BF)
    ident = passed[:, WIDTH : WIDTH + 1].astype(F32).astype(jnp.int32)
    low = only(dot_t(normed[...], down[...]), ident).astype(BF)
    total = SCALE * dot(low, up[...])
    for i in range(8):
        total += dot(normed[:, columns(where[i])], vals[i][...])
    values = total.astype(BF)
    for i in range(8):
        span = columns(where[i])
        out[:, span] = (rows[:, span].astype(F32) + dot(values, outs[i][...])).astype(BF)


def forward(where, fresh, passed, gain, down, up, vals, outs):
    return call(
        forward_kernel,
        (where,),
        [fresh, passed, gain, down, up, *vals, *outs],
        [shape((ROWS, WIDTH), BF)],
        4 * ROWS * WIDTH * VALUES,
        [pltpu.VMEM((ROWS, WIDTH), BF), pltpu.VMEM((ROWS, WIDTH), BF)],
    )[0]


def pair_sum_kernel(mine, other, total):
    total[...] = (mine[...].astype(F32) + other[...].astype(F32)).astype(BF)


def pair_sum(mine, other):
    return call(pair_sum_kernel, (), [mine, other], [shape((4, RANK, PACK), BF)], 0)[0]


def stack_kernel(where, first, mine, other, own, one, two, three):
    core = where[0] % 2
    for ahead, ref in enumerate((own, one, two, three)):
        sums = (mine[ahead].astype(F32) + other[ahead].astype(F32)).astype(BF)
        ref[:, :PART] = first[ahead, :, :PART]
        ref[:, PART : 2 * PART] = sums[:, :PART]
        ups = [
            jnp.where(core == 0, pair[:, : RANK].astype(F32), pair[:, RANK:].astype(F32))
            for pair in (first[ahead, :, PART:], sums[:, PART:])
        ]
        ref[:, 2 * PART :] = jnp.concatenate(ups, axis=1).astype(BF)


def spread(where, first, mine, received):
    block = shape((RANK, 2 * PART + 128), BF)
    own, one, two, three = call(
        stack_kernel, (where,), [first, mine, received], [block] * 4, 0
    )
    return (
        own,
        lax.ppermute(two, "dp", chips(2)),
        lax.ppermute(one, "dp", chips(1)),
        lax.ppermute(three, "dp", chips(3)),
    )


def tables_kernel(ahead, back, where, relayed, *refs):
    terms, (down, up) = refs[:4], refs[4:]
    came = relayed[:RANK, :1].astype(F32).astype(jnp.int32)
    ident = jnp.where(where[9] == 1, ahead[0], came)
    total = terms[0][...].astype(F32)
    for k in range(1, 4):
        total += terms[k][...].astype(F32)
    end = 2 * PART
    for label in range(ADAPTERS):
        one = jnp.where(back[0] == label, 1.0, 0.0)
        two = jnp.where(ident == label, 1.0, 0.0)
        down[label] = one * total[:, :PART] + two * total[:, PART:end]
        up[label] = one * total[:, end : end + RANK] + two * total[:, end + RANK :]


def tables(ahead, back, where, relayed, terms):
    tail = (relayed, (ROWS, 128), lambda i, *s: (0, WIDTH // 128))
    return call(
        tables_kernel,
        (ahead, back, where),
        [tail, *terms],
        [shape((ADAPTERS, RANK, PART), F32), shape((ADAPTERS, RANK, 64), F32)],
        0,
    )


CORE = [(i, i ^ 1) for i in range(8)]


def chips(by):
    return [(i, ((i // 2 + by) % 4) * 2 + i % 2) for i in range(8)]


def split_ring(sign):
    return [(i, ((i // 2 + (sign if i % 2 == 0 else -sign)) % 4) * 2 + i % 2) for i in range(8)]


def send(block, pairs):
    return lax.ppermute(block, "dp", pairs)


def block_index():
    place = lax.axis_index("dp")
    chip, core = place // 2, place % 2
    other = 1 - core
    step = jnp.where(core == 0, 1, -1)
    block = lambda k, c: 2 * (k % 4) + c
    return [
        block(chip, core), block(chip, other),
        block(chip - step + 4, core), block(chip + step + 4, other),
        block(chip + step + 4, core), block(chip - step + 4, other),
        block(chip + 2, core), block(chip + 2, other),
    ]


def body(
    forward_state, backward_state, saved, fresh, target, forward_adapter, backward_adapter,
    value_projection, output_matrix, norm_gain_frozen, adapter_down, adapter_up,
):
    count = lax.axis_size("section")
    onward = [(i, (i + 1) % count) for i in range(count)]
    before = [(i, i - 1) for i in range(1, count)]
    position = lax.axis_index("section")
    where = jnp.stack(
        [v.astype(jnp.int32) for v in (*block_index(), position == 0, position == count - 1)]
    )
    gain = norm_gain_frozen
    down = jnp.swapaxes(adapter_down[0], 1, 2).reshape(LOWS, WIDTH)
    up = adapter_up[0].reshape(LOWS, VALUES)
    rows, grad = forward_state[0], backward_state[0]
    ahead, back = forward_adapter, backward_adapter

    out_own, val_own = output_matrix[0], value_projection[0]
    out_near, out_away = send(out_own, split_ring(1)), send(out_own, split_ring(-1))
    val_near, val_away = send(val_own, split_ring(1)), send(val_own, split_ring(-1))
    out_sibling, val_sibling = send(out_own, CORE), send(val_own, CORE)

    normed_f, _, low_f, normed_b, factor_b, low_b, normed_n, factor_n, low_n = prepare(
        ahead, back, where, rows, saved, gain, down
    )
    out_near, out_away, normed_f, out_sibling, val_sibling = lax.optimization_barrier(
        (out_near, out_away, normed_f, out_sibling, val_sibling)
    )
    out_far, val_far = send(out_near, split_ring(1)), send(val_near, split_ring(1))
    outs = [
        out_own, out_sibling, out_near, send(out_near, CORE), out_away, send(out_away, CORE)
    ]
    vals = [
        val_own, val_sibling, val_near, send(val_near, CORE), val_away, send(val_away, CORE)
    ]
    outs += [out_far, send(out_far, CORE)]
    d_values, d_low, kept, inner, share_f = near_share(
        back, where, grad, normed_f, saved, factor_b, gain, down, up, outs, vals
    )
    other = pack(where, low_b, normed_b, d_values, d_low, True)
    mine = pack(where, low_b, normed_b, d_values, d_low, False)
    first_sums = pair_sum(mine, send(other, CORE))
    val_far, first_sums = lax.optimization_barrier((val_far, first_sums))
    vals += [val_far, send(val_far, CORE)]

    first_back = first_gradient(
        back, where, kept, inner, d_values, d_low, grad, saved, factor_b, gain, down, vals
    )
    relayed = lax.ppermute(first_back, "section", before)
    share_f, first_back = lax.optimization_barrier((share_f, first_back))
    first_out = output(ahead, where, share_f, normed_f, low_f, up, rows, outs, vals)
    passed = lax.ppermute(first_out, "section", onward)
    first_out, normed_n = lax.optimization_barrier((first_out, normed_n))
    sums_n = project(where, normed_n, vals)
    relayed, sums_n = lax.optimization_barrier((relayed, sums_n))

    grad_n, d_values, d_low, chosen_low, other = second_values(
        ahead, where, relayed, first_out, target, low_n, normed_n, up, outs
    )
    received = send(other, CORE)
    mine = pack(where, chosen_low, normed_n, d_values, d_low, False)
    terms = spread(where, first_sums, mine, received)
    bwd_out = second_input(
        where, sums_n, low_n, grad_n, rows, saved, factor_n, gain, down, d_values, d_low, vals
    )
    fwd_out = forward(where, fresh, passed, gain, down, up, vals, outs)
    down_table, up_table = tables(ahead, back, where, relayed, terms)
    return (
        fwd_out[None], bwd_out[None], jnp.swapaxes(down_table, 1, 2)[None], up_table[None]
    )


def solution(mesh):
    return jax.shard_map(
        body,
        mesh=mesh,
        in_specs=(
            P("section", "dp", None),
            P("section", "dp", None),
            P("section", None, "dp", None),
            P("dp", None),
            P("dp", None),
            P("section"),
            P("section"),
            P("section", "dp", None),
            P("section", None, "dp"),
            P("section", None),
            P("section", None, None, None),
            P("section", None, None, None),
        ),
        out_specs=(
            P("section", "dp", None),
            P("section", "dp", None),
            P("section", None, "dp", None),
            P("section", None, None, "dp"),
        ),
        check_vma=False,
    )
```

```python
import jax
import jax.numpy as jnp
from jax import lax
from jax.experimental import pallas as pl
from jax.experimental.pallas import tpu as pltpu
from jax.sharding import PartitionSpec as P

SCALE = 0.5
EPS = 1e-05
BF = jnp.bfloat16
F32 = jnp.float32
ROWS = 128
WIDTH = 4096
VALUES = 512
PART = 512
RANK = 64
ADAPTERS = 4
PACK = PART + 128
LOWS = 256
WIDE = WIDTH + 128
VMEM = 20 * 1024 * 1024
ONCE = pl.Buffered(1)


def dot(left, right, dims=((1,), (0,))):
    return lax.dot_general(left, right, (dims, ((), ())), preferred_element_type=F32)


def dot_t(left, right):
    return dot(left, right, ((1,), (1,)))


def t_dot(left, right):
    return dot(left, right, ((0,), (0,)))


def call(kernel, scalars, ins, outs, flops, scratch=()):
    specs, arrays = [], []
    for item in ins:
        array, block, index = item if isinstance(item, tuple) else (item, None, None)
        arrays.append(array)
        if block is None:
            zeros = (0,) * array.ndim
            specs.append(pl.BlockSpec(array.shape, lambda i, *s, z=zeros: z, pipeline_mode=ONCE))
        else:
            specs.append(pl.BlockSpec(block, index, pipeline_mode=ONCE))
    out_specs = [
        pl.BlockSpec(o.shape, lambda i, *s, z=(0,) * len(o.shape): z, pipeline_mode=ONCE)
        for o in outs
    ]
    size = sum(a.size * a.dtype.itemsize for a in arrays)
    return pl.pallas_call(
        kernel,
        out_shape=outs,
        grid_spec=pltpu.PrefetchScalarGridSpec(
            num_scalar_prefetch=len(scalars),
            grid=(1,),
            in_specs=specs,
            out_specs=out_specs,
            scratch_shapes=list(scratch),
        ),
        compiler_params=pltpu.CompilerParams(vmem_limit_bytes=VMEM),
        cost_estimate=pl.CostEstimate(
            flops=flops // 1000, bytes_accessed=size // 1000, transcendentals=0
        ),
    )(*scalars, *arrays)


def shape(dims, dtype):
    return jax.ShapeDtypeStruct(dims, dtype)


def factor_of(rows):
    return lax.rsqrt(jnp.sum(rows * rows, axis=-1, keepdims=True) * (1.0 / WIDTH) + EPS)


def columns(index):
    return pl.ds(pl.multiple_of(index * PART, PART), PART)


def only(lows, ident):
    lane = lax.broadcasted_iota(jnp.int32, lows.shape, 1)
    return jnp.where(lane // RANK == ident, lows, jnp.zeros_like(lows))


def compact(lows):
    total = lows[:, :RANK].astype(F32)
    for k in range(1, ADAPTERS):
        total += lows[:, k * RANK : (k + 1) * RANK].astype(F32)
    return total.astype(BF)


def saved_of(saved, which):
    return (saved, (1, 1, ROWS, WIDTH), lambda i, *s: (0, which, 0, 0))


def prepare_kernel(ahead, back, where, rows_f, rows_b, rows_s, gain, down, *refs):
    last = where[9] == 1
    for kind in range(3):
        normed, factor, low = refs[3 * kind : 3 * kind + 3]
        for top in range(0, ROWS, 32):
            part = slice(top, top + 32)
            if kind == 0:
                whole = rows_f[part, :]
            elif kind == 1:
                whole = rows_b[0, 0, part, :]
            else:
                whole = jnp.where(last, rows_f[part, :], rows_s[0, 0, part, :])
                refs[9][part, :] = whole
            whole = whole.astype(F32)
            scale = factor_of(whole)
            normed[part, :] = (whole * scale * gain[...]).astype(BF)
            factor[part, :] = jnp.broadcast_to(scale, (32, 128))
        lows = dot_t(normed[...], down[...])
        if kind == 0:
            lows = only(lows, ahead[0])
        elif kind == 1:
            lows = only(lows, back[0])
        low[...] = lows.astype(BF)


def prepare(ahead, back, where, rows, saved, gain, down):
    kinds = [shape((ROWS, WIDTH), BF), shape((ROWS, 128), F32), shape((ROWS, LOWS), BF)]
    return call(
        prepare_kernel,
        (ahead, back, where),
        [rows, saved_of(saved, 0), saved_of(saved, 1), gain, down],
        [*kinds * 3, shape((ROWS, WIDTH), BF)],
        6 * ROWS * WIDTH * LOWS,
    )


def gained_block(values, lowered, span, gain, down, block):
    return (dot_t(values, block[...]) + dot(lowered, down[:, span])) * gain[:, span]


def input_gradient(where, grad, rows, scale, inner, gained, out):
    inner = inner * (1.0 / WIDTH)
    for i in range(8):
        span = columns(where[i])
        pre = rows(span).astype(F32) * scale
        out[:, span] = (
            grad[:, span].astype(F32) + scale * (gained(i) - pre * inner)
        ).astype(BF)


def near_kernel(back, where, grad, normed, rows, factor, gain, down, up, *refs):
    outs, vals, (d_values, d_low, kept, inner, share) = refs[:8], refs[8:14], refs[14:]
    total = jnp.zeros((ROWS, VALUES), F32)
    for i in range(8):
        total += dot_t(grad[:, columns(where[i])], outs[i][...])
    values = total.astype(BF)
    lowered = only(SCALE * dot_t(values, up[...]), back[0]).astype(BF)
    d_values[...] = values
    d_low[...] = lowered
    scale = factor[:, :1]
    mean = jnp.zeros((ROWS, 1), F32)
    for i in range(6):
        span = columns(where[i])
        gained = gained_block(values, lowered, span, gain, down, vals[i])
        kept[i] = gained
        mean += jnp.sum(
            gained * (rows[0, 0, :, span].astype(F32) * scale), axis=-1, keepdims=True
        )
    inner[...] = jnp.broadcast_to(mean, (ROWS, 128))
    total = jnp.zeros((ROWS, VALUES), F32)
    for i in range(6):
        total += dot(normed[:, columns(where[i])], vals[i][...])
    share[...] = total


GRADS = [shape((ROWS, VALUES), BF), shape((ROWS, LOWS), BF)]


def near_share(back, where, grad, normed, saved, factor, gain, down, up, outs, vals):
    return call(
        near_kernel,
        (back, where),
        [grad, normed, saved_of(saved, 0), factor, gain, down, up, *outs, *vals],
        [*GRADS, shape((6, ROWS, PART), F32), shape((ROWS, 128), F32), shape((ROWS, VALUES), F32)],
        6 * ROWS * WIDTH * VALUES,
    )


def first_kernel(
    back, where, kept, inner, values, lowered, grad, rows, factor, gain, down, far, far_other, out
):
    scale = factor[:, :1]
    mean = inner[:, :1]
    last = []
    for i, block in ((6, far), (7, far_other)):
        span = columns(where[i])
        gained = gained_block(values[...], lowered[...], span, gain, down, block)
        mean += jnp.sum(
            gained * (rows[0, 0, :, span].astype(F32) * scale), axis=-1, keepdims=True
        )
        last.append(gained)
    input_gradient(
        where, grad, lambda span: rows[0, 0, :, span], scale, mean,
        lambda i: kept[i] if i < 6 else last[i - 6], out,
    )
    out[:, WIDTH:] = jnp.full((ROWS, 128), back[0], jnp.int32).astype(F32).astype(BF)


def first_gradient(back, where, kept, inner, d_values, d_low, grad, saved, factor, gain, down, vals):
    return call(
        first_kernel,
        (back, where),
        [
            kept, inner, d_values, d_low, grad, saved_of(saved, 0), factor, gain, down, *vals[6:]
        ],
        [shape((ROWS, WIDE), BF)],
        ROWS * WIDTH * VALUES,
    )[0]


def output_kernel(ahead, where, share, normed, low, up, rows, far, far_other, *refs):
    blocks, out = refs[:8], refs[8]
    total = share[...] + SCALE * dot(low[...], up[...])
    total += dot(normed[:, columns(where[6])], far[...])
    total += dot(normed[:, columns(where[7])], far_other[...])
    values = total.astype(BF)
    for i in range(8):
        span = columns(where[i])
        out[:, span] = (rows[:, span].astype(F32) + dot(values, blocks[i][...])).astype(BF)
    out[:, WIDTH:] = jnp.full((ROWS, 128), ahead[0], jnp.int32).astype(F32).astype(BF)


def output(ahead, where, share, normed, low, up, rows, outs, vals):
    return call(
        output_kernel,
        (ahead, where),
        [share, normed, low, up, rows, *vals[6:], *outs],
        [shape((ROWS, WIDE), BF)],
        2 * ROWS * WIDTH * VALUES,
    )[0]


def pack_gradients(where, low, normed, d_values, d_low, core, ref):
    up_term = SCALE * t_dot(low, d_values)
    chip = where[0] // 2
    for ahead in range(4):
        target = lax.rem(chip + ahead, 4)
        pair = up_term[:, 0:128]
        for k in range(1, 4):
            pair = jnp.where(target == k, up_term[:, 128 * k : 128 * (k + 1)], pair)
        ref[ahead, :, :PART] = t_dot(d_low, normed[:, columns(2 * target + core)]).astype(BF)
        ref[ahead, :, PART:] = pair.astype(BF)


PACKED = [shape((4, RANK, PACK), BF)]


def pack(where, low, normed, d_values, d_low, other):
    def kernel(where, low, normed, d_values, d_low, ref):
        core = 1 - where[0] % 2 if other else where[0] % 2
        pack_gradients(
            where, compact(low[...]), normed, d_values[...], compact(d_low[...]), core, ref
        )

    return call(
        kernel, (where,), [low, normed, d_values, d_low], PACKED, ROWS * WIDTH * RANK
    )[0]


def second_kernel(ahead, where, relayed, out, target, low, normed, up, *refs):
    blocks, (grad, d_values, d_low, chosen_low, other) = refs[:8], refs[8:]
    last = where[9] == 1
    total = jnp.zeros((ROWS, VALUES), F32)
    for i in range(8):
        span = columns(where[i])
        loss = (out[:, span].astype(F32) - target[:, span].astype(F32)).astype(BF)
        chosen = jnp.where(last, loss, relayed[:, span])
        grad[:, span] = chosen
        total += dot_t(chosen, blocks[i][...])
    values = total.astype(BF)
    came = relayed[:, WIDTH : WIDTH + 1].astype(F32).astype(jnp.int32)
    ident = jnp.where(last, ahead[0], came)
    lowered = only(SCALE * dot_t(values, up[...]), ident).astype(BF)
    d_values[...] = values
    d_low[...] = lowered
    chosen = only(low[...], ident)
    chosen_low[...] = chosen
    pack_gradients(
        where, compact(chosen), normed, values, compact(lowered), 1 - where[0] % 2, other
    )


def second_values(ahead, where, relayed, out, target, low, normed, up, blocks):
    return call(
        second_kernel,
        (ahead, where),
        [relayed, out, target, low, normed, up, *blocks],
        [shape((ROWS, WIDTH), BF), *GRADS, shape((ROWS, LOWS), BF), *PACKED],
        2 * ROWS * WIDTH * (VALUES + RANK),
    )


def project_kernel(where, normed, *refs):
    blocks, out = refs[:8], refs[8]
    total = jnp.zeros((ROWS, VALUES), F32)
    for i in range(8):
        total += dot(normed[:, columns(where[i])], blocks[i][...])
    out[...] = total


def project(where, normed, vals):
    return call(
        project_kernel, (where,), [normed, *vals], [shape((ROWS, VALUES), F32)],
        2 * ROWS * WIDTH * VALUES,
    )[0]


def second_input_kernel(
    where, sums, low, grad, rows, factor, gain, down, d_values, d_low, *refs
):
    blocks, out = refs[:8], refs[8]
    scale = factor[:, :1]
    values, lowered = d_values[...], d_low[...]
    inner = jnp.sum(values.astype(F32) * sums[...], axis=-1, keepdims=True)
    inner += jnp.sum(lowered.astype(F32) * low[...].astype(F32), axis=-1, keepdims=True)
    weight = scale * scale * inner * (1.0 / WIDTH)
    for i in range(8):
        span = columns(where[i])
        gained = gained_block(values, lowered, span, gain, down, blocks[i])
        out[:, span] = (
            grad[:, span].astype(F32) + scale * gained - weight * rows[:, span].astype(F32)
        ).astype(BF)


def second_input(where, sums, low, grad, rows, factor, gain, down, d_values, d_low, blocks):
    return call(
        second_input_kernel,
        (where,),
        [
            sums, low, grad, rows, factor, gain, down, d_values, d_low, *blocks
        ],
        [shape((ROWS, WIDTH), BF)],
        2 * ROWS * WIDTH * (VALUES + RANK),
    )[0]


def forward_kernel(where, fresh, passed, gain, down, up, *refs):
    vals, outs, (out, rows, gained) = refs[:8], refs[8:16], refs[16:]
    first = where[8] == 1
    sums = []
    for top in range(0, ROWS, 32):
        part = slice(top, top + 32)
        total = jnp.zeros((32, 1), F32)
        for left in range(0, WIDTH, PART):
            span = slice(left, left + PART)
            chosen = jnp.where(first, fresh[part, span], passed[part, span])
            whole = chosen.astype(F32)
            rows[part, span] = chosen
            gained[part, span] = (whole * gain[:, span]).astype(BF)
            total += jnp.sum(whole * whole, axis=-1, keepdims=True)
        sums.append(total)
    factor = lax.rsqrt(jnp.concatenate(sums, axis=0) * (1.0 / WIDTH) + EPS)
    ident = passed[:, WIDTH : WIDTH + 1].astype(F32).astype(jnp.int32)
    low = only(factor * dot_t(gained[...], down[...]), ident).astype(BF)
    total = jnp.zeros((ROWS, VALUES), F32)
    for i in range(8):
        total += dot(gained[:, columns(where[i])], vals[i][...])
    values = (factor * total + SCALE * dot(low, up[...])).astype(BF)
    for i in range(8):
        span = columns(where[i])
        out[:, span] = (rows[:, span].astype(F32) + dot(values, outs[i][...])).astype(BF)


def forward(where, fresh, passed, gain, down, up, vals, outs):
    return call(
        forward_kernel,
        (where,),
        [fresh, passed, gain, down, up, *vals, *outs],
        [shape((ROWS, WIDTH), BF)],
        4 * ROWS * WIDTH * VALUES,
        [pltpu.VMEM((ROWS, WIDTH), BF), pltpu.VMEM((ROWS, WIDTH), BF)],
    )[0]


def pair_sum_kernel(mine, other, total):
    total[...] = (mine[...].astype(F32) + other[...].astype(F32)).astype(BF)


def pair_sum(mine, other):
    return call(pair_sum_kernel, (), [mine, other], [shape((4, RANK, PACK), BF)], 0)[0]


def stack_kernel(where, first, mine, other, own, one, two, three):
    core = where[0] % 2
    for ahead, ref in enumerate((own, one, two, three)):
        sums = (mine[ahead].astype(F32) + other[ahead].astype(F32)).astype(BF)
        ref[:, :PART] = first[ahead, :, :PART]
        ref[:, PART : 2 * PART] = sums[:, :PART]
        ups = [
            jnp.where(core == 0, pair[:, : RANK].astype(F32), pair[:, RANK:].astype(F32))
            for pair in (first[ahead, :, PART:], sums[:, PART:])
        ]
        ref[:, 2 * PART :] = jnp.concatenate(ups, axis=1).astype(BF)


def spread(where, first, mine, received):
    block = shape((RANK, 2 * PART + 128), BF)
    own, one, two, three = call(
        stack_kernel, (where,), [first, mine, received], [block] * 4, 0
    )
    return (
        own,
        lax.ppermute(two, "dp", chips(2)),
        lax.ppermute(one, "dp", chips(1)),
        lax.ppermute(three, "dp", chips(3)),
    )


def tables_kernel(ahead, back, where, relayed, *refs):
    terms, (down, up) = refs[:4], refs[4:]
    came = relayed[:RANK, :1].astype(F32).astype(jnp.int32)
    ident = jnp.where(where[9] == 1, ahead[0], came)
    total = terms[0][...].astype(F32)
    for k in range(1, 4):
        total += terms[k][...].astype(F32)
    end = 2 * PART
    for label in range(ADAPTERS):
        one = jnp.where(back[0] == label, 1.0, 0.0)
        two = jnp.where(ident == label, 1.0, 0.0)
        down[label] = one * total[:, :PART] + two * total[:, PART:end]
        up[label] = one * total[:, end : end + RANK] + two * total[:, end + RANK :]


def tables(ahead, back, where, relayed, terms):
    tail = (relayed, (ROWS, 128), lambda i, *s: (0, WIDTH // 128))
    return call(
        tables_kernel,
        (ahead, back, where),
        [tail, *terms],
        [shape((ADAPTERS, RANK, PART), F32), shape((ADAPTERS, RANK, 64), F32)],
        0,
    )


CORE = [(i, i ^ 1) for i in range(8)]


def chips(by):
    return [(i, ((i // 2 + by) % 4) * 2 + i % 2) for i in range(8)]


def split_ring(sign):
    return [(i, ((i // 2 + (sign if i % 2 == 0 else -sign)) % 4) * 2 + i % 2) for i in range(8)]


def send(block, pairs):
    return lax.ppermute(block, "dp", pairs)


def block_index():
    place = lax.axis_index("dp")
    chip, core = place // 2, place % 2
    other = 1 - core
    step = jnp.where(core == 0, 1, -1)
    block = lambda k, c: 2 * (k % 4) + c
    return [
        block(chip, core), block(chip, other),
        block(chip - step + 4, core), block(chip + step + 4, other),
        block(chip + step + 4, core), block(chip - step + 4, other),
        block(chip + 2, core), block(chip + 2, other),
    ]


def body(
    forward_state, backward_state, saved, fresh, target, forward_adapter, backward_adapter,
    value_projection, output_matrix, norm_gain_frozen, adapter_down, adapter_up,
):
    count = lax.axis_size("section")
    onward = [(i, (i + 1) % count) for i in range(count)]
    before = [(i, i - 1) for i in range(1, count)]
    position = lax.axis_index("section")
    where = jnp.stack(
        [v.astype(jnp.int32) for v in (*block_index(), position == 0, position == count - 1)]
    )
    gain = norm_gain_frozen
    down = jnp.swapaxes(adapter_down[0], 1, 2).reshape(LOWS, WIDTH)
    up = adapter_up[0].reshape(LOWS, VALUES)
    rows, grad = forward_state[0], backward_state[0]
    ahead, back = forward_adapter, backward_adapter

    out_own, val_own = output_matrix[0], value_projection[0]
    out_near, out_away = send(out_own, split_ring(1)), send(out_own, split_ring(-1))
    val_near, val_away = send(val_own, split_ring(1)), send(val_own, split_ring(-1))
    out_sibling, val_sibling = send(out_own, CORE), send(val_own, CORE)

    normed_f, _, low_f, normed_b, factor_b, low_b, normed_n, factor_n, low_n, rows_n = prepare(
        ahead, back, where, rows, saved, gain, down
    )
    out_near, out_away, normed_f, out_sibling, val_sibling = lax.optimization_barrier(
        (out_near, out_away, normed_f, out_sibling, val_sibling)
    )
    out_far, val_far = send(out_near, split_ring(1)), send(val_near, split_ring(1))
    outs = [
        out_own, out_sibling, out_near, send(out_near, CORE), out_away, send(out_away, CORE)
    ]
    vals = [
        val_own, val_sibling, val_near, send(val_near, CORE), val_away, send(val_away, CORE)
    ]
    outs += [out_far, send(out_far, CORE)]
    d_values, d_low, kept, inner, share_f = near_share(
        back, where, grad, normed_f, saved, factor_b, gain, down, up, outs, vals
    )
    other = pack(where, low_b, normed_b, d_values, d_low, True)
    mine = pack(where, low_b, normed_b, d_values, d_low, False)
    first_sums = pair_sum(mine, send(other, CORE))
    val_far, first_sums = lax.optimization_barrier((val_far, first_sums))
    vals += [val_far, send(val_far, CORE)]

    first_back = first_gradient(
        back, where, kept, inner, d_values, d_low, grad, saved, factor_b, gain, down, vals
    )
    relayed = lax.ppermute(first_back, "section", before)
    share_f, first_back = lax.optimization_barrier((share_f, first_back))
    first_out = output(ahead, where, share_f, normed_f, low_f, up, rows, outs, vals)
    passed = lax.ppermute(first_out, "section", onward)
    first_out, normed_n = lax.optimization_barrier((first_out, normed_n))
    sums_n = project(where, normed_n, vals)
    relayed, sums_n = lax.optimization_barrier((relayed, sums_n))

    grad_n, d_values, d_low, chosen_low, other = second_values(
        ahead, where, relayed, first_out, target, low_n, normed_n, up, outs
    )
    received = send(other, CORE)
    mine = pack(where, chosen_low, normed_n, d_values, d_low, False)
    terms = spread(where, first_sums, mine, received)
    bwd_out = second_input(
        where, sums_n, low_n, grad_n, rows_n, factor_n, gain, down, d_values, d_low, vals
    )
    fwd_out = forward(where, fresh, passed, gain, down, up, vals, outs)
    down_table, up_table = tables(ahead, back, where, relayed, terms)
    return (
        fwd_out[None], bwd_out[None], jnp.swapaxes(down_table, 1, 2)[None], up_table[None]
    )


def solution(mesh):
    return jax.shard_map(
        body,
        mesh=mesh,
        in_specs=(
            P("section", "dp", None),
            P("section", "dp", None),
            P("section", None, "dp", None),
            P("dp", None),
            P("dp", None),
            P("section"),
            P("section"),
            P("section", "dp", None),
            P("section", None, "dp"),
            P("section", None),
            P("section", None, None, None),
            P("section", None, None, None),
        ),
        out_specs=(
            P("section", "dp", None),
            P("section", "dp", None),
            P("section", None, "dp", None),
            P("section", None, None, "dp"),
        ),
        check_vma=False,
    )
```

```python
import jax
import jax.numpy as jnp
from jax import lax
from jax.experimental import pallas as pl
from jax.experimental.pallas import tpu as pltpu
from jax.sharding import PartitionSpec as P

SCALE = 0.5
EPS = 1e-05
BF = jnp.bfloat16
F32 = jnp.float32
ROWS = 128
WIDTH = 4096
VALUES = 512
PART = 512
RANK = 64
ADAPTERS = 4
PACK = PART + 128
LOWS = 256
WIDE = WIDTH + 128
VMEM = 20 * 1024 * 1024
ONCE = pl.Buffered(1)


def dot(left, right, dims=((1,), (0,))):
    return lax.dot_general(left, right, (dims, ((), ())), preferred_element_type=F32)


def dot_t(left, right):
    return dot(left, right, ((1,), (1,)))


def t_dot(left, right):
    return dot(left, right, ((0,), (0,)))


def call(kernel, scalars, ins, outs, flops, scratch=()):
    specs, arrays = [], []
    for item in ins:
        array, block, index = item if isinstance(item, tuple) else (item, None, None)
        arrays.append(array)
        if block is None:
            zeros = (0,) * array.ndim
            specs.append(pl.BlockSpec(array.shape, lambda i, *s, z=zeros: z, pipeline_mode=ONCE))
        else:
            specs.append(pl.BlockSpec(block, index, pipeline_mode=ONCE))
    out_specs = [
        pl.BlockSpec(o.shape, lambda i, *s, z=(0,) * len(o.shape): z, pipeline_mode=ONCE)
        for o in outs
    ]
    size = sum(a.size * a.dtype.itemsize for a in arrays)
    return pl.pallas_call(
        kernel,
        out_shape=outs,
        grid_spec=pltpu.PrefetchScalarGridSpec(
            num_scalar_prefetch=len(scalars),
            grid=(1,),
            in_specs=specs,
            out_specs=out_specs,
            scratch_shapes=list(scratch),
        ),
        compiler_params=pltpu.CompilerParams(vmem_limit_bytes=VMEM),
        cost_estimate=pl.CostEstimate(
            flops=flops // 1000, bytes_accessed=size // 1000, transcendentals=0
        ),
    )(*scalars, *arrays)


def shape(dims, dtype):
    return jax.ShapeDtypeStruct(dims, dtype)


def factor_of(rows):
    return lax.rsqrt(jnp.sum(rows * rows, axis=-1, keepdims=True) * (1.0 / WIDTH) + EPS)


def columns(index):
    return pl.ds(pl.multiple_of(index * PART, PART), PART)


def only(lows, ident):
    lane = lax.broadcasted_iota(jnp.int32, lows.shape, 1)
    return jnp.where(lane // RANK == ident, lows, jnp.zeros_like(lows))


def compact(lows):
    total = lows[:, :RANK].astype(F32)
    for k in range(1, ADAPTERS):
        total += lows[:, k * RANK : (k + 1) * RANK].astype(F32)
    return total.astype(BF)


def saved_of(saved, which):
    return (saved, (1, 1, ROWS, WIDTH), lambda i, *s: (0, which, 0, 0))


def prepare_kernel(ahead, back, where, rows_f, rows_b, rows_s, gain, down, *refs):
    last = where[9] == 1
    for kind in range(3):
        normed, factor, low = refs[3 * kind : 3 * kind + 3]
        for top in range(0, ROWS, 32):
            part = slice(top, top + 32)
            if kind == 0:
                whole = rows_f[part, :]
            elif kind == 1:
                whole = rows_b[0, 0, part, :]
            else:
                whole = jnp.where(last, rows_f[part, :], rows_s[0, 0, part, :])
            whole = whole.astype(F32)
            scale = factor_of(whole)
            normed[part, :] = (whole * scale * gain[...]).astype(BF)
            factor[part, :] = jnp.broadcast_to(scale, (32, 128))
        lows = dot_t(normed[...], down[...])
        if kind == 0:
            lows = only(lows, ahead[0])
        elif kind == 1:
            lows = only(lows, back[0])
        low[...] = lows.astype(BF)


def prepare(ahead, back, where, rows, saved, gain, down):
    kinds = [shape((ROWS, WIDTH), BF), shape((ROWS, 128), F32), shape((ROWS, LOWS), BF)]
    return call(
        prepare_kernel,
        (ahead, back, where),
        [rows, saved_of(saved, 0), saved_of(saved, 1), gain, down],
        kinds * 3,
        6 * ROWS * WIDTH * LOWS,
    )


def gained_block(values, lowered, span, gain, down, block):
    return (dot_t(values, block[...]) + dot(lowered, down[:, span])) * gain[:, span]


def input_gradient(where, grad, rows, scale, inner, gained, out):
    inner = inner * (1.0 / WIDTH)
    for i in range(8):
        span = columns(where[i])
        pre = rows(span).astype(F32) * scale
        out[:, span] = (
            grad[:, span].astype(F32) + scale * (gained(i) - pre * inner)
        ).astype(BF)


def near_kernel(back, where, grad, normed, rows, factor, gain, down, up, *refs):
    outs, vals, (d_values, d_low, kept, inner, share) = refs[:8], refs[8:14], refs[14:]
    total = jnp.zeros((ROWS, VALUES), F32)
    for i in range(8):
        total += dot_t(grad[:, columns(where[i])], outs[i][...])
    values = total.astype(BF)
    lowered = only(SCALE * dot_t(values, up[...]), back[0]).astype(BF)
    d_values[...] = values
    d_low[...] = lowered
    scale = factor[:, :1]
    mean = jnp.zeros((ROWS, 1), F32)
    for i in range(6):
        span = columns(where[i])
        gained = gained_block(values, lowered, span, gain, down, vals[i])
        kept[i] = gained
        mean += jnp.sum(
            gained * (rows[0, 0, :, span].astype(F32) * scale), axis=-1, keepdims=True
        )
    inner[...] = jnp.broadcast_to(mean, (ROWS, 128))
    total = jnp.zeros((ROWS, VALUES), F32)
    for i in range(6):
        total += dot(normed[:, columns(where[i])], vals[i][...])
    share[...] = total


GRADS = [shape((ROWS, VALUES), BF), shape((ROWS, LOWS), BF)]


def near_share(back, where, grad, normed, saved, factor, gain, down, up, outs, vals):
    return call(
        near_kernel,
        (back, where),
        [grad, normed, saved_of(saved, 0), factor, gain, down, up, *outs, *vals],
        [*GRADS, shape((6, ROWS, PART), F32), shape((ROWS, 128), F32), shape((ROWS, VALUES), F32)],
        6 * ROWS * WIDTH * VALUES,
    )


def first_kernel(
    back, where, kept, inner, values, lowered, grad, rows, factor, gain, down, far, far_other, out
):
    scale = factor[:, :1]
    mean = inner[:, :1]
    last = []
    for i, block in ((6, far), (7, far_other)):
        span = columns(where[i])
        gained = gained_block(values[...], lowered[...], span, gain, down, block)
        mean += jnp.sum(
            gained * (rows[0, 0, :, span].astype(F32) * scale), axis=-1, keepdims=True
        )
        last.append(gained)
    input_gradient(
        where, grad, lambda span: rows[0, 0, :, span], scale, mean,
        lambda i: kept[i] if i < 6 else last[i - 6], out,
    )
    out[:, WIDTH:] = jnp.full((ROWS, 128), back[0], jnp.int32).astype(F32).astype(BF)


def first_gradient(back, where, kept, inner, d_values, d_low, grad, saved, factor, gain, down, vals):
    return call(
        first_kernel,
        (back, where),
        [
            kept, inner, d_values, d_low, grad, saved_of(saved, 0), factor, gain, down, *vals[6:]
        ],
        [shape((ROWS, WIDE), BF)],
        ROWS * WIDTH * VALUES,
    )[0]


def output_kernel(ahead, where, share, normed, low, up, rows, far, far_other, *refs):
    blocks, out = refs[:8], refs[8]
    total = share[...] + SCALE * dot(low[...], up[...])
    total += dot(normed[:, columns(where[6])], far[...])
    total += dot(normed[:, columns(where[7])], far_other[...])
    values = total.astype(BF)
    for i in range(8):
        span = columns(where[i])
        out[:, span] = (rows[:, span].astype(F32) + dot(values, blocks[i][...])).astype(BF)
    out[:, WIDTH:] = jnp.full((ROWS, 128), ahead[0], jnp.int32).astype(F32).astype(BF)


def output(ahead, where, share, normed, low, up, rows, outs, vals):
    return call(
        output_kernel,
        (ahead, where),
        [share, normed, low, up, rows, *vals[6:], *outs],
        [shape((ROWS, WIDE), BF)],
        2 * ROWS * WIDTH * VALUES,
    )[0]


def pack_gradients(where, low, normed, d_values, d_low, core, ref):
    up_term = SCALE * t_dot(low, d_values)
    chip = where[0] // 2
    for ahead in range(4):
        target = lax.rem(chip + ahead, 4)
        pair = up_term[:, 0:128]
        for k in range(1, 4):
            pair = jnp.where(target == k, up_term[:, 128 * k : 128 * (k + 1)], pair)
        ref[ahead, :, :PART] = t_dot(d_low, normed[:, columns(2 * target + core)]).astype(BF)
        ref[ahead, :, PART:] = pair.astype(BF)


PACKED = [shape((4, RANK, PACK), BF)]


def pack(where, low, normed, d_values, d_low, other):
    def kernel(where, low, normed, d_values, d_low, ref):
        core = 1 - where[0] % 2 if other else where[0] % 2
        pack_gradients(
            where, compact(low[...]), normed, d_values[...], compact(d_low[...]), core, ref
        )

    return call(
        kernel, (where,), [low, normed, d_values, d_low], PACKED, ROWS * WIDTH * RANK
    )[0]


def second_kernel(ahead, where, relayed, out, target, low, normed, up, *refs):
    blocks, (grad, d_values, d_low, chosen_low, other) = refs[:8], refs[8:]
    last = where[9] == 1
    total = jnp.zeros((ROWS, VALUES), F32)
    for i in range(8):
        span = columns(where[i])
        loss = (out[:, span].astype(F32) - target[:, span].astype(F32)).astype(BF)
        chosen = jnp.where(last, loss, relayed[:, span])
        grad[:, span] = chosen
        total += dot_t(chosen, blocks[i][...])
    values = total.astype(BF)
    came = relayed[:, WIDTH : WIDTH + 1].astype(F32).astype(jnp.int32)
    ident = jnp.where(last, ahead[0], came)
    lowered = only(SCALE * dot_t(values, up[...]), ident).astype(BF)
    d_values[...] = values
    d_low[...] = lowered
    chosen = only(low[...], ident)
    chosen_low[...] = chosen
    pack_gradients(
        where, compact(chosen), normed, values, compact(lowered), 1 - where[0] % 2, other
    )


def second_values(ahead, where, relayed, out, target, low, normed, up, blocks):
    return call(
        second_kernel,
        (ahead, where),
        [relayed, out, target, low, normed, up, *blocks],
        [shape((ROWS, WIDTH), BF), *GRADS, shape((ROWS, LOWS), BF), *PACKED],
        2 * ROWS * WIDTH * (VALUES + RANK),
    )


def project_kernel(where, normed, *refs):
    blocks, out = refs[:8], refs[8]
    total = jnp.zeros((ROWS, VALUES), F32)
    for i in range(8):
        total += dot(normed[:, columns(where[i])], blocks[i][...])
    out[...] = total


def project(where, normed, vals):
    return call(
        project_kernel, (where,), [normed, *vals], [shape((ROWS, VALUES), F32)],
        2 * ROWS * WIDTH * VALUES,
    )[0]


def second_input_kernel(
    where, sums, low, grad, rows_f, rows_s, factor, gain, down, d_values, d_low, *refs
):
    blocks, out = refs[:8], refs[8]
    last = where[9] == 1
    scale = factor[:, :1]
    values, lowered = d_values[...], d_low[...]
    inner = jnp.sum(values.astype(F32) * sums[...], axis=-1, keepdims=True)
    inner += jnp.sum(lowered.astype(F32) * low[...].astype(F32), axis=-1, keepdims=True)
    weight = scale * scale * inner * (1.0 / WIDTH)
    for i in range(8):
        span = columns(where[i])
        rows = jnp.where(last, rows_f[:, span], rows_s[0, 0, :, span]).astype(F32)
        gained = gained_block(values, lowered, span, gain, down, blocks[i])
        out[:, span] = (grad[:, span].astype(F32) + scale * gained - weight * rows).astype(BF)


def second_input(where, sums, low, grad, rows, saved, factor, gain, down, d_values, d_low, blocks):
    return call(
        second_input_kernel,
        (where,),
        [
            sums, low, grad, rows, saved_of(saved, 1), factor, gain, down, d_values, d_low, *blocks
        ],
        [shape((ROWS, WIDTH), BF)],
        2 * ROWS * WIDTH * (VALUES + RANK),
    )[0]


def forward_kernel(where, fresh, passed, gain, down, up, *refs):
    vals, outs, (out, rows, normed) = refs[:8], refs[8:16], refs[16:]
    first = where[8] == 1
    for top in range(0, ROWS, 32):
        part = slice(top, top + 32)
        chosen = jnp.where(first, fresh[part, :], passed[part, :WIDTH])
        whole = chosen.astype(F32)
        rows[part, :] = chosen
        normed[part, :] = (whole * factor_of(whole) * gain[...]).astype(BF)
    ident = passed[:, WIDTH : WIDTH + 1].astype(F32).astype(jnp.int32)
    low = only(dot_t(normed[...], down[...]), ident).astype(BF)
    total = SCALE * dot(low, up[...])
    for i in range(8):
        total += dot(normed[:, columns(where[i])], vals[i][...])
    values = total.astype(BF)
    for i in range(8):
        span = columns(where[i])
        out[:, span] = (rows[:, span].astype(F32) + dot(values, outs[i][...])).astype(BF)


def forward(where, fresh, passed, gain, down, up, vals, outs):
    return call(
        forward_kernel,
        (where,),
        [fresh, passed, gain, down, up, *vals, *outs],
        [shape((ROWS, WIDTH), BF)],
        4 * ROWS * WIDTH * VALUES,
        [pltpu.VMEM((ROWS, WIDTH), BF), pltpu.VMEM((ROWS, WIDTH), BF)],
    )[0]


def pair_sum_kernel(mine, other, total):
    total[...] = (mine[...].astype(F32) + other[...].astype(F32)).astype(BF)


def pair_sum(mine, other):
    return call(pair_sum_kernel, (), [mine, other], [shape((4, RANK, PACK), BF)], 0)[0]


def stack_kernel(where, first, mine, other, own, one, two, three):
    core = where[0] % 2
    for ahead, ref in enumerate((own, one, two, three)):
        sums = (mine[ahead].astype(F32) + other[ahead].astype(F32)).astype(BF)
        ref[:, :PART] = first[ahead, :, :PART]
        ref[:, PART : 2 * PART] = sums[:, :PART]
        ups = [
            jnp.where(core == 0, pair[:, : RANK].astype(F32), pair[:, RANK:].astype(F32))
            for pair in (first[ahead, :, PART:], sums[:, PART:])
        ]
        ref[:, 2 * PART :] = jnp.concatenate(ups, axis=1).astype(BF)


def spread(where, first, mine, received):
    block = shape((RANK, 2 * PART + 128), BF)
    own, one, two, three = call(
        stack_kernel, (where,), [first, mine, received], [block] * 4, 0
    )
    return (
        own,
        lax.ppermute(two, "dp", chips(2)),
        lax.ppermute(one, "dp", chips(1)),
        lax.ppermute(three, "dp", chips(3)),
    )


def tables_kernel(ahead, back, where, relayed, *refs):
    terms, (down, up) = refs[:4], refs[4:]
    came = relayed[:RANK, :1].astype(F32).astype(jnp.int32)
    ident = jnp.where(where[9] == 1, ahead[0], came)
    total = terms[0][...].astype(F32)
    for k in range(1, 4):
        total += terms[k][...].astype(F32)
    end = 2 * PART
    for label in range(ADAPTERS):
        one = jnp.where(back[0] == label, 1.0, 0.0)
        two = jnp.where(ident == label, 1.0, 0.0)
        down[label] = one * total[:, :PART] + two * total[:, PART:end]
        up[label] = one * total[:, end : end + RANK] + two * total[:, end + RANK :]


def tables(ahead, back, where, relayed, terms):
    tail = (relayed, (ROWS, 128), lambda i, *s: (0, WIDTH // 128))
    return call(
        tables_kernel,
        (ahead, back, where),
        [tail, *terms],
        [shape((ADAPTERS, RANK, PART), F32), shape((ADAPTERS, RANK, 64), F32)],
        0,
    )


CORE = [(i, i ^ 1) for i in range(8)]


def chips(by):
    return [(i, ((i // 2 + by) % 4) * 2 + i % 2) for i in range(8)]


def split_ring(sign):
    return [(i, ((i // 2 + (sign if i % 2 == 0 else -sign)) % 4) * 2 + i % 2) for i in range(8)]


def send(block, pairs):
    return lax.ppermute(block, "dp", pairs)


def block_index():
    place = lax.axis_index("dp")
    chip, core = place // 2, place % 2
    other = 1 - core
    step = jnp.where(core == 0, 1, -1)
    block = lambda k, c: 2 * (k % 4) + c
    return [
        block(chip, core), block(chip, other),
        block(chip - step + 4, core), block(chip + step + 4, other),
        block(chip + step + 4, core), block(chip - step + 4, other),
        block(chip + 2, core), block(chip + 2, other),
    ]


def body(
    forward_state, backward_state, saved, fresh, target, forward_adapter, backward_adapter,
    value_projection, output_matrix, norm_gain_frozen, adapter_down, adapter_up,
):
    count = lax.axis_size("section")
    onward = [(i, (i + 1) % count) for i in range(count)]
    before = [(i, i - 1) for i in range(1, count)]
    position = lax.axis_index("section")
    where = jnp.stack(
        [v.astype(jnp.int32) for v in (*block_index(), position == 0, position == count - 1)]
    )
    gain = norm_gain_frozen
    down = jnp.swapaxes(adapter_down[0], 1, 2).reshape(LOWS, WIDTH)
    up = adapter_up[0].reshape(LOWS, VALUES)
    rows, grad = forward_state[0], backward_state[0]
    ahead, back = forward_adapter, backward_adapter

    out_own, val_own = output_matrix[0], value_projection[0]
    out_near, out_away = send(out_own, split_ring(1)), send(out_own, split_ring(-1))
    val_near, val_away = send(val_own, split_ring(1)), send(val_own, split_ring(-1))
    out_sibling, val_sibling = send(out_own, CORE), send(val_own, CORE)

    normed_f, _, low_f, normed_b, factor_b, low_b, normed_n, factor_n, low_n = prepare(
        ahead, back, where, rows, saved, gain, down
    )
    out_near, out_away, normed_f = lax.optimization_barrier((out_near, out_away, normed_f))
    out_far, val_far = send(out_near, split_ring(1)), send(val_near, split_ring(1))
    outs = [
        out_own, out_sibling, out_near, send(out_near, CORE), out_away, send(out_away, CORE)
    ]
    vals = [
        val_own, val_sibling, val_near, send(val_near, CORE), val_away, send(val_away, CORE)
    ]
    outs += [out_far, send(out_far, CORE)]
    d_values, d_low, kept, inner, share_f = near_share(
        back, where, grad, normed_f, saved, factor_b, gain, down, up, outs, vals
    )
    other = pack(where, low_b, normed_b, d_values, d_low, True)
    mine = pack(where, low_b, normed_b, d_values, d_low, False)
    first_sums = pair_sum(mine, send(other, CORE))
    val_far, first_sums = lax.optimization_barrier((val_far, first_sums))
    vals += [val_far, send(val_far, CORE)]

    first_back = first_gradient(
        back, where, kept, inner, d_values, d_low, grad, saved, factor_b, gain, down, vals
    )
    relayed = lax.ppermute(first_back, "section", before)
    share_f, first_back = lax.optimization_barrier((share_f, first_back))
    first_out = output(ahead, where, share_f, normed_f, low_f, up, rows, outs, vals)
    passed = lax.ppermute(first_out, "section", onward)
    first_out, normed_n = lax.optimization_barrier((first_out, normed_n))
    sums_n = project(where, normed_n, vals)
    relayed, sums_n = lax.optimization_barrier((relayed, sums_n))

    grad_n, d_values, d_low, chosen_low, other = second_values(
        ahead, where, relayed, first_out, target, low_n, normed_n, up, outs
    )
    received = send(other, CORE)
    mine = pack(where, chosen_low, normed_n, d_values, d_low, False)
    terms = spread(where, first_sums, mine, received)
    bwd_out = second_input(
        where, sums_n, low_n, grad_n, rows, saved, factor_n, gain, down, d_values, d_low, vals
    )
    fwd_out = forward(where, fresh, passed, gain, down, up, vals, outs)
    down_table, up_table = tables(ahead, back, where, relayed, terms)
    return (
        fwd_out[None], bwd_out[None], jnp.swapaxes(down_table, 1, 2)[None], up_table[None]
    )


def solution(mesh):
    return jax.shard_map(
        body,
        mesh=mesh,
        in_specs=(
            P("section", "dp", None),
            P("section", "dp", None),
            P("section", None, "dp", None),
            P("dp", None),
            P("dp", None),
            P("section"),
            P("section"),
            P("section", "dp", None),
            P("section", None, "dp"),
            P("section", None),
            P("section", None, None, None),
            P("section", None, None, None),
        ),
        out_specs=(
            P("section", "dp", None),
            P("section", "dp", None),
            P("section", None, "dp", None),
            P("section", None, None, "dp"),
        ),
        check_vma=False,
    )
```
